32 devices in a mesh: dp: 8 (over z, y), tensor: 4 (over x, core).
Axes of the slice: x: 2, y: 2, z: 4, core: 2. Of those that a mesh axis runs over, the one named last changes fastest.
Arguments:
- tokens: bfloat16 [16, 1024, 1024], P('dp', 'tensor'), may hold values from -6 to 6
- doc_ids: int32 [16, 1024], P('dp'), may hold values from 0 to 3, as said below
- targets: int32 [16, 1024], P('dp'), may hold values from 0 to 63, as said below
- cotangent: bfloat16 [16, 1024, 1024], P('dp', 'tensor'), may hold values from -6 to 6
- ln1_gain: bfloat16 [1024], replicated, may hold values from 0.5 to 1.5
- ln1_bias: bfloat16 [1024], replicated, may hold values from -1.25 to 1.25
- qkv_weight: bfloat16 [3, 1024, 1024], P(None, None, 'tensor'), may hold values from -0.1875 to 0.1875
- query_bias: bfloat16 [1024], P('tensor'), may hold values from -3 to 3
- value_bias: bfloat16 [1024], P('tensor'), may hold values from -0.125 to 0.125
- output_weight: bfloat16 [1024, 1024], P('tensor'), may hold values from -1.5 to 1.5
- out_bias: bfloat16 [1024], replicated, may hold values from -1.25 to 1.25
- ln2_gain: bfloat16 [1024], replicated, may hold values from 0.5 to 1.5
- ln2_bias: bfloat16 [1024], replicated, may hold values from -1.25 to 1.25
- up_weight: bfloat16 [1024, 4096], P(None, 'tensor'), may hold values from -0.1875 to 0.1875
- up_bias: bfloat16 [4096], P('tensor'), may hold values from -1.25 to 1.25
- down_weight: bfloat16 [4096, 1024], P('tensor'), may hold values from -0.09375 to 0.09375
- down_bias: bfloat16 [1024], replicated, may hold values from -1.25 to 1.25
Outputs:
- activations: bfloat16 [16, 1024, 1024], P('dp', 'tensor')
- loss: float32 [16, 1024], P('dp', 'tensor')
- input_grad: float32 [16, 1024, 1024], P('dp', 'tensor')
- ln1_gain_grad: float32 [1024], replicated
- ln1_bias_grad: float32 [1024], replicated
- qkv_weight_grad: float32 [3, 1024, 1024], P(None, None, 'tensor')
- query_bias_grad: float32 [1024], P('tensor')
- value_bias_grad: float32 [1024], P('tensor')
- out_weight_grad: float32 [1024, 1024], P('tensor')
- out_bias_grad: float32 [1024], replicated
- ln2_gain_grad: float32 [1024], replicated
- ln2_bias_grad: float32 [1024], replicated
- up_weight_grad: float32 [1024, 4096], P(None, 'tensor')
- up_bias_grad: float32 [4096], P('tensor')
- down_weight_grad: float32 [4096, 1024], P('tensor')
- down_bias_grad: float32 [1024], replicated
The draws below stay inside these ranges and needn't reach their ends.
Inputs may be any that keep to these rules, and one draw needn't show every extreme that they name: `doc_ids`: segment numbers never fall along a sequence and start at 0. Among the 2 sequences of each index of dp exactly one, drawn from the seed, is a single document; each other sequence ends with segment 3. `targets`: each aligned block of 64 positions of a sequence holds every target once.
All inputs are finite; a program needn't handle non-finite values.
Results may differ from the reference program's by a relative error of at most 0.02.
Values may be sent and summed in bfloat16 or wider, within the bound.
No kernel may reach another device: no remote copies, remote signals or barrier semaphores. Data moves between devices by JAX's collectives and lax.ppermute only.
A program may use at most 192 MiB of HBM per device.

```python
import math
import jax
import jax.numpy as jnp
from jax import lax

D = 1024
HEADS = 8
FF = 4096
HEAD_DIM = 128
SEQ = 1024
SEQS_DEV = 2
CLASSES = 64
SEQUENCES = 16
N_DP = 8


def draw_doc_ids(key, part):
    key = jax.random.fold_in(key, 11)
    cut_key, pick_key = jax.random.split(key)
    cut_points = jax.random.randint(cut_key, (SEQUENCES, 3), 1, SEQ, dtype=jnp.int32)
    position = jnp.arange(SEQ, dtype=jnp.int32)
    split_ids = jnp.sum((position[None, :, None] >= cut_points[:, None, :]).astype(jnp.int32), axis=-1)
    chosen = jax.random.randint(pick_key, (SEQUENCES // SEQS_DEV,), 0, SEQS_DEV, dtype=jnp.int32)
    member = jnp.arange(SEQUENCES, dtype=jnp.int32) % SEQS_DEV
    single = member == jnp.repeat(chosen, SEQS_DEV)
    return jnp.where(single[:, None], 0, split_ids).astype(jnp.int32)


def draw_targets(key, part):
    key = jax.random.fold_in(key, 23)
    block_keys = jax.random.split(key, SEQUENCES * (SEQ // CLASSES))
    orders = jax.vmap(lambda one_key: jax.random.permutation(one_key, CLASSES))(block_keys)
    return orders.reshape(SEQUENCES, SEQ).astype(jnp.int32)


def steps_of(stream_key, extent, cuts, low, largest):
    gain = 1.0
    for dim, blocks in cuts:
        steps = jax.random.uniform(jax.random.fold_in(jax.random.fold_in(stream_key, 6), dim), (blocks,), jnp.float32, low / len(cuts), largest / len(cuts))
        gain = gain * jnp.repeat(jnp.exp(steps), extent[dim] // blocks).reshape((-1,) + (1,) * (len(extent) - 1 - dim))
    return gain


def normal_values(rng, extent, spread, most, shards=(), kind=jnp.bfloat16):
    values = spread * jax.random.normal(rng, extent, jnp.float32)
    if shards:
        values = values * steps_of(rng, extent, shards, -0.22, 0.18)
    return jnp.clip(values, -most, most).astype(kind)


def setup_inputs(seed: int = 0) -> dict:
    keys = jax.random.split(jax.random.key(seed), 18)
    tokens = normal_values(keys[0], (SEQUENCES, SEQ, D), 1.0, 6.0, ((0, 8), (1, 4)))
    doc_ids = draw_doc_ids(jax.random.fold_in(keys[17], 71), 0)
    targets = draw_targets(jax.random.fold_in(keys[17], 71), 0)
    cotangent = normal_values(keys[3], (SEQUENCES, SEQ, D), 1.0, 6.0, ((0, 8), (1, 4)))
    ln1_gain = jnp.clip(1.0 + 0.1 * jax.random.normal(keys[4], (D,), jnp.float32), 0.5, 1.5).astype(jnp.bfloat16)
    ln1_bias = normal_values(keys[5], (D,), 0.2, 1.25)
    qkv_weight = normal_values(keys[6], (3, D, D), D ** -0.5, 0.1875, ((2, 4),))
    query_bias = normal_values(keys[7], (D,), 0.5, 3.0, ((0, 4),))
    value_bias = normal_values(keys[8], (D,), 0.02, 0.125, ((0, 4),))
    output_weight = normal_values(keys[9], (D, D), 16 ** -0.5, 1.5, ((0, 4),))
    out_bias = normal_values(keys[10], (D,), 0.2, 1.25)
    ln2_gain = jnp.clip(1.0 + 0.1 * jax.random.normal(keys[11], (D,), jnp.float32), 0.5, 1.5).astype(jnp.bfloat16)
    ln2_bias = normal_values(keys[12], (D,), 0.2, 1.25)
    up_weight = normal_values(keys[13], (D, FF), D ** -0.5, 0.1875, ((1, 4),))
    up_bias = normal_values(keys[14], (FF,), 0.2, 1.25, ((0, 4),))
    down_weight = normal_values(keys[15], (FF, D), FF ** -0.5, 0.09375, ((0, 4),))
    down_bias = normal_values(keys[16], (D,), 0.2, 1.25)
    return {"tokens": tokens, "doc_ids": doc_ids, "targets": targets, "cotangent": cotangent, "ln1_gain": ln1_gain, "ln1_bias": ln1_bias, "qkv_weight": qkv_weight, "query_bias": query_bias, "value_bias": value_bias, "output_weight": output_weight, "out_bias": out_bias, "ln2_gain": ln2_gain, "ln2_bias": ln2_bias, "up_weight": up_weight, "up_bias": up_bias, "down_weight": down_weight, "down_bias": down_bias}


@jax.custom_vjp
def low(v):
    return lax.optimization_barrier(v.astype(jnp.bfloat16)).astype(jnp.float32)

@jax.custom_vjp
def reduced_backward(v):
    return v

def low_keep(v):
    return (low(v), None)

def low_pass(kept, grad):
    return (grad,)

def back_keep(v):
    return (v, None)

def back_low(kept, grad):
    return (low(grad),)
low.defvjp(low_keep, low_pass)
reduced_backward.defvjp(back_keep, back_low)
BEST_PRECISION = lax.Precision.HIGHEST
NORM_EPS = 1e-05
CONTRAST_SCALE = 32.0
CONTRAST_WEIGHT = 64.0
NEGATIVE = -1e+30

def positions(places, features):
    paired = (jnp.arange(features, dtype=jnp.int32) // 2).astype(places.dtype)
    angles = places[:, None] * jnp.exp(paired * (-2.0 * math.log(10000.0) / features))[None, :]
    is_odd = jnp.arange(features, dtype=jnp.int32) % 2 == 1
    return jnp.where(is_odd[None, :], jnp.cos(angles), jnp.sin(angles))

def layer_norm(values, gain_vec, shift_vec):
    centered = values - lax.optimization_barrier(jnp.mean(values, axis=-1, keepdims=True))
    variance = lax.optimization_barrier(jnp.mean(centered * centered, axis=-1, keepdims=True))
    return centered * lax.rsqrt(variance + NORM_EPS) * gain_vec + shift_vec

def masked_lse(scores, allowed):
    masked = jnp.where(allowed, scores, NEGATIVE)
    row_top = lax.optimization_barrier(jnp.max(masked, axis=-1, keepdims=True))
    summed = lax.optimization_barrier(jnp.sum(jnp.where(allowed, jnp.exp(masked - row_top), 0.0), axis=-1))
    return row_top[..., 0] + jnp.log(summed)

def one_sequence(packed):
    queries, key_rows, value_rows, documents = packed
    indices = jnp.arange(SEQ, dtype=jnp.int32)
    allowed = (documents[:, None] == documents[None, :]) & (indices[:, None] >= indices[None, :])
    scores = reduced_backward(jnp.einsum('qhd,khd->hqk', queries, key_rows, precision=BEST_PRECISION) * HEAD_DIM ** (-0.5))
    masked = jnp.where(allowed[None], scores, NEGATIVE)
    row_top = lax.optimization_barrier(jnp.max(masked, axis=-1, keepdims=True))
    exp_terms = jnp.where(allowed[None], jnp.exp(masked - row_top), 0.0)
    weights = low(exp_terms / lax.optimization_barrier(jnp.sum(exp_terms, axis=-1, keepdims=True)))
    return jnp.einsum('hqk,khd->qhd', weights, value_rows, precision=BEST_PRECISION).reshape(SEQ, D)

def contrast(unit_rows, groups, labels):
    scores = reduced_backward(jnp.dot(unit_rows, unit_rows.T, precision=BEST_PRECISION) * (CONTRAST_SCALE / D))
    memory = groups[:, None] != groups[None, :]
    positive = memory & (labels[:, None] == labels[None, :])
    return masked_lse(scores, memory) - masked_lse(scores, positive)

def layer_block(parameters, inputs, documents, labels):
    gain_one, shift_one, qkv_mat, query_shift, value_shift, output_matrix, output_offset, gain_two, shift_two, up_mat, up_shift, down_mat, down_shift = parameters
    seq_count = inputs.shape[0]
    places = jnp.arange(SEQ, dtype=jnp.int32).astype(inputs.dtype)
    hidden_state = inputs + positions(places, D)[None]
    normed = low(layer_norm(hidden_state, gain_one, shift_one))
    biases = jnp.stack([query_shift, jnp.zeros_like(query_shift), value_shift])
    qkv_all = jnp.einsum('snd,cde->csne', normed, qkv_mat, precision=BEST_PRECISION) + biases[:, None, None, :]
    qkv_all = low(reduced_backward(qkv_all))
    head_view = qkv_all.reshape(3, seq_count, SEQ, HEADS, HEAD_DIM)
    attended_rows = lax.map(jax.checkpoint(one_sequence), (head_view[0], head_view[1], head_view[2], documents))
    attended_rows = low(reduced_backward(attended_rows))
    residual_stream = hidden_state + reduced_backward(jnp.einsum('cjt,to->cjo', attended_rows, output_matrix, precision=BEST_PRECISION)) + output_offset
    second = low(layer_norm(residual_stream, gain_two, shift_two))
    up_value = reduced_backward(jnp.einsum('snd,df->snf', second, up_mat, precision=BEST_PRECISION) + up_shift)
    hidden_act = low(jax.nn.gelu(up_value, approximate=True))
    output = residual_stream + reduced_backward(jnp.einsum('snf,fd->snd', hidden_act, down_mat, precision=BEST_PRECISION)) + down_shift
    unit_rows = low(output * lax.rsqrt(lax.optimization_barrier(jnp.mean(output * output, axis=-1, keepdims=True)) + NORM_EPS))
    groups = (jnp.arange(seq_count, dtype=jnp.int32)[:, None] * SEQ + documents).reshape(-1)
    losses = contrast(unit_rows.reshape(seq_count * SEQ, D), groups, labels.reshape(-1))
    return (output, losses.reshape(seq_count, SEQ))

def reference(tokens, doc_ids, targets, cotangent, ln1_gain, ln1_bias, qkv_weight, query_bias, value_bias, output_weight, out_bias, ln2_gain, ln2_bias, up_weight, up_bias, down_weight, down_bias):
    parameters = tuple((item.astype(jnp.float32) for item in (ln1_gain, ln1_bias, qkv_weight, query_bias, value_bias, output_weight, out_bias, ln2_gain, ln2_bias, up_weight, up_bias, down_weight, down_bias)))

    def one_group(totals, group_item):
        inputs, documents, labels, cotan_rows = group_item

        def forward(params_now, values_now):
            return layer_block(params_now, values_now, documents, labels)
        (output, losses), pullback = jax.vjp(forward, parameters, inputs.astype(jnp.float32))
        gradients, input_grads = pullback((cotan_rows.astype(jnp.float32), jnp.full_like(losses, CONTRAST_WEIGHT)))
        return (jax.tree.map(jnp.add, totals, gradients), (output.astype(jnp.bfloat16), losses, input_grads))
    group_shape = (N_DP, SEQS_DEV, SEQ)
    zero_totals = tuple((jnp.zeros_like(item) for item in parameters))
    totals, (outputs, losses, input_grads) = lax.scan(one_group, zero_totals, (tokens.reshape(group_shape + (D,)), doc_ids.reshape(group_shape), targets.reshape(group_shape), cotangent.reshape(group_shape + (D,))))
    return (outputs.reshape(SEQUENCES, SEQ, D), losses.reshape(SEQUENCES, SEQ), input_grads.reshape(SEQUENCES, SEQ, D), totals[0], totals[1], totals[2], totals[3], totals[4], totals[5], totals[6], totals[7], totals[8], totals[9], totals[10], totals[11], totals[12])
```

```python
import functools
import math

import jax
import jax.numpy as jnp
from jax import lax
from jax.experimental import pallas as pl
from jax.experimental.pallas import tpu as pltpu
from jax.sharding import PartitionSpec as P

HEADS = 8
NORM_EPS = 1e-05
CONTRAST_SCALE = 32.0
CONTRAST_WEIGHT = 64.0
NEGATIVE = -1e30
LOG2E = math.log2(math.e)
F32 = jnp.float32
BF16 = jnp.bfloat16
MIB = 1 << 20
NN = (((1,), (0,)), ((), ()))
NT = (((1,), (1,)), ((), ()))
TN = (((0,), (0,)), ((), ()))
VMEM = pltpu.VMEM


def dot(a, b, dims=NN):
    return lax.dot_general(a, b, dims, preferred_element_type=F32)


def whole(shape):
    return pl.BlockSpec(shape, lambda *_: (0,) * len(shape))


def kernel_call(body, outs, out_specs, in_specs, grid=(1,), scratch=(), flops=0, nbytes=0, trans=0,
                limit=40, aliases=None, prefetch=0):
    return pl.pallas_call(
        body,
        out_shape=outs,
        grid_spec=pltpu.PrefetchScalarGridSpec(
            num_scalar_prefetch=prefetch,
            grid=grid,
            in_specs=in_specs,
            out_specs=out_specs,
            scratch_shapes=scratch,
        ),
        input_output_aliases=aliases or {},
        cost_estimate=pl.CostEstimate(flops=int(flops), bytes_accessed=int(nbytes), transcendentals=int(trans)),
        compiler_params=pltpu.CompilerParams(vmem_limit_bytes=limit * MIB),
    )


def struct(shape, dtype):
    return jax.ShapeDtypeStruct(shape, dtype)


def into(shape, dtype, block, index, previous):
    out = struct(shape, dtype)
    spec = pl.BlockSpec(block, lambda *_: index)
    return out, spec, ([] if previous is None else [previous])


def norm_stats(v):
    centered = v - jnp.mean(v, axis=-1, keepdims=True)
    rstd = lax.rsqrt(jnp.mean(centered * centered, axis=-1, keepdims=True) + NORM_EPS)
    return centered * rstd, rstd


def first_norm(seq, tokens, tables, gain, shift):
    rows, feats = tokens.shape[1:]
    fine = tables[2].shape[0]

    def body(tok, pa, qa, cb, sb, g, b, h_out, a_out):
        for c in range(rows // fine):
            at = pl.ds(c * fine, fine)
            pos = pa[c : c + 1, :] * cb[...] + qa[c : c + 1, :] * sb[...]
            h = tok[0, at, :].astype(F32) + pos
            h_out[at, :] = h
            z, _ = norm_stats(h)
            a_out[at, :] = (z * g[...] + b[...]).astype(BF16)

    return kernel_call(
        body,
        (struct((rows, feats), F32), struct((rows, feats), BF16)),
        (whole((rows, feats)), whole((rows, feats))),
        [pl.BlockSpec((1, rows, feats), lambda *_: (seq, 0, 0))]
        + [whole(t.shape) for t in tables]
        + [whole((1, feats))] * 2,
        nbytes=rows * feats * 8,
        flops=rows * feats * 20,
        limit=16,
    )(tokens, *tables, gain, shift)


def second_norm(h, keep, core, cross, offset, gain, shift):
    rows, feats = h.shape
    step = 64

    def body(h_ref, k_ref, c_ref, x_ref, o_ref, g, b, r_out, n_out):
        for c in range(rows // step):
            at = pl.ds(c * step, step)
            r = (
                h_ref[at, :]
                + (k_ref[0, at, :].astype(F32) + c_ref[0, at, :].astype(F32) + x_ref[at, :].astype(F32))
                + o_ref[...]
            )
            r_out[at, :] = r
            z, _ = norm_stats(r)
            n_out[at, :] = (z * g[...] + b[...]).astype(BF16)

    block = pl.BlockSpec((1, rows, feats), lambda *_: (0, 0, 0))
    return kernel_call(
        body,
        (struct((rows, feats), F32), struct((rows, feats), BF16)),
        (whole((rows, feats)), whole((rows, feats))),
        [whole((rows, feats)), block, block, whole((rows, feats))] + [whole((1, feats))] * 3,
        nbytes=rows * feats * 16,
        flops=rows * feats * 20,
        limit=16,
    )(h, keep, core, cross, offset, gain, shift)


def output_rows(seq, seqs, r1, keep, core, cross, offset, previous):
    rows, feats = r1.shape
    step = 64

    def body(r_ref, k_ref, c_ref, x_ref, o_ref, *rest):
        act_out, n_out, q_out = rest[-3:]
        for c in range(rows // step):
            at = pl.ds(c * step, step)
            y = (
                r_ref[at, :]
                + (k_ref[0, at, :].astype(F32) + c_ref[0, at, :].astype(F32) + x_ref[at, :].astype(F32))
                + o_ref[...]
            )
            act_out[0, at, :] = y.astype(BF16)
            q = lax.rsqrt(jnp.mean(y * y, axis=-1, keepdims=True) + NORM_EPS)
            n_out[at, :] = (y * q).astype(BF16)
            q_out[at, :] = jnp.broadcast_to(q, (step, 128))

    block = pl.BlockSpec((1, rows, feats), lambda *_: (0, 0, 0))
    act, act_spec, extra = into((seqs, rows, feats), BF16, (1, rows, feats), (seq, 0, 0), previous)
    return kernel_call(
        body,
        (act, struct((rows, feats), BF16), struct((rows, 128), F32)),
        (act_spec, whole((rows, feats)), whole((rows, 128))),
        [whole((rows, feats)), block, block, whole((rows, feats)), whole((1, feats))]
        + [pl.BlockSpec(memory_space=pl.ANY)] * len(extra),
        nbytes=rows * feats * 14,
        flops=rows * feats * 12,
        limit=16,
        aliases={5: 0} if extra else None,
    )(r1, keep, core, cross, offset, *extra)


def norm_backward(seq, seqs, v, keep, core, cross, gain, base, final, previous):
    rows, feats = v.shape
    step = 64

    def body(v_ref, k_ref, c_ref, x_ref, g, base_ref, *rest):
        if final:
            out, sums = rest[-2:]
        else:
            out, low, sums = rest[-3:]
        acc = [jnp.zeros((8, feats), F32) for _ in range(4)]
        for c in range(rows // step):
            at = pl.ds(c * step, step)
            got = k_ref[0, at, :].astype(F32) + c_ref[0, at, :].astype(F32) + x_ref[at, :].astype(F32)
            z, rstd = norm_stats(v_ref[at, :])
            w = got * g[...]
            inner = rstd * (w - jnp.mean(w, axis=-1, keepdims=True) - z * jnp.mean(w * z, axis=-1, keepdims=True))
            old = base_ref[at, :] if final else base_ref[0, at, :]
            new = old + inner
            if final:
                out[0, at, :] = new
            else:
                out[at, :] = new
                low[at, :] = new.astype(BF16)
            terms = [got * z, got] + ([] if final else [new, old])
            for k, term in enumerate(terms):
                acc[k] = acc[k] + jnp.sum(term.reshape(step // 8, 8, feats), axis=0)
        for k in range(4):
            sums[k : k + 1, :] = jnp.sum(acc[k], axis=0, keepdims=True)

    block = pl.BlockSpec((1, rows, feats), lambda *_: (0, 0, 0))
    if final:
        out, spec, extra = into((seqs, rows, feats), F32, (1, rows, feats), (seq, 0, 0), previous)
        outs, specs = (out, struct((4, feats), F32)), (spec, whole((4, feats)))
        base_spec = whole((rows, feats))
    else:
        extra = []
        outs = (struct((rows, feats), F32), struct((rows, feats), BF16), struct((4, feats), F32))
        specs = (whole((rows, feats)), whole((rows, feats)), whole((4, feats)))
        base_spec = pl.BlockSpec((1, rows, feats), lambda *_: (seq, 0, 0))
    return kernel_call(
        body,
        outs,
        specs,
        [whole((rows, feats)), block, block, whole((rows, feats)), whole((1, feats)), base_spec]
        + [pl.BlockSpec(memory_space=pl.ANY)] * len(extra),
        nbytes=rows * feats * 20,
        flops=rows * feats * 30,
        limit=20,
        aliases={6: 0} if extra else None,
    )(v, keep, core, cross, gain, base, *extra)


def pick(refs, index, out):
    for k, ref in enumerate(refs):

        @pl.when(index == k)
        def _(ref=ref):
            out[...] = ref[...].reshape(out.shape)


def attend_forward(seq, seqs, place, docs_row, docs_col, blocks, wqkv, q_shift, v_shift, wo, previous):
    rows, feats = blocks[0].shape
    parts = len(blocks)
    length = rows * parts
    width = wqkv.shape[2]
    size = feats // HEADS
    heads = width // size
    scale = LOG2E * size ** (-0.5)

    def body(t_ref, dr, dc, x0, x1, x2, x3, w, qb, vb, wo_ref, *rest):
        keep, send, cat, qkv, att, lse, keys, vals = rest[-8:]
        i = pl.program_id(0)
        rel = lax.bitwise_xor(i, t_ref[0])
        pick((x0, x1, x2, x3), rel, cat)
        x = cat[0]
        q = (dot(x, w[0]) + qb[...]).astype(BF16)
        k = dot(x, w[1]).astype(BF16)
        v = (dot(x, w[2]) + vb[...]).astype(BF16)
        qkv[0], qkv[1], qkv[2] = q, k, v
        at = pl.ds(pl.multiple_of(i * rows, rows), rows)
        keys[at, :] = k
        vals[at, :] = v

        for step in range(parts):

            @pl.when(i == step)
            def _(step=step):
                span = (step + 1) * rows
                same = dc[step * rows : span, :] == dr[:, :span]
                before = lax.broadcasted_iota(jnp.int32, (rows, span), 0) + step * rows >= lax.broadcasted_iota(
                    jnp.int32, (rows, span), 1
                )
                allowed = same & before
                for hd in range(heads):
                    cols = slice(hd * size, (hd + 1) * size)
                    s = jnp.where(allowed, dot(qkv[0, :, cols], keys[:span, cols], NT) * scale, NEGATIVE)
                    top = jnp.max(s, axis=-1, keepdims=True)
                    e = jnp.exp2(s - top)
                    total = jnp.sum(e, axis=-1, keepdims=True)
                    o = dot(e.astype(BF16), vals[:span, cols]) / total
                    att[0, :, cols] = o.astype(BF16)
                    lse[:, hd * 128 : (hd + 1) * 128] = jnp.broadcast_to(top + jnp.log2(total), (rows, 128))

        partial = dot(att[0], wo_ref[...]).astype(BF16)

        @pl.when(lax.rem(rel, 2) == 0)
        def _():
            keep[0] = partial

        @pl.when(lax.rem(rel, 2) == 1)
        def _():
            send[0] = partial

    rel_of = lambda i, t: lax.bitwise_xor(i, t[0])
    pair = pl.BlockSpec((1, rows, feats), lambda i, t: (lax.div(rel_of(i, t), 2), 0, 0))
    extra = [] if previous is None else list(previous)
    return kernel_call(
        body,
        (
            struct((2, rows, feats), BF16),
            struct((2, rows, feats), BF16),
            struct((seqs, length, feats), BF16),
            struct((3, length, width), BF16),
            struct((seqs, length, width), BF16),
            struct((length, heads * 128), F32),
        ),
        (
            pair,
            pair,
            pl.BlockSpec((1, rows, feats), lambda i, t: (seq, rel_of(i, t), 0)),
            pl.BlockSpec((3, rows, width), lambda i, t: (0, i, 0)),
            pl.BlockSpec((1, rows, width), lambda i, t: (seq, rel_of(i, t), 0)),
            pl.BlockSpec((rows, heads * 128), lambda i, t: (i, 0)),
        ),
        [
            whole((1, length)),
            whole((length, 1)),
            *[whole((rows, feats))] * 4,
            whole(wqkv.shape),
            whole((1, width)),
            whole((1, width)),
            whole(wo.shape),
        ]
        + [pl.BlockSpec(memory_space=pl.ANY)] * len(extra),
        grid=(parts,),
        scratch=[VMEM((length, width), BF16), VMEM((length, width), BF16)],
        flops=2 * length * feats * width * 4 + 5 * length * length * width // 2 * 2,
        nbytes=length * feats * 8,
        trans=length * length * heads // 2,
        prefetch=1,
        aliases={11: 2, 12: 4} if extra else None,
    )(place, docs_row, docs_col, *blocks, wqkv, q_shift, v_shift, wo, *extra)


def attend_backward(seq, seqs, place, docs_row, docs_col, blocks, qkv, att, lse, wqkv, wo, previous):
    rows, feats = blocks[0].shape
    parts = len(blocks)
    length = rows * parts
    width = wqkv.shape[2]
    size = feats // HEADS
    heads = width // size
    root = size ** (-0.5)
    scale = LOG2E * root

    def body(t_ref, dr, dc, x0, x1, x2, x3, qkv_ref, att_ref, lse_ref, w, wo_ref, *rest):
        keep, send, cat, gq_out, gk_out, gv_out, sums, gk, gv, ga, gq = rest[-11:]
        s_id = pl.program_id(0)
        i = parts - 1 - s_id
        rel = lax.bitwise_xor(i, t_ref[0])
        pick((x0, x1, x2, x3), rel, cat)

        @pl.when(s_id == 0)
        def _():
            gk[...] = jnp.zeros_like(gk)
            gv[...] = jnp.zeros_like(gv)
            sums[...] = jnp.zeros_like(sums)

        ga[...] = dot(cat[0], wo_ref[...], NT).astype(BF16)

        for step in range(parts):

            @pl.when(i == step)
            def _(step=step):
                span = (step + 1) * rows
                own = slice(step * rows, span)
                same = dc[own, :] == dr[:, :span]
                before = lax.broadcasted_iota(jnp.int32, (rows, span), 0) + step * rows >= lax.broadcasted_iota(
                    jnp.int32, (rows, span), 1
                )
                allowed = same & before
                for hd in range(heads):
                    cols = slice(hd * size, (hd + 1) * size)
                    q = qkv_ref[0, own, cols]
                    k = qkv_ref[1, :span, cols]
                    g = ga[:, cols]
                    s = dot(q, k, NT) * scale - lse_ref[:, hd * 128 : hd * 128 + 1]
                    p = jnp.exp2(jnp.where(allowed, s, NEGATIVE))
                    gp = dot(g, qkv_ref[2, :span, cols], NT)
                    row = jnp.sum(g.astype(F32) * att_ref[0, :, cols].astype(F32), axis=-1, keepdims=True)
                    gs = (p * (gp - row)).astype(BF16)
                    gq[:, cols] = (dot(gs, k) * root).astype(BF16)
                    gk[:span, cols] += dot(gs, q, TN)
                    gv[:span, cols] += dot(p.astype(BF16), g, TN)

        at = pl.ds(pl.multiple_of(i * rows, rows), rows)
        low_k = (gk[at, :] * root).astype(BF16)
        low_v = gv[at, :].astype(BF16)
        gq_out[0], gk_out[0], gv_out[0] = gq[...], low_k, low_v
        sums[0:1, :] += jnp.sum(gq[...].astype(F32), axis=0, keepdims=True)
        sums[1:2, :] += jnp.sum(low_v.astype(F32), axis=0, keepdims=True)
        partial = (dot(gq[...], w[0], NT) + dot(low_k, w[1], NT) + dot(low_v, w[2], NT)).astype(BF16)

        @pl.when(lax.rem(rel, 2) == 0)
        def _():
            keep[0] = partial

        @pl.when(lax.rem(rel, 2) == 1)
        def _():
            send[0] = partial

    rel_of = lambda s, t: lax.bitwise_xor(parts - 1 - s, t[0])
    pair = pl.BlockSpec((1, rows, feats), lambda s, t: (lax.div(rel_of(s, t), 2), 0, 0))
    part = pl.BlockSpec((1, rows, width), lambda s, t: (seq, rel_of(s, t), 0))
    extra = [] if previous is None else list(previous)
    return kernel_call(
        body,
        (
            struct((2, rows, feats), BF16),
            struct((2, rows, feats), BF16),
            struct((seqs, length, feats), BF16),
            *[struct((seqs, length, width), BF16)] * 3,
            struct((2, width), F32),
        ),
        (
            pair,
            pair,
            pl.BlockSpec((1, rows, feats), lambda s, t: (seq, rel_of(s, t), 0)),
            part,
            part,
            part,
            whole((2, width)),
        ),
        [
            whole((1, length)),
            whole((length, 1)),
            *[whole((rows, feats))] * 4,
            whole((3, length, width)),
            part,
            pl.BlockSpec((rows, heads * 128), lambda s, t: (parts - 1 - s, 0)),
            whole(wqkv.shape),
            whole(wo.shape),
        ]
        + [pl.BlockSpec(memory_space=pl.ANY)] * len(extra),
        grid=(parts,),
        scratch=[
            VMEM((length, width), F32),
            VMEM((length, width), F32),
            VMEM((rows, width), BF16),
            VMEM((rows, width), BF16),
        ],
        flops=2 * length * feats * width * 4 + 5 * length * length * width,
        nbytes=length * feats * 8,
        trans=length * length * heads // 2,
        prefetch=1,
        aliases={12: 2, 13: 3, 14: 4, 15: 5} if extra else None,
    )(place, docs_row, docs_col, *blocks, qkv, att, lse, wqkv, wo, *extra)


ORDER = (1, 3, 0, 2)


def ordered(s):
    return lax.select(s < 2, 2 * s + 1, 2 * s - 4)


def pair_specs(rows, feats):
    send = pl.BlockSpec((1, rows, feats), lambda s: (lax.min(s, 1), 0, 0))
    keep = pl.BlockSpec((1, rows, feats), lambda s: (lax.max(s - 2, 0), 0, 0))
    return keep, send


def feed_forward(seq, seqs, blocks, w_up, b_up, w_down, previous):
    rows, feats = blocks[0].shape
    units = w_up.shape[1]
    root = math.sqrt(2.0 / math.pi)

    def body(x0, x1, x2, x3, up, bu, down, *rest):
        keep, send, cat, act, slope = rest[-5:]
        s = pl.program_id(0)
        pick([(x0, x1, x2, x3)[k] for k in ORDER], s, cat)
        u = dot(cat[0], up[...]) + bu[...]
        sq = u * u
        th = jnp.tanh(root * u * (1.0 + 0.044715 * sq))
        half = 0.5 * (1.0 + th)
        g = (u * half).astype(BF16)
        act[0] = g
        slope[0] = (half + (0.5 * root) * u * (1.0 - th * th) * (1.0 + (3 * 0.044715) * sq)).astype(BF16)
        partial = dot(g, down[...]).astype(BF16)

        @pl.when(s < 2)
        def _():
            send[0] = partial

        @pl.when(s >= 2)
        def _():
            keep[0] = partial

    extra = [] if previous is None else list(previous)
    keep, send = pair_specs(rows, feats)
    part = lambda cols: pl.BlockSpec((1, rows, cols), lambda s: (seq, ordered(s), 0))
    length = rows * len(blocks)
    return kernel_call(
        body,
        (
            struct((2, rows, feats), BF16),
            struct((2, rows, feats), BF16),
            struct((seqs, length, feats), BF16),
            struct((seqs, length, units), BF16),
            struct((seqs, length, units), BF16),
        ),
        (keep, send, part(feats), part(units), part(units)),
        [*[whole((rows, feats))] * 4, whole(w_up.shape), whole((1, units)), whole(w_down.shape)]
        + [pl.BlockSpec(memory_space=pl.ANY)] * len(extra),
        grid=(4,),
        flops=4 * length * feats * units,
        nbytes=length * feats * 14,
        trans=length * units,
        aliases={7: 2, 8: 3, 9: 4} if extra else None,
    )(*blocks, w_up, b_up, w_down, *extra)


def feed_backward(seq, seqs, own, got, slope, w_up, w_down, previous):
    rows, feats = own.shape[1:]
    units = w_up.shape[1]

    def body(own_ref, got_ref, slope_ref, up, down, *rest):
        keep, send, cat, grad, sums = rest[-5:]
        s = pl.program_id(0)
        pick([got_ref.at[0], got_ref.at[1], own_ref.at[0], own_ref.at[1]], s, cat)
        gu = (dot(cat[0], down[...], NT) * slope_ref[0].astype(F32)).astype(BF16)
        grad[0] = gu
        total = jnp.sum(gu.astype(F32), axis=0, keepdims=True)

        @pl.when(s == 0)
        def _():
            sums[...] = total

        @pl.when(s > 0)
        def _():
            sums[...] += total

        partial = dot(gu, up[...], NT).astype(BF16)

        @pl.when(s < 2)
        def _():
            send[0] = partial

        @pl.when(s >= 2)
        def _():
            keep[0] = partial

    extra = [] if previous is None else list(previous)
    keep, send = pair_specs(rows, feats)
    part = lambda cols: pl.BlockSpec((1, rows, cols), lambda s: (seq, ordered(s), 0))
    length = rows * 4
    return kernel_call(
        body,
        (
            struct((2, rows, feats), BF16),
            struct((2, rows, feats), BF16),
            struct((seqs, length, feats), BF16),
            struct((seqs, length, units), BF16),
            struct((1, units), F32),
        ),
        (keep, send, part(feats), part(units), whole((1, units))),
        [whole((2, rows, feats)), whole((2, rows, feats)), part(units), whole(w_up.shape), whole(w_down.shape)]
        + [pl.BlockSpec(memory_space=pl.ANY)] * len(extra),
        grid=(4,),
        flops=4 * length * feats * units,
        nbytes=length * feats * 14,
        aliases={5: 2, 6: 3} if extra else None,
    )(own, got, slope, w_up, w_down, *extra)


def column(row):
    return jnp.transpose(jnp.broadcast_to(row, (8, row.shape[1])))[:, :1]


def contrast_scores(place, docs, labels, units):
    rows, feats = units[0].shape
    factor = CONTRAST_SCALE / feats * LOG2E
    count = len(units)

    def body(t_ref, doc_ref, lab_ref, *rest):
        refs, (exps, col_out, row_out, both) = rest[:count], rest[count:]
        s = pl.program_id(0)
        t = t_ref[0]

        @pl.when(s == 0)
        def _():
            for k in range(count):
                both[k] = refs[k][...]

        seq = lax.div(s, 2)
        part = lax.rem(s, 2) * 2
        mine = both[seq * 4 + part]
        own_at = lax.bitwise_xor(part, t)
        own_doc = column(doc_ref[seq, own_at])
        own_lab = column(lab_ref[seq, own_at])
        total = jnp.zeros((rows, 1), F32)
        total_pos = jnp.zeros((rows, 1), F32)
        for k in range(count):
            other = k // 4
            e = jnp.exp2(dot(mine, both[k], NT) * factor)
            at = lax.bitwise_xor(jnp.int32(k % 4), t)
            memory = (own_doc != doc_ref[other, at]) | (seq != other)
            e = jnp.where(memory, e, 0.0)
            total += jnp.sum(e, axis=-1, keepdims=True)
            total_pos += jnp.sum(jnp.where(own_lab == lab_ref[other, at], e, 0.0), axis=-1, keepdims=True)
            exps[:, k * rows : (k + 1) * rows] = e.astype(BF16)
        lanes = lax.broadcasted_iota(jnp.int32, (rows, 128), 1)
        wide = jnp.where(lanes == 0, total, total_pos)
        col_out[...] = wide
        row_out[...] = jnp.transpose(wide)[:8, :]

    return kernel_call(
        body,
        (
            struct((4 * rows, count * rows), BF16),
            struct((4 * rows, 128), F32),
            struct((8, 4 * rows), F32),
        ),
        (
            pl.BlockSpec((rows, count * rows), lambda s, t: (s, 0)),
            pl.BlockSpec((rows, 128), lambda s, t: (s, 0)),
            pl.BlockSpec((8, rows), lambda s, t: (0, s)),
        ),
        [whole(docs.shape), whole(labels.shape)] + [whole((rows, feats))] * count,
        grid=(4,),
        scratch=[VMEM((count, rows, feats), BF16)],
        flops=2 * 4 * rows * count * rows * feats,
        nbytes=count * rows * feats * 4,
        trans=4 * rows * count * rows,
        prefetch=1,
    )(place, docs, labels, *units)


def contrast_grads(place, labels, units, exps, col_sums, row_own, row_got, q_own, q_got, cot, cot_got):
    rows, feats = units[0].shape
    factor = CONTRAST_SCALE / feats
    count = len(units)
    seqs = count // 4

    def body(t_ref, lab_ref, *rest):
        refs = rest[:count]
        (e_ref, col, own, got, qo, qg, ct, cg, full, low0, low1, both, grad) = rest[count:]
        s = pl.program_id(0)
        t = t_ref[0]

        @pl.when(s == 0)
        def _():
            for k in range(count):
                both[k * rows : (k + 1) * rows, :] = refs[k][...]

        seq = lax.div(s, 2)
        half = lax.rem(s, 2)
        part = half * 2
        own_lab = column(lab_ref[seq, lax.bitwise_xor(part, t)])
        inv = CONTRAST_WEIGHT / col[...]
        all_i, pos_i = inv[:, 0:1], inv[:, 1:2]
        for k in range(count):
            other, piece = k // 4, k % 4
            source = own if piece % 2 == 0 else got
            at = (other * 2 + piece // 2) * rows
            inv_j = CONTRAST_WEIGHT / source[0:2, at : at + rows]
            same = own_lab == lab_ref[other, lax.bitwise_xor(jnp.int32(piece), t)]
            coef = (all_i + inv_j[0:1]) - jnp.where(same, pos_i + inv_j[1:2], 0.0)
            cols = slice(k * rows, (k + 1) * rows)
            grad[:, cols] = (e_ref[:, cols].astype(F32) * coef).astype(BF16)
        gn = dot(grad[...], both[...]) * factor
        n = both[pl.ds(pl.multiple_of((seq * 4 + part) * rows, rows), rows), :].astype(F32)
        inner = gn - n * jnp.mean(gn * n, axis=-1, keepdims=True)

        @pl.when(half == 0)
        def _():
            gy = ct[0].astype(F32) + qo[0, :, 0:1] * inner
            full[0] = gy
            low = gy.astype(BF16)

            @pl.when(seq == 0)
            def _():
                low0[0] = low

            @pl.when(seq == 1)
            def _():
                low1[0] = low

        @pl.when(half == 1)
        def _():
            low = (cg[0].astype(F32) + qg[0, :, 0:1] * inner).astype(BF16)

            @pl.when(seq == 0)
            def _():
                low0[0] = low

            @pl.when(seq == 1)
            def _():
                low1[0] = low

    per_seq = lambda cols: pl.BlockSpec((1, rows, cols), lambda s, t: (lax.div(s, 2), 0, 0))
    return kernel_call(
        body,
        (
            struct((seqs, rows, feats), F32),
            struct((2, rows, feats), BF16),
            struct((2, rows, feats), BF16),
        ),
        (
            per_seq(feats),
            pl.BlockSpec((1, rows, feats), lambda s, t: (lax.min(s, 1), 0, 0)),
            pl.BlockSpec((1, rows, feats), lambda s, t: (lax.max(s - 2, 0), 0, 0)),
        ),
        [whole(labels.shape)]
        + [whole((rows, feats))] * count
        + [
            pl.BlockSpec((rows, count * rows), lambda s, t: (s, 0)),
            pl.BlockSpec((rows, 128), lambda s, t: (s, 0)),
            whole((8, 4 * rows)),
            whole((8, 4 * rows)),
            per_seq(128),
            per_seq(128),
            per_seq(feats),
            per_seq(feats),
        ],
        grid=(4,),
        scratch=[VMEM((count * rows, feats), BF16), VMEM((rows, count * rows), BF16)],
        flops=2 * 4 * rows * count * rows * feats,
        nbytes=count * rows * feats * 5,
        prefetch=1,
    )(place, labels, *units, exps, col_sums, row_own, row_got, q_own, q_got, cot, cot_got)


def swap(value, axis, size, bit):
    return lax.ppermute(value, axis, [(i, i ^ bit) for i in range(size)])


CORE, CROSS = 1, 2


def tensor_swap(value, bit):
    return swap(value, "tensor", 4, bit)


def gather_rows(value):
    cross = tensor_swap(value, CROSS)
    core = tensor_swap(value, CORE)
    return [value, core, cross, tensor_swap(cross, CORE)]


def scatter_rows(keep, send):
    core = tensor_swap(send, CORE)
    cross = tensor_swap((keep[1].astype(F32) + core[1].astype(F32)).astype(BF16), CROSS)
    return keep, core, cross


def sum_over_dp(value, size, bits):
    me = lax.axis_index("dp")
    for bit in bits:
        half = value.shape[0] // 2
        high = (me & bit) != 0
        keep = lax.dynamic_slice_in_dim(value, jnp.where(high, half, 0), half, 0)
        send = lax.dynamic_slice_in_dim(value, jnp.where(high, 0, half), half, 0)
        got = swap(send, "dp", size, bit)
        value = (keep.astype(F32) + got.astype(F32)).astype(BF16)
    for bit in reversed(bits):
        high = (me & bit) != 0
        got = swap(value, "dp", size, bit)
        value = jnp.concatenate([jnp.where(high, got, value), jnp.where(high, value, got)])
    return value


def sum_pair(first, second, size):
    bits = [1 << k for k in range(size.bit_length() - 1)]
    other = bits[1::-1] + bits[2:]
    return sum_over_dp(first, size, bits), sum_over_dp(second, size, other)


def shards(
    dp_size,
    tokens,
    doc_ids,
    targets,
    cotangent,
    ln1_gain,
    ln1_bias,
    qkv_weight,
    query_bias,
    value_bias,
    output_weight,
    out_bias,
    ln2_gain,
    ln2_bias,
    up_weight,
    up_bias,
    down_weight,
    down_bias,
):
    seqs, rows, feats = tokens.shape
    length = doc_ids.shape[1]
    parts = length // rows
    me = lax.axis_index("tensor")
    place = me.reshape(1).astype(jnp.int32)
    vec = lambda v: v.astype(F32).reshape(1, -1)
    gain_one, shift_one, gain_two, shift_two = vec(ln1_gain), vec(ln1_bias), vec(ln2_gain), vec(ln2_bias)
    out_offset, down_offset, up_shift = vec(out_bias), vec(down_bias), vec(up_bias)
    q_shift, v_shift = vec(query_bias), vec(value_bias)

    fine = 16
    paired = (jnp.arange(feats, dtype=jnp.int32) // 2).astype(F32)
    freq = jnp.exp(paired * (-2.0 * math.log(10000.0) / feats))[None, :]
    odd = (jnp.arange(feats, dtype=jnp.int32) % 2 == 1)[None, :]
    coarse_at = (me * rows + fine * jnp.arange(rows // fine, dtype=jnp.int32)).astype(F32)[:, None] * freq
    fine_at = jnp.arange(fine, dtype=jnp.int32).astype(F32)[:, None] * freq
    sin_a, cos_a = jnp.sin(coarse_at), jnp.cos(coarse_at)
    tables = (jnp.where(odd, cos_a, sin_a), jnp.where(odd, -sin_a, cos_a), jnp.cos(fine_at), jnp.sin(fine_at))

    docs_f, labels_f = doc_ids.astype(F32), targets.astype(F32)
    docs4 = docs_f.reshape(seqs, parts, 1, rows)
    labels4 = labels_f.reshape(seqs, parts, 1, rows)
    each = range(seqs)
    docs_row = [docs_f[s : s + 1] for s in each]
    docs_col = [docs_f[s].reshape(length, 1) for s in each]

    hidden, normed = zip(*[first_norm(s, tokens, tables, gain_one, shift_one) for s in each])
    rows_one = [gather_rows(v) for v in normed]
    kept, shared = [], None
    attn = []
    for s in each:
        keep, send, cat_one, qkv, att, lse = attend_forward(
            s, seqs, place, docs_row[s], docs_col[s], rows_one[s], qkv_weight, q_shift, v_shift, output_weight, shared
        )
        shared = (cat_one, att)
        kept.append((qkv, lse))
        attn.append(scatter_rows(keep, send))
    cot_got = jnp.stack([tensor_swap(cotangent[s], CROSS) for s in each])
    stream, normed_two = zip(
        *[second_norm(hidden[s], *attn[s], out_offset, gain_two, shift_two) for s in each]
    )
    rows_two = [gather_rows(v) for v in normed_two]
    fed, ffn = None, []
    for s in each:
        keep, send, cat_two, hidden_act, slope = feed_forward(
            s, seqs, rows_two[s], up_weight, up_shift, down_weight, fed
        )
        fed = (cat_two, hidden_act, slope)
        ffn.append(scatter_rows(keep, send))
    activations, units, scales = None, [], []
    for s in each:
        activations, unit, scale = output_rows(s, seqs, stream[s], *ffn[s], down_offset, activations)
        units.append(unit)
        scales.append(scale)
    units_all = [block for unit in units for block in gather_rows(unit)]
    scales_own = jnp.stack(scales)
    scales_got = tensor_swap(scales_own, CROSS)

    exps, col_sums, row_sums = contrast_scores(place, docs4, labels4, units_all)
    row_got = tensor_swap(row_sums, CORE)
    grad_y, *low_y = contrast_grads(
        place, labels4, units_all, exps, col_sums, row_sums, row_got, scales_own, scales_got, cotangent, cot_got
    )
    own_cols = col_sums.reshape(seqs, 2, rows, 128)[:, 0, :, :2]
    loss = jnp.log(own_cols[..., 0]) - jnp.log(own_cols[..., 1])

    got_y = [tensor_swap(v, CORE) for v in low_y]
    back, gb, up_sums = None, [], []
    for s in each:
        keep, send, cat_y, grad_up, sums = feed_backward(
            s, seqs, low_y[s], got_y[s], slope, up_weight, down_weight, back
        )
        back = (cat_y, grad_up)
        up_sums.append(sums)
        gb.append(scatter_rows(keep, send))
    grad_down_w = jnp.einsum("snf,snd->fd", hidden_act, cat_y, preferred_element_type=F32).astype(BF16)
    grad_up_w = jnp.einsum("snd,snf->df", cat_two, grad_up, preferred_element_type=F32).astype(BF16)
    grad_down_w, grad_up_w = sum_pair(grad_down_w, grad_up_w, dp_size)

    grad_r, low_r, sums_two = zip(
        *[norm_backward(s, seqs, stream[s], *gb[s], gain_two, grad_y, False, None) for s in each]
    )
    rows_r = [gather_rows(v) for v in low_r]
    back, ga, head_sums = None, [], []
    for s in each:
        keep, send, *back, sums = attend_backward(
            s, seqs, place, docs_row[s], docs_col[s], rows_r[s], kept[s][0], att, kept[s][1], qkv_weight,
            output_weight, back,
        )
        head_sums.append(sums)
        ga.append(scatter_rows(keep, send))
    cat_r, *grad_qkv = back
    grad_out_w = jnp.einsum("yak,yac->kc", att, cat_r, preferred_element_type=F32).astype(BF16)
    grad_qkv_w = [
        jnp.einsum("snd,sne->de", cat_one, g, preferred_element_type=F32).astype(BF16) for g in grad_qkv
    ]
    first = jnp.concatenate([grad_qkv_w[0], grad_qkv_w[1]], axis=1)
    second = jnp.concatenate([grad_qkv_w[2], grad_out_w.reshape(feats, -1)], axis=1)
    first, second = sum_pair(first, second, dp_size)
    width = grad_out_w.shape[0]
    grad_qkv_w = jnp.stack([first[:, :width], first[:, width:], second[:, :width]]).astype(F32)
    grad_out_w = second[:, width:].reshape(width, feats).astype(F32)

    input_grad, sums_one = None, []
    for s in each:
        input_grad, sums = norm_backward(s, seqs, hidden[s], *ga[s], gain_one, grad_r[s], True, input_grad)
        sums_one.append(sums)
    total = lambda items: functools.reduce(jnp.add, items)
    heads_sum = total(head_sums)
    heads_row = jnp.pad(heads_sum.reshape(1, -1), ((0, 0), (0, feats - heads_sum.size)))
    small = jnp.concatenate([total(sums_one)[:2], total(sums_two), total(up_sums), heads_row])
    bit = 1
    while bit < dp_size:
        small = small + swap(small, "dp", dp_size, bit)
        bit *= 2
    local, small = small[6:], small[:6]
    for bit in (CORE, CROSS):
        small = small + tensor_swap(small, bit)
    return (
        activations,
        loss,
        input_grad,
        small[0],
        small[1],
        grad_qkv_w,
        local[1, : heads_sum.shape[1]],
        local[1, heads_sum.shape[1] : 2 * heads_sum.shape[1]],
        grad_out_w,
        small[4],
        small[2],
        small[3],
        grad_up_w.astype(F32),
        local[0],
        grad_down_w.astype(F32),
        small[5],
    )


def solution(mesh):
    in_specs = (
        P("dp", "tensor", None),
        P("dp", None),
        P("dp", None),
        P("dp", "tensor", None),
        P(),
        P(),
        P(None, None, "tensor"),
        P("tensor"),
        P("tensor"),
        P("tensor", None),
        P(),
        P(),
        P(),
        P(None, "tensor"),
        P("tensor"),
        P("tensor", None),
        P(),
    )
    out_specs = (
        P("dp", "tensor", None),
        P("dp", "tensor"),
        P("dp", "tensor", None),
        P(),
        P(),
        P(None, None, "tensor"),
        P("tensor"),
        P("tensor"),
        P("tensor", None),
        P(),
        P(),
        P(),
        P(None, "tensor"),
        P("tensor"),
        P("tensor", None),
        P(),
    )
    return jax.shard_map(
        functools.partial(shards, mesh.shape["dp"]),
        mesh=mesh,
        in_specs=in_specs,
        out_specs=out_specs,
        check_vma=False,
    )
```

```python
import functools
import math

import jax
import jax.numpy as jnp
from jax import lax
from jax.experimental import pallas as pl
from jax.experimental.pallas import tpu as pltpu
from jax.sharding import PartitionSpec as P

HEADS = 8
NORM_EPS = 1e-05
CONTRAST_SCALE = 32.0
CONTRAST_WEIGHT = 64.0
NEGATIVE = -1e30
LOG2E = math.log2(math.e)
F32 = jnp.float32
BF16 = jnp.bfloat16
MIB = 1 << 20
LIMIT, SMALL = 40, 16
COST = 0.02
NN = (((1,), (0,)), ((), ()))
NT = (((1,), (1,)), ((), ()))
TN = (((0,), (0,)), ((), ()))
VMEM = pltpu.VMEM


def dot(a, b, dims=NN):
    return lax.dot_general(a, b, dims, preferred_element_type=F32)


def whole(shape):
    return pl.BlockSpec(shape, lambda *_: (0,) * len(shape))


def kernel_call(body, outs, out_specs, in_specs, grid=(1,), scratch=(), flops=0, nbytes=0, trans=0,
                limit=LIMIT, aliases=None, prefetch=0, name=None):
    return pl.pallas_call(
        body,
        out_shape=outs,
        grid_spec=pltpu.PrefetchScalarGridSpec(
            num_scalar_prefetch=prefetch,
            grid=grid,
            in_specs=in_specs,
            out_specs=out_specs,
            scratch_shapes=scratch,
        ),
        name=name,
        input_output_aliases=aliases or {},
        cost_estimate=pl.CostEstimate(
            flops=int(flops * COST), bytes_accessed=int(nbytes * COST), transcendentals=int(trans * COST)
        ),
        compiler_params=pltpu.CompilerParams(vmem_limit_bytes=limit * MIB),
    )


def struct(shape, dtype):
    return jax.ShapeDtypeStruct(shape, dtype)


ANY = pl.BlockSpec(memory_space=pl.ANY)
HBM = pl.BlockSpec(memory_space=pltpu.HBM)
DMA = pltpu.SemaphoreType.DMA


def move(src, dst, sem):
    copy = pltpu.make_async_copy(src, dst, sem)
    copy.start()
    return copy


def column(row):
    return jnp.transpose(jnp.broadcast_to(row, (8, row.shape[1])))[:, :1]


def norm_stats(v):
    centered = v - jnp.mean(v, axis=-1, keepdims=True)
    rstd = lax.rsqrt(jnp.mean(centered * centered, axis=-1, keepdims=True) + NORM_EPS)
    return centered * rstd, rstd


ROW_STEPS = 4


def row_blocks(rows, cols):
    return pl.BlockSpec((rows // ROW_STEPS, cols), lambda i: (i, 0))


def first_norm(seq, tokens, tables, gain, shift):
    rows, feats = tokens.shape[1:]
    fine = tables[2].shape[0]
    step = rows // ROW_STEPS

    def body(tok, pa, qa, cb, sb, g, b, h_out, a_out):
        i = pl.program_id(0)
        for c in range(step // fine):
            at = pl.ds(c * fine, fine)
            row = pl.ds(i * (step // fine) + c, 1)
            pos = pa[row, :] * cb[...] + qa[row, :] * sb[...]
            h = tok[0, at, :].astype(F32) + pos
            h_out[at, :] = h
            z, _ = norm_stats(h)
            a_out[at, :] = (z * g[...] + b[...]).astype(BF16)

    return kernel_call(
        body,
        (struct((rows, feats), F32), struct((rows, feats), BF16)),
        (row_blocks(rows, feats), row_blocks(rows, feats)),
        [pl.BlockSpec((1, step, feats), lambda i: (seq, i, 0))]
        + [whole(t.shape) for t in tables]
        + [whole((1, feats))] * 2,
        grid=(ROW_STEPS,),
        nbytes=rows * feats * 8,
        limit=SMALL,
        name="first_norm",
    )(tokens, *tables, gain, shift)


def joined(parts, at):
    return functools.reduce(jnp.add, [p[at, :].astype(F32) for p in parts])


def second_norm(h, parts, offset, gain, shift):
    rows, feats = h.shape
    chunk = 32
    step = rows // ROW_STEPS

    def body(h_ref, k_ref, c_ref, x_ref, o_ref, g, b, r_out, n_out):
        for c in range(step // chunk):
            at = pl.ds(c * chunk, chunk)
            r = h_ref[at, :] + joined((k_ref, c_ref, x_ref), at) + o_ref[...]
            r_out[at, :] = r
            z, _ = norm_stats(r)
            n_out[at, :] = (z * g[...] + b[...]).astype(BF16)

    block = row_blocks(rows, feats)
    return kernel_call(
        body,
        (struct((rows, feats), F32), struct((rows, feats), BF16)),
        (block, block),
        [block] * 4 + [whole((1, feats))] * 3,
        grid=(ROW_STEPS,),
        nbytes=rows * feats * 16,
        limit=SMALL,
        name="second_norm",
    )(h, *parts, offset, gain, shift)


EXTRA = 16


def output_rows(seq, seqs, r1, parts, offset, previous):
    rows, feats = r1.shape
    step, chunk = 128, 32

    def body(r_ref, k_ref, c_ref, x_ref, o_ref, *rest):
        act_out, n_out, q_all = rest[-3:]
        i = pl.program_id(0)
        for c in range(step // chunk):
            at = pl.ds(c * chunk, chunk)
            y = r_ref[at, :] + joined((k_ref, c_ref, x_ref), at) + o_ref[...]
            act_out[0, at, :] = y.astype(BF16)
            q = lax.rsqrt(jnp.mean(y * y, axis=-1, keepdims=True) + NORM_EPS)
            n_out[pl.ds(pl.multiple_of(i * step + c * chunk, chunk), chunk), :] = (y * q).astype(BF16)
            q_all[at, :] = jnp.broadcast_to(q, (chunk, step))

        @pl.when(i == 0)
        def _():
            n_out[rows:, :] = jnp.zeros((EXTRA, feats), BF16)

        row = jnp.transpose(q_all[...])[:EXTRA, :]
        high = row.astype(BF16).astype(F32)
        which = lax.broadcasted_iota(jnp.int32, (EXTRA, step), 0)
        lanes = pl.ds(pl.multiple_of(i * step, step), step)
        n_out[rows:, lanes] = jnp.where(which == 0, high, jnp.where(which == 1, row - high, 0.0)).astype(BF16)

    block = pl.BlockSpec((step, feats), lambda i: (i, 0))
    extra = [] if previous is None else [previous]
    return kernel_call(
        body,
        (struct((seqs, rows, feats), BF16), struct((rows + EXTRA, feats), BF16)),
        (pl.BlockSpec((1, step, feats), lambda i: (seq, i, 0)), whole((rows + EXTRA, feats))),
        [block] * 4 + [whole((1, feats))] + [ANY] * len(extra),
        grid=(rows // step,),
        scratch=[VMEM((step, step), F32)],
        nbytes=rows * feats * 14,
        aliases={5: 0} if extra else None,
        limit=SMALL,
        name="output_rows",
    )(r1, *parts, offset, *extra)


def norm_backward(seq, seqs, v, parts, gain, base, final, previous):
    rows, feats = v.shape
    chunk = 16
    step = rows // ROW_STEPS

    def body(v_ref, k_ref, c_ref, x_ref, g, base_ref, *rest):
        if final:
            out, sums = rest[-2:]
        else:
            out, low, sums = rest[-3:]
        acc = [jnp.zeros((8, feats), F32) for _ in range(2 if final else 4)]
        for c in range(step // chunk):
            at = pl.ds(c * chunk, chunk)
            got = joined((k_ref, c_ref, x_ref), at)
            z, rstd = norm_stats(v_ref[at, :])
            w = got * g[...]
            inner = rstd * (w - jnp.mean(w, axis=-1, keepdims=True) - z * jnp.mean(w * z, axis=-1, keepdims=True))
            old = base_ref[at, :] if final else base_ref[0, at, :]
            new = old + inner
            if final:
                out[0, at, :] = new
            else:
                out[at, :] = new
                low[at, :] = new.astype(BF16)
            terms = [got * z, got] + ([] if final else [new, old])
            for k, term in enumerate(terms):
                acc[k] = acc[k] + jnp.sum(term.reshape(chunk // 8, 8, feats), axis=0)

        @pl.when(pl.program_id(0) == 0)
        def _():
            sums[...] = jnp.zeros_like(sums)

        for k, term in enumerate(acc):
            sums[k : k + 1, :] += jnp.sum(term, axis=0, keepdims=True)

    block = row_blocks(rows, feats)
    extra = [] if previous is None else [previous]
    seq_block = pl.BlockSpec((1, step, feats), lambda i: (seq, i, 0))
    if final:
        outs, specs = (struct((seqs, rows, feats), F32), struct((4, feats), F32)), (seq_block, whole((4, feats)))
    else:
        outs = (struct((rows, feats), F32), struct((rows, feats), BF16), struct((4, feats), F32))
        specs = (block, block, whole((4, feats)))
    return kernel_call(
        body,
        outs,
        specs,
        [block] * 4 + [whole((1, feats)), block if final else seq_block] + [ANY] * len(extra),
        grid=(ROW_STEPS,),
        nbytes=rows * feats * 20,
        aliases={6: 0} if extra else None,
        limit=SMALL,
        name="norm_backward",
    )(v, *parts, gain, base, *extra)


def send_block(refs, rel, src, sems):
    for r, ref in enumerate(refs):

        @pl.when(rel == r)
        def _(r=r, ref=ref):
            pltpu.make_async_copy(src, ref, sems.at[r]).start()


def wait_blocks(refs, src, sems):
    for r, ref in enumerate(refs):
        pltpu.make_async_copy(src, ref, sems.at[r]).wait()


def lane_pair(first, second, rows):
    lanes = lax.broadcasted_iota(jnp.int32, (rows, 128), 1)
    return jnp.where(lanes == 0, first, second)


def attend_forward(seq, seqs, place, docs_row, blocks, wqkv, q_shift, v_shift, wo, previous):
    rows, feats = blocks[0].shape
    parts = len(blocks)
    length = rows * parts
    width = wqkv.shape[2]
    size = feats // HEADS
    heads = width // size
    scale = LOG2E * size ** (-0.5)

    def body(t_ref, dr, qb, vb, *rest):
        x_refs, (w_ref, wo_ref), rest = rest[:4], rest[4:6], rest[6:]
        p_refs, (cat, qkv_out, att_out, lse_out), rest = rest[-19:-15], rest[-15:-11], rest[-11:]
        xs, w, wov, qkv, att, lse, ps, in_sem, p_sem, c_sem, o_sem = rest
        t = t_ref[0]
        load_w = move(w_ref, w, in_sem.at[4])
        for r in range(parts):
            at = lax.bitwise_xor(jnp.int32(r), t)
            move(x_refs[r], xs.at[at], in_sem.at[at])
        load_wo = move(wo_ref, wov, in_sem.at[5])
        pending = []

        def project(i):
            pltpu.make_async_copy(x_refs[0], xs.at[i], in_sem.at[i]).wait()
            rel = lax.bitwise_xor(jnp.int32(i), t)
            pending.append(move(xs.at[i], cat.at[seq, pl.ds(pl.multiple_of(rel * rows, rows), rows)], c_sem.at[i]))
            x = xs[i]
            at = slice(i * rows, (i + 1) * rows)
            qkv[0, at, :] = (dot(x, w[0]) + qb[...]).astype(BF16)
            qkv[1, at, :] = dot(x, w[1]).astype(BF16)
            qkv[2, at, :] = (dot(x, w[2]) + vb[...]).astype(BF16)

        load_w.wait()
        project(0)
        load_wo.wait()
        for i in range(parts):
            if i + 1 < parts:
                project(i + 1)
            span = (i + 1) * rows
            own = slice(i * rows, span)
            same = column(dr[:, own]) == dr[:, :span]
            before = lax.broadcasted_iota(jnp.int32, (rows, span), 0) + i * rows >= lax.broadcasted_iota(
                jnp.int32, (rows, span), 1
            )
            allowed = same & before
            logs = []
            for hd in range(heads):
                cols = slice(hd * size, (hd + 1) * size)
                s = jnp.where(allowed, dot(qkv[0, own, cols], qkv[1, :span, cols], NT) * scale, NEGATIVE)
                top = jnp.max(s, axis=-1, keepdims=True)
                e = jnp.exp2(s - top)
                total = jnp.sum(e, axis=-1, keepdims=True)
                att[i, :, cols] = (dot(e.astype(BF16), qkv[2, :span, cols]) / total).astype(BF16)
                logs.append(top + jnp.log2(total))
            lse[own, :] = lane_pair(logs[0], logs[-1], rows)
            ps[i] = dot(att[i], wov[...]).astype(BF16)
            rel = lax.bitwise_xor(jnp.int32(i), t)
            send_block(p_refs, rel, ps.at[i], p_sem)
            pending.append(
                move(att.at[i], att_out.at[seq, pl.ds(pl.multiple_of(rel * rows, rows), rows)], o_sem.at[i])
            )
        pending.append(move(qkv, qkv_out, in_sem.at[4]))
        pending.append(move(lse, lse_out, in_sem.at[5]))
        for copy in pending:
            copy.wait()
        wait_blocks(p_refs, ps.at[0], p_sem)

    extra = [] if previous is None else list(previous)
    return kernel_call(
        body,
        (
            *[struct((rows, feats), BF16)] * 4,
            struct((seqs, length, feats), BF16),
            struct((3, length, width), BF16),
            struct((seqs, length, width), BF16),
            struct((length, 128), F32),
        ),
        (ANY,) * 4 + (HBM,) * 4,
        [pl.BlockSpec(memory_space=pltpu.SMEM), whole((1, length)), whole((1, width)), whole((1, width))]
        + [ANY] * 4
        + [HBM] * (2 + len(extra)),
        scratch=[
            VMEM((parts, rows, feats), BF16),
            VMEM(wqkv.shape, BF16),
            VMEM(wo.shape, BF16),
            VMEM((3, length, width), BF16),
            VMEM((parts, rows, width), BF16),
            VMEM((length, 128), F32),
            VMEM((parts, rows, feats), BF16),
            DMA((6,)),
            DMA((4,)),
            DMA((4,)),
            DMA((4,)),
        ],
        flops=2 * length * feats * width * 4 + 5 * length * length * width,
        nbytes=length * feats * 8,
        trans=length * length * heads // 2,
        aliases={10: 4, 11: 6} if extra else None,
        name="attend_forward",
    )(place, docs_row, q_shift, v_shift, *blocks, wqkv, wo, *extra)


def attend_backward(seq, seqs, place, docs_row, blocks, qkv, att, lse, wqkv, wo, previous):
    rows, feats = blocks[0].shape
    parts = len(blocks)
    length = rows * parts
    width = wqkv.shape[2]
    size = feats // HEADS
    heads = width // size
    root = size ** (-0.5)
    scale = LOG2E * root

    def body(t_ref, dr, *rest):
        x_refs, (qkv_ref, att_ref, lse_ref, w_ref, wo_ref), rest = rest[:4], rest[4:9], rest[9:]
        p_refs, (cat, gq_out, gk_out, gv_out, sums), rest = rest[-23:-19], rest[-19:-14], rest[-14:]
        xs, w, wov, qkvv, attv, lsev, gk, gv, ga, low, ps, in_sem, p_sem, o_sem = rest
        t = t_ref[0]
        load_wo = move(wo_ref, wov, in_sem.at[4])
        for r in (3, 2, 1, 0):
            at = lax.bitwise_xor(jnp.int32(r), t)
            move(x_refs[r], xs.at[at], in_sem.at[at])
        loads = [move(qkv_ref, qkvv, in_sem.at[5]), move(lse_ref, lsev, in_sem.at[6])]
        for i in range(parts):
            rel = lax.bitwise_xor(jnp.int32(i), t)
            at = pl.ds(pl.multiple_of(rel * rows, rows), rows)
            loads.append(move(att_ref.at[seq, at], attv.at[i], in_sem.at[8 + i]))
        load_w = move(w_ref, w, in_sem.at[7])
        pending = []

        def project(i):
            pltpu.make_async_copy(x_refs[0], xs.at[i], in_sem.at[i]).wait()
            rel = lax.bitwise_xor(jnp.int32(i), t)
            pending.append(
                move(xs.at[i], cat.at[seq, pl.ds(pl.multiple_of(rel * rows, rows), rows)], o_sem.at[i])
            )
            ga[i] = dot(xs[i], wov[...], NT).astype(BF16)

        load_wo.wait()
        project(parts - 1)
        for copy in loads:
            copy.wait()
        load_w.wait()
        q_sum = jnp.zeros((1, width), F32)
        v_sum = jnp.zeros((1, width), F32)
        for i in reversed(range(parts)):
            if i:
                project(i - 1)
            span = (i + 1) * rows
            own = slice(i * rows, span)
            same = column(dr[:, own]) == dr[:, :span]
            before = lax.broadcasted_iota(jnp.int32, (rows, span), 0) + i * rows >= lax.broadcasted_iota(
                jnp.int32, (rows, span), 1
            )
            allowed = same & before
            for hd in range(heads):
                cols = slice(hd * size, (hd + 1) * size)
                q = qkvv[0, own, cols]
                k = qkvv[1, :span, cols]
                g = ga[i, :, cols]
                s = dot(q, k, NT) * scale - lsev[own, hd : hd + 1]
                p = jnp.exp2(jnp.where(allowed, s, NEGATIVE))
                gp = dot(g, qkvv[2, :span, cols], NT)
                row = jnp.sum(g.astype(F32) * attv[i, :, cols].astype(F32), axis=-1, keepdims=True)
                gs = (p * (gp - row)).astype(BF16)
                low[0, own, cols] = (dot(gs, k) * root).astype(BF16)
                new_k = dot(gs, q, TN)
                new_v = dot(p.astype(BF16), g, TN)
                if i == parts - 1:
                    gk[:span, cols] = new_k
                    gv[:span, cols] = new_v
                else:
                    gk[:span, cols] += new_k
                    gv[:span, cols] += new_v
            low[1, own, :] = (gk[own, :] * root).astype(BF16)
            low[2, own, :] = gv[own, :].astype(BF16)
            q_sum += jnp.sum(low[0, own, :].astype(F32), axis=0, keepdims=True)
            v_sum += jnp.sum(low[2, own, :].astype(F32), axis=0, keepdims=True)
            ps[i] = (
                dot(low[0, own, :], w[0], NT) + dot(low[1, own, :], w[1], NT) + dot(low[2, own, :], w[2], NT)
            ).astype(BF16)
            rel = lax.bitwise_xor(jnp.int32(i), t)
            send_block(p_refs, rel, ps.at[i], p_sem)
            at = pl.ds(pl.multiple_of(rel * rows, rows), rows)
            for c, out in enumerate((gq_out, gk_out, gv_out)):
                pending.append(move(low.at[c, own], out.at[seq, at], o_sem.at[4 + 3 * i + c]))
        sums[0:1, :] = q_sum
        sums[1:2, :] = v_sum
        for copy in pending:
            copy.wait()
        wait_blocks(p_refs, ps.at[0], p_sem)

    extra = [] if previous is None else list(previous)
    return kernel_call(
        body,
        (
            *[struct((rows, feats), BF16)] * 4,
            struct((seqs, length, feats), BF16),
            *[struct((seqs, length, width), BF16)] * 3,
            struct((2, width), F32),
        ),
        (ANY,) * 4 + (HBM,) * 4 + (whole((2, width)),),
        [pl.BlockSpec(memory_space=pltpu.SMEM), whole((1, length))] + [ANY] * 4 + [HBM] * (5 + len(extra)),
        scratch=[
            VMEM((parts, rows, feats), BF16),
            VMEM(wqkv.shape, BF16),
            VMEM(wo.shape, BF16),
            VMEM((3, length, width), BF16),
            VMEM((parts, rows, width), BF16),
            VMEM((length, 128), F32),
            VMEM((length, width), F32),
            VMEM((length, width), F32),
            VMEM((parts, rows, width), BF16),
            VMEM((3, length, width), BF16),
            VMEM((parts, rows, feats), BF16),
            DMA((12,)),
            DMA((4,)),
            DMA((16,)),
        ],
        flops=2 * length * feats * width * 4 + 10 * length * length * width,
        nbytes=length * feats * 8,
        trans=length * length * heads // 2,
        aliases={11: 4, 12: 5, 13: 6, 14: 7} if extra else None,
        name="attend_backward",
    )(place, docs_row, *blocks, qkv, att, lse, wqkv, wo, *extra)


ORDER = (3, 1, 2, 0)


def feed_forward(seq, seqs, blocks, w_up, b_up, w_down, previous):
    rows, feats = blocks[0].shape
    parts = len(blocks)
    length = rows * parts
    units = w_up.shape[1]
    root = math.sqrt(2.0 / math.pi)

    def body(bu, *rest):
        x_refs, (up_ref, down_ref), rest = rest[:4], rest[4:6], rest[6:]
        p_refs, (cat, act_out, slope_out), rest = rest[-17:-13], rest[-13:-10], rest[-10:]
        xs, up, down, u, act, slope, ps, in_sem, p_sem, o_sem = rest
        load_up = move(up_ref, up, in_sem.at[4])
        loads = {r: move(x_refs[r], xs.at[r], in_sem.at[r]) for r in ORDER}
        load_down = move(down_ref, down, in_sem.at[5])
        pending = []

        def project(k):
            r = ORDER[k]
            loads[r].wait()
            pending.append(move(xs.at[r], cat.at[seq, pl.ds(r * rows, rows)], o_sem.at[r]))
            u[k % 2] = dot(xs[r], up[...]) + bu[...]

        load_up.wait()
        project(0)
        load_down.wait()
        for k, r in enumerate(ORDER):
            if k + 1 < parts:
                project(k + 1)
            v = u[k % 2]
            sq = v * v
            th = jnp.tanh(v * (root + (root * 0.044715) * sq))
            half = 0.5 + 0.5 * th
            g = (v * half).astype(BF16)
            act[r] = g
            slope[r] = (half + v * (1.0 - th * th) * (0.5 * root + (1.5 * 0.044715 * root) * sq)).astype(BF16)
            ps[r] = dot(g, down[...]).astype(BF16)
            at = pl.ds(r * rows, rows)
            pending.append(move(ps.at[r], p_refs[r], p_sem.at[r]))
            pending.append(move(act.at[r], act_out.at[seq, at], o_sem.at[4 + r]))
            pending.append(move(slope.at[r], slope_out.at[seq, at], o_sem.at[8 + r]))
        for copy in pending:
            copy.wait()

    extra = [] if previous is None else list(previous)
    return kernel_call(
        body,
        (
            *[struct((rows, feats), BF16)] * 4,
            struct((seqs, length, feats), BF16),
            struct((seqs, length, units), BF16),
            struct((seqs, length, units), BF16),
        ),
        (ANY,) * 4 + (HBM,) * 3,
        [whole((1, units))] + [ANY] * 4 + [HBM] * (2 + len(extra)),
        scratch=[
            VMEM((parts, rows, feats), BF16),
            VMEM(w_up.shape, BF16),
            VMEM(w_down.shape, BF16),
            VMEM((2, rows, units), F32),
            VMEM((parts, rows, units), BF16),
            VMEM((parts, rows, units), BF16),
            VMEM((parts, rows, feats), BF16),
            DMA((6,)),
            DMA((4,)),
            DMA((12,)),
        ],
        flops=4 * length * feats * units,
        nbytes=length * feats * 14,
        trans=length * units,
        aliases={7: 4, 8: 5, 9: 6} if extra else None,
        name="feed_forward",
    )(b_up, *blocks, w_up, w_down, *extra)


def feed_backward(seq, seqs, own, got, slope, w_up, w_down, previous):
    rows, feats = own.shape[1:]
    parts = 4
    length = rows * parts
    units = w_up.shape[1]

    def body(own_ref, got_ref, slope_ref, up_ref, down_ref, *rest):
        p_refs, (grad_out, sums), rest = rest[-16:-12], rest[-12:-10], rest[-10:]
        ys, up, down, slopes, u, grad, ps, in_sem, p_sem, o_sem = rest
        load_down = move(down_ref, down, in_sem.at[4])
        loads, slope_loads = {}, {}
        for r in ORDER:
            loads[r] = move((got_ref if r % 2 else own_ref).at[r // 2], ys.at[r], in_sem.at[r])
            slope_loads[r] = move(slope_ref.at[seq, pl.ds(r * rows, rows)], slopes.at[r], in_sem.at[6 + r])
        load_up = move(up_ref, up, in_sem.at[5])
        pending = []

        def project(k):
            r = ORDER[k]
            loads[r].wait()
            slope_loads[r].wait()
            u[k % 2] = dot(ys[r], down[...], NT)

        load_down.wait()
        project(0)
        load_up.wait()
        total = jnp.zeros((8, units), F32)
        for k, r in enumerate(ORDER):
            if k + 1 < parts:
                project(k + 1)
            gu = (u[k % 2] * slopes[r].astype(F32)).astype(BF16)
            grad[r] = gu
            total += jnp.sum(gu.astype(F32).reshape(rows // 8, 8, units), axis=0)
            ps[r] = dot(gu, up[...], NT).astype(BF16)
            pending.append(move(ps.at[r], p_refs[r], p_sem.at[r]))
            pending.append(move(grad.at[r], grad_out.at[seq, pl.ds(r * rows, rows)], o_sem.at[4 + r]))
        sums[...] = jnp.sum(total, axis=0, keepdims=True)
        for copy in pending:
            copy.wait()

    extra = [] if previous is None else [previous]
    return kernel_call(
        body,
        (
            *[struct((rows, feats), BF16)] * 4,
            struct((seqs, length, units), BF16),
            struct((1, units), F32),
        ),
        (ANY,) * 4 + (HBM, whole((1, units))),
        [ANY] * 2 + [HBM] * (3 + len(extra)),
        scratch=[
            VMEM((parts, rows, feats), BF16),
            VMEM(w_up.shape, BF16),
            VMEM(w_down.shape, BF16),
            VMEM((parts, rows, units), BF16),
            VMEM((2, rows, units), F32),
            VMEM((parts, rows, units), BF16),
            VMEM((parts, rows, feats), BF16),
            DMA((10,)),
            DMA((4,)),
            DMA((8,)),
        ],
        flops=4 * length * feats * units,
        nbytes=length * feats * 14,
        aliases={5: 4} if extra else None,
        name="feed_backward",
    )(own, got, slope, w_up, w_down, *extra)


def contrast_scores(place, docs, labels, units):
    rows, feats = units[0].shape[0] - EXTRA, units[0].shape[1]
    factor = CONTRAST_SCALE / feats * LOG2E
    count = len(units)
    seqs = count // 4

    def body(t_ref, doc_ref, lab_ref, *rest):
        refs, (exp_out, col_out, row_out, loss_out, both, exps, in_sem, out_sem) = rest[:count], rest[count:]
        t = t_ref[0]
        loads = [move(refs[k].at[pl.ds(0, rows)], both.at[k], in_sem.at[k]) for k in range(count)]
        pending = []
        for s in range(4):
            seq, part = s // 2, s % 2 * 2
            if s == 0:
                loads[0].wait()
            own_at = lax.bitwise_xor(jnp.int32(part), t)
            own_doc = column(doc_ref[seq, own_at])
            own_lab = column(lab_ref[seq, own_at])
            total = jnp.zeros((rows, 128), F32)
            total_pos = jnp.zeros((rows, 128), F32)
            for k in range(count):
                if s == 0 and k:
                    loads[k].wait()
                other = k // 4
                e = jnp.exp2(dot(both[seq * 4 + part], both[k], NT) * factor)
                at = lax.bitwise_xor(jnp.int32(k % 4), t)
                if seq == other:
                    e = jnp.where(own_doc != doc_ref[other, at], e, 0.0)
                picked = jnp.where(own_lab == lab_ref[other, at], e, 0.0)
                for c in range(rows // 128):
                    lanes = slice(c * 128, (c + 1) * 128)
                    total += e[:, lanes]
                    total_pos += picked[:, lanes]
                exps[s, :, k * rows : (k + 1) * rows] = e.astype(BF16)
            pending.append(move(exps.at[s], exp_out.at[s], out_sem.at[s]))
            wide = lane_pair(
                jnp.sum(total, axis=-1, keepdims=True), jnp.sum(total_pos, axis=-1, keepdims=True), rows
            )
            col_out[s * rows : (s + 1) * rows, :] = wide
            flat = jnp.transpose(wide)[:8, :]
            row_out[:, s * rows : (s + 1) * rows] = flat
            if part == 0:
                logs = jnp.log(flat)
                loss_out[seq : seq + 1, :] = logs[0:1] - logs[1:2]
        for copy in pending:
            copy.wait()

    return kernel_call(
        body,
        (
            struct((4, rows, count * rows), BF16),
            struct((4 * rows, 128), F32),
            struct((8, 4 * rows), F32),
            struct((seqs, rows), F32),
        ),
        (HBM, whole((4 * rows, 128)), whole((8, 4 * rows)), whole((seqs, rows))),
        [pl.BlockSpec(memory_space=pltpu.SMEM), whole(docs.shape), whole(labels.shape)] + [ANY] * count,
        scratch=[VMEM((count, rows, feats), BF16), VMEM((4, rows, count * rows), BF16), DMA((count,)), DMA((4,))],
        flops=2 * 4 * rows * count * rows * feats,
        nbytes=count * rows * feats * 4,
        trans=4 * rows * count * rows,
        name="contrast_scores",
    )(place, docs, labels, *units)


def contrast_grads(place, labels, units, exps, col_sums, row_own, row_got, cot, cot_got):
    rows, feats = units[0].shape[0] - EXTRA, units[0].shape[1]
    factor = CONTRAST_SCALE / feats
    count = len(units)
    seqs = count // 4

    def body(t_ref, lab_ref, col, own, got, *rest):
        refs, (e_ref, cot_ref, *other_refs), rest = rest[:count], rest[count : count + 4], rest[count + 4 :]
        full, low0, low1, both, exps, scales, cots, grad, full_v, low_v, in_sem, e_sem, q_sem, c_sem, o_sem = rest
        t = t_ref[0]
        e_loads = [move(e_ref.at[0], exps.at[0], e_sem.at[0])]
        loads = [
            move(refs[k].at[pl.ds(0, rows)], both.at[pl.ds(k * rows, rows)], in_sem.at[k]) for k in range(count)
        ]
        e_loads += [move(e_ref.at[s], exps.at[s], e_sem.at[s]) for s in range(1, 4)]
        small = []
        for s in range(4):
            seq, half = s // 2, s % 2
            small.append(
                (
                    move(refs[seq * 4 + half * 2].at[pl.ds(rows, EXTRA)], scales.at[s], q_sem.at[s]),
                    move(other_refs[seq] if half else cot_ref.at[seq], cots.at[s], c_sem.at[s]),
                )
            )
        pending = []

        def weigh(s):
            seq, half = s // 2, s % 2
            own_lab = column(lab_ref[seq, lax.bitwise_xor(jnp.int32(half * 2), t)])
            inv = CONTRAST_WEIGHT / col[s * rows : (s + 1) * rows, :]
            all_i, pos_i = inv[:, 0:1], inv[:, 1:2]
            e_loads[s].wait()
            for k in range(count):
                other, piece = k // 4, k % 4
                source = own if piece % 2 == 0 else got
                at = (other * 2 + piece // 2) * rows
                inv_j = CONTRAST_WEIGHT / source[0:2, at : at + rows]
                same = own_lab == lab_ref[other, lax.bitwise_xor(jnp.int32(piece), t)]
                coef = (all_i + inv_j[0:1]) - jnp.where(same, pos_i + inv_j[1:2], 0.0)
                cols = slice(k * rows, (k + 1) * rows)
                grad[s % 2, :, cols] = (exps[s, :, cols].astype(F32) * coef).astype(BF16)

        weigh(0)
        for copy in loads:
            copy.wait()
        for s in range(4):
            seq, half = s // 2, s % 2
            if s + 1 < 4:
                weigh(s + 1)
            gn = dot(grad[s % 2], both[...]) * factor
            first = (seq * 4 + half * 2) * rows
            n = both[first : first + rows, :].astype(F32)
            inner = gn - n * jnp.mean(gn * n, axis=-1, keepdims=True)
            for copy in small[s]:
                copy.wait()
            pieces = scales[s, :, :rows].astype(F32)
            gy = cots[s].astype(F32) + column(pieces[0:1] + pieces[1:2]) * inner
            low_v[s] = gy.astype(BF16)
            pending.append(move(low_v.at[s], (low1 if seq else low0).at[half], o_sem.at[s]))
            if half == 0:
                full_v[seq] = gy
                pending.append(move(full_v.at[seq], full.at[seq], o_sem.at[4 + seq]))
        for copy in pending:
            copy.wait()

    return kernel_call(
        body,
        (
            struct((seqs, rows, feats), F32),
            struct((2, rows, feats), BF16),
            struct((2, rows, feats), BF16),
        ),
        (ANY,) * 3,
        [
            pl.BlockSpec(memory_space=pltpu.SMEM),
            whole(labels.shape),
            whole((4 * rows, 128)),
            whole((8, 4 * rows)),
            whole((8, 4 * rows)),
        ]
        + [ANY] * count
        + [HBM] * 2
        + [ANY] * 2,
        scratch=[
            VMEM((count * rows, feats), BF16),
            VMEM((4, rows, count * rows), BF16),
            VMEM((4, EXTRA, feats), BF16),
            VMEM((4, rows, feats), BF16),
            VMEM((2, rows, count * rows), BF16),
            VMEM((seqs, rows, feats), F32),
            VMEM((4, rows, feats), BF16),
            DMA((count,)),
            DMA((4,)),
            DMA((4,)),
            DMA((4,)),
            DMA((4 + seqs,)),
        ],
        flops=2 * 4 * rows * count * rows * feats,
        nbytes=count * rows * feats * 5,
        name="contrast_grads",
    )(place, labels, col_sums, row_own, row_got, *units, exps, cot, *cot_got)


def down_grad(act, own, got, flags, bit):
    seqs, length, units = act.shape
    rows, feats = own[0].shape[1:]
    tiles = units // TILE

    def body(flag, a_ref, *rest):
        own_refs, got_refs = rest[:seqs], rest[seqs : 2 * seqs]
        other_ref, kept_ref, a, b, out, a_sem, b_sem, o_sem = rest[2 * seqs :]
        b_loads = []
        for s in range(seqs):
            for r in range(4):
                src = (got_refs if r % 2 else own_refs)[s].at[r // 2]
                b_loads.append(move(src, b.at[s, pl.ds(r * rows, rows)], b_sem.at[4 * s + r]))
        columns = [pl.ds(i * TILE, TILE) for i in range(tiles)]
        a_loads = [move(a_ref.at[:, :, columns[i]], a.at[i], a_sem.at[i]) for i in range(tiles)]
        for copy in b_loads:
            copy.wait()
        stores = []
        for i in range(tiles):
            a_loads[i].wait()
            out[i] = functools.reduce(jnp.add, [dot(a[i, s], b[s], TN) for s in range(seqs)]).astype(BF16)
            stores.append(
                send_half(i, tiles, flag[bit], out.at[i], other_ref, kept_ref, pl.ds(0, feats), o_sem.at[i])
            )
        for copy in stores:
            copy.wait()

    return kernel_call(
        body,
        (struct((units // 2, feats), BF16),) * 2,
        (ANY,) * 2,
        [pl.BlockSpec(memory_space=pltpu.SMEM), HBM] + [ANY] * (2 * seqs),
        scratch=[
            VMEM((tiles, seqs, length, TILE), BF16),
            VMEM((seqs, length, feats), BF16),
            VMEM((tiles, TILE, feats), BF16),
            DMA((tiles,)),
            DMA((4 * seqs,)),
            DMA((tiles,)),
        ],
        flops=2 * seqs * length * units * feats,
        nbytes=4 * seqs * length * feats,
        name="down_grad",
    )(flags, act, *own, *got)


TILE = 256


def send_half(tile, tiles, high, src, to_other, kept, at, sem):
    upper = tile >= tiles // 2
    rows = pl.ds((tile % (tiles // 2)) * TILE, TILE)

    @pl.when(high == int(upper))
    def _():
        pltpu.make_async_copy(src, kept.at[rows, at], sem).start()

    @pl.when(high != int(upper))
    def _():
        pltpu.make_async_copy(src, to_other.at[rows, at], sem).start()

    return pltpu.make_async_copy(src, kept.at[rows, at], sem)


def weight_grad(lhs, rhs, flags, bit):
    seqs, length, out_rows = lhs.shape
    cols = rhs.shape[2]
    tiles = out_rows // TILE

    def body(flag, a_ref, b_ref, other_ref, kept_ref, a, b, out, a_sem, b_sem, o_sem):
        b_loads = [move(b_ref.at[s], b.at[s], b_sem.at[s]) for s in range(seqs)]
        columns = [pl.ds(i * TILE, TILE) for i in range(tiles)]
        a_loads = [move(a_ref.at[:, :, columns[i]], a.at[i], a_sem.at[i]) for i in range(tiles)]
        for copy in b_loads:
            copy.wait()
        stores = []
        for i in range(tiles):
            a_loads[i].wait()
            out[i] = functools.reduce(jnp.add, [dot(a[i, s], b[s], TN) for s in range(seqs)]).astype(BF16)
            stores.append(
                send_half(i, tiles, flag[bit], out.at[i], other_ref, kept_ref, pl.ds(0, cols), o_sem.at[i])
            )
        for copy in stores:
            copy.wait()

    return kernel_call(
        body,
        (struct((out_rows // 2, cols), BF16),) * 2,
        (ANY,) * 2,
        [pl.BlockSpec(memory_space=pltpu.SMEM)] + [HBM] * 2,
        scratch=[
            VMEM((tiles, seqs, length, TILE), BF16),
            VMEM((seqs, length, cols), BF16),
            VMEM((tiles, TILE, cols), BF16),
            DMA((tiles,)),
            DMA((seqs,)),
            DMA((tiles,)),
        ],
        flops=2 * seqs * length * out_rows * cols,
        nbytes=4 * seqs * length * cols,
        name="weight_grad",
    )(flags, lhs, rhs)


def head_grads(lhs, grads, att, rows_r, flags, bits):
    seqs, length, feats = lhs.shape
    width = att.shape[2]
    tiles = feats // width

    def body(*refs):
        flag, a_ref, *g_refs, r_ref = refs[:7]
        first_refs, second_refs = refs[7:9], refs[9:11]
        a, g, r, first, second, a_sem, g_sem, r_sem, o_sem = refs[11:]
        columns = [pl.ds(i * width, width) for i in range(tiles)]
        g_loads = [move(ref, g.at[n], g_sem.at[n]) for n, ref in enumerate(g_refs)]
        a_loads, r_loads = [], []
        for i in range(tiles):
            a_loads.append(move(a_ref.at[:, :, columns[i]], a.at[i], a_sem.at[i]))
            r_loads.append(move(r_ref.at[:, :, columns[i]], r.at[i], r_sem.at[i]))
        for copy in g_loads:
            copy.wait()

        def total(x, y):
            return functools.reduce(jnp.add, [dot(x[s], y[s], TN) for s in range(seqs)]).astype(BF16)

        stores = []
        for i in range(tiles):
            a_loads[i].wait()
            first[i, :, :width] = total(a[i], g[0])
            first[i, :, width:] = total(a[i], g[1])
            second[i, :, :width] = total(a[i], g[2])
            r_loads[i].wait()
            second[i, :, width:] = total(g[3], r[i])
            for n, (src, outs) in enumerate(((first, first_refs), (second, second_refs))):
                stores.append(
                    send_half(i, tiles, flag[bits[n]], src.at[i], *outs, pl.ds(0, 2 * width), o_sem.at[2 * i + n])
                )
        for copy in stores:
            copy.wait()

    return kernel_call(
        body,
        (struct((feats // 2, 2 * width), BF16),) * 4,
        (ANY,) * 4,
        [pl.BlockSpec(memory_space=pltpu.SMEM)] + [HBM] * 6,
        scratch=[
            VMEM((tiles, seqs, length, width), BF16),
            VMEM((4, seqs, length, width), BF16),
            VMEM((tiles, seqs, length, width), BF16),
            VMEM((tiles, width, 2 * width), BF16),
            VMEM((tiles, width, 2 * width), BF16),
            DMA((tiles,)),
            DMA((4,)),
            DMA((tiles,)),
            DMA((2 * tiles,)),
        ],
        flops=2 * seqs * length * feats * width * 4,
        nbytes=4 * seqs * length * feats,
        name="head_grads",
    )(flags, lhs, *grads, att, rows_r)


def halve_step(flags, bit, keep, got):
    rows, cols = keep.shape
    half = rows // 2

    def body(flag, k_ref, g_ref, *outs):
        if bit is None:
            outs[0][...] = (k_ref[...].astype(F32) + g_ref[...].astype(F32)).astype(BF16)
            return
        for high in (0, 1):

            @pl.when(flag[bit] == high)
            def _(high=high):
                for out, upper in ((outs[0], 1 - high), (outs[1], high)):
                    at = slice(upper * half, (upper + 1) * half)
                    out[...] = (k_ref[at, :].astype(F32) + g_ref[at, :].astype(F32)).astype(BF16)

    shape = (rows, cols) if bit is None else (half, cols)
    return kernel_call(
        body,
        (struct(shape, BF16),) * (1 if bit is None else 2),
        (whole(shape),) * (1 if bit is None else 2),
        [pl.BlockSpec(memory_space=pltpu.SMEM)] + [whole((rows, cols))] * 2,
        nbytes=rows * cols * 6,
        limit=SMALL,
        name="halve_step",
    )(flags, keep, got)


def join_step(flags, bit, own, got, dtype):
    rows, cols = own.shape
    steps = 2 if dtype == F32 else 1
    part = rows // steps

    def body(flag, own_ref, got_ref, out):
        for high in (0, 1):

            @pl.when(flag[bit] == high)
            def _(high=high):
                out[high] = own_ref[...].astype(dtype)
                out[1 - high] = got_ref[...].astype(dtype)

    block = pl.BlockSpec((part, cols), lambda i: (i, 0))
    return kernel_call(
        body,
        struct((2, rows, cols), dtype),
        pl.BlockSpec((2, part, cols), lambda i: (0, i, 0)),
        [pl.BlockSpec(memory_space=pltpu.SMEM), block, block],
        grid=(steps,),
        nbytes=rows * cols * 8,
        limit=SMALL,
        name="join_step",
    )(flags, own, got).reshape(2 * rows, cols)


def head_outputs(flags, bits, first, second):
    feats = 2 * first[0].shape[0]
    width = first[0].shape[1] // 2
    tile = width

    def body(h_ref, a_ref, b_ref, c_ref, d_ref, qkv, out):
        mine = (lax.div(pl.program_id(0) * tile, feats // 2) == h_ref[bits[0]])

        for case, x in ((True, a_ref), (False, b_ref)):
            @pl.when(mine == case)
            def _(x=x):
                qkv[0] = x[:, :width].astype(F32)
                qkv[1] = x[:, width:].astype(F32)

        mine_two = (lax.div(pl.program_id(0) * tile, feats // 2) == h_ref[bits[1]])
        for case, y in ((True, c_ref), (False, d_ref)):
            @pl.when(mine_two == case)
            def _(y=y):
                qkv[2] = y[:, :width].astype(F32)
                out[...] = y[:, width:].astype(F32)

    half = pl.BlockSpec((tile, 2 * width), lambda i, h: (lax.rem(i, feats // 2 // tile), 0))
    return kernel_call(
        body,
        (struct((3, feats, width), F32), struct((width, feats), F32)),
        (pl.BlockSpec((3, tile, width), lambda i, h: (0, i, 0)), pl.BlockSpec((width, tile), lambda i, h: (0, i))),
        [half] * 4,
        grid=(feats // tile,),
        nbytes=10 * feats * width * 4,
        prefetch=1,
        limit=SMALL,
        name="head_outputs",
    )(flags, *first, *second)


def swap(value, axis, size, bit):
    return lax.ppermute(value, axis, [(i, i ^ bit) for i in range(size)])


CORE, CROSS = 1, 2


def tensor_swap(value, bit):
    return swap(value, "tensor", 4, bit)


def tie(value, *earlier):
    return lax.optimization_barrier((value, *earlier))[0] if earlier else value


class Gather:
    def __init__(self, value):
        self.value = value
        self.cross = tensor_swap(value, CROSS)
        self.core = tensor_swap(value, CORE)

    def blocks(self, *earlier):
        return [self.value, self.core, self.cross, tensor_swap(tie(self.cross, *earlier), CORE)]


class Scatter:
    def __init__(self, blocks):
        self.own, self.other = blocks[0], blocks[2]
        self.core_other = tensor_swap(blocks[3], CORE)
        self.core_own = tensor_swap(blocks[1], CORE)
        self.mark = blocks[3]

    def cross(self, *earlier):
        block = (tie(self.other, *earlier).astype(F32) + self.core_other.astype(F32)).astype(BF16)
        self.parts = (self.own, self.core_own, tensor_swap(block, CROSS))
        return block


class DpSum:
    def __init__(self, send, keep, flags, size, order):
        self.send, self.value, self.flags, self.size = send, keep, flags, size
        self.left = [(bit, True) for bit in order] + [(bit, False) for bit in reversed(order)]
        self.got, self.now = None, None

    def advance(self, *earlier):
        if self.now is not None and self.now[1]:
            more = self.left and self.left[0][1]
            parts = halve_step(self.flags, self.left[0][0] if more else None, tie(self.value, *earlier), self.got)
            self.send, self.value = parts if more else (parts[0], parts[0])
        elif self.now is not None:
            self.send = self.value = join_step(self.flags, self.now[0], tie(self.value, *earlier), self.got, BF16)
        self.now = self.left.pop(0)
        self.got = swap(self.send, "dp", self.size, 1 << self.now[0])
        return self.send

    def halves(self):
        return self.value, self.got


def shards(
    dp_size,
    tokens,
    doc_ids,
    targets,
    cotangent,
    ln1_gain,
    ln1_bias,
    qkv_weight,
    query_bias,
    value_bias,
    output_weight,
    out_bias,
    ln2_gain,
    ln2_bias,
    up_weight,
    up_bias,
    down_weight,
    down_bias,
):
    seqs, rows, feats = tokens.shape
    length = doc_ids.shape[1]
    parts = length // rows
    me = lax.axis_index("tensor")
    place = me.reshape(1).astype(jnp.int32)
    vec = lambda v: v.astype(F32).reshape(1, -1)
    gain_one, shift_one, gain_two, shift_two = vec(ln1_gain), vec(ln1_bias), vec(ln2_gain), vec(ln2_bias)
    out_offset, down_offset, up_shift = vec(out_bias), vec(down_bias), vec(up_bias)
    q_shift, v_shift = vec(query_bias), vec(value_bias)

    fine = 16
    paired = (jnp.arange(feats, dtype=jnp.int32) // 2).astype(F32)
    freq = jnp.exp(paired * (-2.0 * math.log(10000.0) / feats))[None, :]
    odd = (jnp.arange(feats, dtype=jnp.int32) % 2 == 1)[None, :]
    coarse_at = (me * rows + fine * jnp.arange(rows // fine, dtype=jnp.int32)).astype(F32)[:, None] * freq
    fine_at = jnp.arange(fine, dtype=jnp.int32).astype(F32)[:, None] * freq
    sin_a, cos_a = jnp.sin(coarse_at), jnp.cos(coarse_at)
    tables = (jnp.where(odd, cos_a, sin_a), jnp.where(odd, -sin_a, cos_a), jnp.cos(fine_at), jnp.sin(fine_at))

    docs_f, labels_f = doc_ids.astype(F32), targets.astype(F32)
    docs4 = docs_f.reshape(seqs, parts, 1, rows)
    labels4 = labels_f.reshape(seqs, parts, 1, rows)
    docs_row = [docs_f[s : s + 1] for s in range(seqs)]

    hidden, stream, grad_r = [None] * 2, [None] * 2, [None] * 2
    kept, up_sums, head_sums, sums_one, sums_two = [None] * 2, [None] * 2, [None] * 2, [None] * 2, [None] * 2
    shared = {"attend": None, "feed": None, "act": None, "up": None, "heads": None, "input": None}

    def attend(s, gathered, *earlier):
        *blocks, cat, qkv, att, logs = attend_forward(
            s, seqs, tie(place, *earlier), docs_row[s], gathered, qkv_weight, q_shift, v_shift, output_weight,
            shared["attend"],
        )
        shared["attend"], kept[s] = (cat, att), (qkv, logs)
        return Scatter(blocks)

    def middle_rows(s, scatter, *earlier):
        stream[s], normed = second_norm(hidden[s], scatter.parts, tie(out_offset, *earlier), gain_two, shift_two)
        return normed, Gather(normed)

    def feed(s, gathered, *earlier):
        *blocks, cat, act, slope = feed_forward(
            s, seqs, gathered, up_weight, tie(up_shift, *earlier), down_weight, shared["feed"]
        )
        shared["feed"] = (cat, act, slope)
        return Scatter(blocks)

    def last_rows(s, scatter, *earlier):
        shared["act"], unit = output_rows(
            s, seqs, stream[s], scatter.parts, tie(down_offset, *earlier), shared["act"]
        )
        return unit, Gather(unit)

    hidden[0], normed_a = first_norm(0, tokens, tables, gain_one, shift_one)
    rows_a = Gather(normed_a)
    hidden[1], normed_b = first_norm(1, tie(tokens, normed_a), tables, gain_one, shift_one)
    rows_b = Gather(normed_b)
    at_a = attend(0, rows_a.blocks(normed_b))
    block = at_a.cross(rows_b.cross)
    at_b = attend(1, rows_b.blocks(), block)
    normed, rows_a = middle_rows(0, at_a, at_b.mark)
    block = at_b.cross(normed)
    ff_a = feed(0, rows_a.blocks(), block)
    normed, rows_b = middle_rows(1, at_b, ff_a.mark)
    block = ff_a.cross(normed)
    ff_b = feed(1, rows_b.blocks(), block)
    unit, units_a = last_rows(0, ff_a, ff_b.mark)
    block = ff_b.cross(unit)
    unit, units_b = last_rows(1, ff_b, block)
    cots = [tensor_swap(tie(cotangent[s], unit), CROSS) for s in range(2)]
    cat_one, att = shared["attend"]
    cat_two, hidden_act, slope = shared["feed"]

    units = units_a.blocks() + units_b.blocks()
    exps, col_sums, row_sums, loss = contrast_scores(place, docs4, labels4, units)
    row_got = tensor_swap(row_sums, CORE)
    grad_y, *low_y = contrast_grads(
        place, labels4, units, exps, col_sums, row_sums, row_got, cotangent, cots
    )
    got_y = [tensor_swap(v, CORE) for v in low_y]

    def feed_back(s, *earlier):
        *blocks, shared["up"], up_sums[s] = feed_backward(
            s, seqs, low_y[s], got_y[s], slope, tie(up_weight, *earlier), down_weight, shared["up"]
        )
        return Scatter(blocks)

    def middle_back(s, scatter, *earlier):
        grad_r[s], low, sums_two[s] = norm_backward(
            s, seqs, stream[s], scatter.parts, tie(gain_two, *earlier), grad_y, False, None
        )
        return low, Gather(low)

    def attend_back(s, gathered, *earlier):
        *blocks, cat, gq, gk, gv, head_sums[s] = attend_backward(
            s, seqs, tie(place, *earlier), docs_row[s], gathered, kept[s][0], att, kept[s][1], qkv_weight,
            output_weight, shared["heads"],
        )
        shared["heads"] = (cat, gq, gk, gv)
        return Scatter(blocks)

    def first_back(s, scatter, *earlier):
        shared["input"], sums_one[s] = norm_backward(
            s, seqs, hidden[s], scatter.parts, tie(gain_one, *earlier), grad_r[s], True, shared["input"]
        )
        return sums_one[s]

    bits = list(range(dp_size.bit_length() - 1))
    other_bits = bits[1::-1] + bits[2:]
    flags = (lax.axis_index("dp") >> jnp.arange(len(bits), dtype=jnp.int32)) & 1
    fb_a = feed_back(0)
    block = fb_a.cross()
    fb_b = feed_back(1, block)
    block = fb_b.cross()
    low, rows_a = middle_back(0, fb_a, block)
    down_sum = DpSum(*down_grad(tie(hidden_act, low), low_y, got_y, flags, bits[0]), flags, dp_size, bits)
    sent = down_sum.advance()
    low, rows_b = middle_back(1, fb_b, sent)
    up_sum = DpSum(*weight_grad(tie(cat_two, low), shared["up"], flags, bits[0]), flags, dp_size, bits)
    sent = up_sum.advance()
    ab_a = attend_back(0, rows_a.blocks(sent), sent)
    sent = down_sum.advance(ab_a.mark)
    block = ab_a.cross(sent)
    ab_b = attend_back(1, rows_b.blocks(block), block)
    sent = up_sum.advance(down_sum.advance(ab_b.mark))
    sums = first_back(0, ab_a, sent)
    block = ab_b.cross(sums)
    cat_r, *grad_qkv = shared["heads"]
    first_send, first_keep, second_send, second_keep = head_grads(
        tie(cat_one, block), grad_qkv, att, cat_r, flags, (bits[0], other_bits[0])
    )
    first = DpSum(first_send, first_keep, flags, dp_size, bits)
    second = DpSum(second_send, second_keep, flags, dp_size, other_bits)
    sent = (first.advance(), second.advance())
    sent = up_sum.advance(down_sum.advance(*sent))
    sums = first_back(1, ab_b, sent)
    sent = (sums,)

    total = lambda items: functools.reduce(jnp.add, items)
    heads_sum = total(head_sums)
    heads_row = jnp.pad(heads_sum.reshape(1, -1), ((0, 0), (0, feats - heads_sum.size)))
    small = jnp.concatenate([total(sums_one)[:2], total(sums_two), total(up_sums), heads_row])
    swaps = [("dp", dp_size, 1 << bit) for bit in bits] + [("tensor", 4, CORE), ("tensor", 4, CROSS)]
    local = None
    while swaps or first.left or up_sum.left or down_sum.left:
        if swaps:
            axis, size, bit = swaps.pop(0)
            if axis == "tensor" and local is None:
                local, small = small[6:], small[:6]
            small = small + swap(tie(small, *sent), axis, size, bit)
        sent = ()
        if first.left:
            sent += (first.advance(small), second.advance(small))
        for other in (down_sum, up_sum):
            if other.left:
                sent += (other.advance(small, *sent),)
    grad_qkv_w, grad_out_w = head_outputs(flags, (bits[0], other_bits[0]), first.halves(), second.halves())
    grad_down_w = join_step(flags, bits[0], *down_sum.halves(), F32)
    grad_up_w = join_step(flags, bits[0], *up_sum.halves(), F32)
    return (
        shared["act"],
        loss,
        shared["input"],
        small[0],
        small[1],
        grad_qkv_w,
        local[1, : heads_sum.shape[1]],
        local[1, heads_sum.shape[1] : 2 * heads_sum.shape[1]],
        grad_out_w,
        small[4],
        small[2],
        small[3],
        grad_up_w,
        local[0],
        grad_down_w,
        small[5],
    )


def solution(mesh):
    in_specs = (
        P("dp", "tensor", None),
        P("dp", None),
        P("dp", None),
        P("dp", "tensor", None),
        P(),
        P(),
        P(None, None, "tensor"),
        P("tensor"),
        P("tensor"),
        P("tensor", None),
        P(),
        P(),
        P(),
        P(None, "tensor"),
        P("tensor"),
        P("tensor", None),
        P(),
    )
    out_specs = (
        P("dp", "tensor", None),
        P("dp", "tensor"),
        P("dp", "tensor", None),
        P(),
        P(),
        P(None, None, "tensor"),
        P("tensor"),
        P("tensor"),
        P("tensor", None),
        P(),
        P(),
        P(),
        P(None, "tensor"),
        P("tensor"),
        P("tensor", None),
        P(),
    )
    return jax.shard_map(
        functools.partial(shards, mesh.shape["dp"]),
        mesh=mesh,
        in_specs=in_specs,
        out_specs=out_specs,
        check_vma=False,
    )
```

```python
import functools
import math

import jax
import jax.numpy as jnp
from jax import lax
from jax.experimental import pallas as pl
from jax.experimental.pallas import tpu as pltpu
from jax.sharding import PartitionSpec as P

HEADS = 8
NORM_EPS = 1e-05
CONTRAST_SCALE = 32.0
CONTRAST_WEIGHT = 64.0
NEGATIVE = -1e30
LOG2E = math.log2(math.e)
F32 = jnp.float32
BF16 = jnp.bfloat16
MIB = 1 << 20
LIMIT, SMALL = 52, 14
COST = 0.02
NN = (((1,), (0,)), ((), ()))
NT = (((1,), (1,)), ((), ()))
TN = (((0,), (0,)), ((), ()))
VMEM = pltpu.VMEM


def dot(a, b, dims=NN):
    return lax.dot_general(a, b, dims, preferred_element_type=F32)


def whole(shape):
    return pl.BlockSpec(shape, lambda *_: (0,) * len(shape))


def kernel_call(body, outs, out_specs, in_specs, grid=(1,), scratch=(), flops=0, nbytes=0, trans=0,
                limit=LIMIT, aliases=None, prefetch=0, name=None):
    return pl.pallas_call(
        body,
        out_shape=outs,
        grid_spec=pltpu.PrefetchScalarGridSpec(
            num_scalar_prefetch=prefetch,
            grid=grid,
            in_specs=in_specs,
            out_specs=out_specs,
            scratch_shapes=scratch,
        ),
        name=name,
        input_output_aliases=aliases or {},
        cost_estimate=pl.CostEstimate(
            flops=int(flops * COST), bytes_accessed=int(nbytes * COST), transcendentals=int(trans * COST)
        ),
        compiler_params=pltpu.CompilerParams(vmem_limit_bytes=limit * MIB),
    )


def struct(shape, dtype):
    return jax.ShapeDtypeStruct(shape, dtype)


ANY = pl.BlockSpec(memory_space=pl.ANY)
HBM = pl.BlockSpec(memory_space=pltpu.HBM)
SMEM = pl.BlockSpec(memory_space=pltpu.SMEM)
DMA = pltpu.SemaphoreType.DMA


def move(src, dst, sem):
    copy = pltpu.make_async_copy(src, dst, sem)
    copy.start()
    return copy


def column(row):
    return jnp.transpose(jnp.broadcast_to(row, (8, row.shape[1])))[:, :1]


def norm_stats(v):
    centered = v - jnp.mean(v, axis=-1, keepdims=True)
    rstd = lax.rsqrt(jnp.mean(centered * centered, axis=-1, keepdims=True) + NORM_EPS)
    return centered * rstd, rstd


ROW_STEPS = 4


def row_blocks(rows, cols):
    return pl.BlockSpec((rows // ROW_STEPS, cols), lambda i: (i, 0))


def first_norm(seq, tokens, tables, gain, shift):
    rows, feats = tokens.shape[1:]
    fine = tables[2].shape[0]
    step = rows // ROW_STEPS

    def body(tok, pa, qa, cb, sb, g, b, h_out, a_out):
        i = pl.program_id(0)
        for c in range(step // fine):
            at = pl.ds(c * fine, fine)
            row = pl.ds(i * (step // fine) + c, 1)
            pos = pa[row, :] * cb[...] + qa[row, :] * sb[...]
            h = tok[0, at, :].astype(F32) + pos
            h_out[at, :] = h
            z, _ = norm_stats(h)
            a_out[at, :] = (z * g[...] + b[...]).astype(BF16)

    return kernel_call(
        body,
        (struct((rows, feats), F32), struct((rows, feats), BF16)),
        (row_blocks(rows, feats), row_blocks(rows, feats)),
        [pl.BlockSpec((1, step, feats), lambda i: (seq, i, 0))]
        + [whole(t.shape) for t in tables]
        + [whole((1, feats))] * 2,
        grid=(ROW_STEPS,),
        nbytes=rows * feats * 8,
        limit=SMALL,
        name="first_norm",
    )(tokens, *tables, gain, shift)


def joined(parts, at):
    return functools.reduce(jnp.add, [p[at, :].astype(F32) for p in parts])


def second_norm(h, parts, offset, gain, shift):
    rows, feats = h.shape
    chunk = 32
    step = rows // ROW_STEPS

    def body(h_ref, k_ref, c_ref, x_ref, o_ref, g, b, r_out, n_out):
        for c in range(step // chunk):
            at = pl.ds(c * chunk, chunk)
            r = h_ref[at, :] + joined((k_ref, c_ref, x_ref), at) + o_ref[...]
            r_out[at, :] = r
            z, _ = norm_stats(r)
            n_out[at, :] = (z * g[...] + b[...]).astype(BF16)

    block = row_blocks(rows, feats)
    return kernel_call(
        body,
        (struct((rows, feats), F32), struct((rows, feats), BF16)),
        (block, block),
        [block] * 4 + [whole((1, feats))] * 3,
        grid=(ROW_STEPS,),
        nbytes=rows * feats * 16,
        limit=SMALL,
        name="second_norm",
    )(h, *parts, offset, gain, shift)


EXTRA = 16


def output_rows(seq, seqs, r1, parts, offset, previous):
    rows, feats = r1.shape
    step, chunk = 128, 32

    def body(r_ref, k_ref, c_ref, x_ref, o_ref, *rest):
        act_out, n_out, q_all = rest[-3:]
        i = pl.program_id(0)
        for c in range(step // chunk):
            at = pl.ds(c * chunk, chunk)
            y = r_ref[at, :] + joined((k_ref, c_ref, x_ref), at) + o_ref[...]
            act_out[0, at, :] = y.astype(BF16)
            q = lax.rsqrt(jnp.mean(y * y, axis=-1, keepdims=True) + NORM_EPS)
            n_out[pl.ds(pl.multiple_of(i * step + c * chunk, chunk), chunk), :] = (y * q).astype(BF16)
            q_all[at, :] = jnp.broadcast_to(q, (chunk, step))

        @pl.when(i == 0)
        def _():
            n_out[rows:, :] = jnp.zeros((EXTRA, feats), BF16)

        row = jnp.transpose(q_all[...])[:EXTRA, :]
        high = row.astype(BF16).astype(F32)
        which = lax.broadcasted_iota(jnp.int32, (EXTRA, step), 0)
        lanes = pl.ds(pl.multiple_of(i * step, step), step)
        n_out[rows:, lanes] = jnp.where(which == 0, high, jnp.where(which == 1, row - high, 0.0)).astype(BF16)

    block = pl.BlockSpec((step, feats), lambda i: (i, 0))
    extra = [] if previous is None else [previous]
    return kernel_call(
        body,
        (struct((seqs, rows, feats), BF16), struct((rows + EXTRA, feats), BF16)),
        (pl.BlockSpec((1, step, feats), lambda i: (seq, i, 0)), whole((rows + EXTRA, feats))),
        [block] * 4 + [whole((1, feats))] + [ANY] * len(extra),
        grid=(rows // step,),
        scratch=[VMEM((step, step), F32)],
        nbytes=rows * feats * 14,
        aliases={5: 0} if extra else None,
        limit=SMALL,
        name="output_rows",
    )(r1, *parts, offset, *extra)


def norm_backward(seq, seqs, v, parts, gain, base, final, previous):
    rows, feats = v.shape
    chunk = 16
    step = rows // ROW_STEPS

    def body(v_ref, k_ref, c_ref, x_ref, g, base_ref, *rest):
        if final:
            out, sums = rest[-2:]
        else:
            out, low, sums = rest[-3:]
        acc = [jnp.zeros((8, feats), F32) for _ in range(2 if final else 4)]
        for c in range(step // chunk):
            at = pl.ds(c * chunk, chunk)
            got = joined((k_ref, c_ref, x_ref), at)
            z, rstd = norm_stats(v_ref[at, :])
            w = got * g[...]
            inner = rstd * (w - jnp.mean(w, axis=-1, keepdims=True) - z * jnp.mean(w * z, axis=-1, keepdims=True))
            old = base_ref[at, :]
            new = old + inner
            if final:
                out[0, at, :] = new
            else:
                out[at, :] = new
                low[at, :] = new.astype(BF16)
            terms = [got * z, got] + ([] if final else [new, old])
            for k, term in enumerate(terms):
                acc[k] = acc[k] + jnp.sum(term.reshape(chunk // 8, 8, feats), axis=0)

        @pl.when(pl.program_id(0) == 0)
        def _():
            sums[...] = jnp.zeros_like(sums)

        for k, term in enumerate(acc):
            sums[k : k + 1, :] += jnp.sum(term, axis=0, keepdims=True)

    block = row_blocks(rows, feats)
    extra = [] if previous is None else [previous]
    seq_block = pl.BlockSpec((1, step, feats), lambda i: (seq, i, 0))
    if final:
        outs, specs = (struct((seqs, rows, feats), F32), struct((4, feats), F32)), (seq_block, whole((4, feats)))
    else:
        outs = (struct((rows, feats), F32), struct((rows, feats), BF16), struct((4, feats), F32))
        specs = (block, block, whole((4, feats)))
    return kernel_call(
        body,
        outs,
        specs,
        [block] * 4 + [whole((1, feats)), block] + [ANY] * len(extra),
        grid=(ROW_STEPS,),
        nbytes=rows * feats * 20,
        aliases={6: 0} if extra else None,
        limit=SMALL,
        name="norm_backward",
    )(v, *parts, gain, base, *extra)


def send_block(refs, rel, src, sems):
    for r, ref in enumerate(refs):

        @pl.when(rel == r)
        def _(r=r, ref=ref):
            pltpu.make_async_copy(src, ref, sems.at[r]).start()


def wait_blocks(refs, src, sems):
    for r, ref in enumerate(refs):
        pltpu.make_async_copy(src, ref, sems.at[r]).wait()


def block_at(rel, rows):
    return pl.ds(pl.multiple_of(rel * rows, rows), rows)


def lane_pair(first, second, rows):
    lanes = lax.broadcasted_iota(jnp.int32, (rows, 128), 1)
    return jnp.where(lanes == 0, first, second)


def attend_forward(seq, place, docs, vecs, blocks, wqkv, wo, previous):
    rows, feats = blocks[0].shape
    parts = len(blocks)
    length = rows * parts
    width = wqkv.shape[2]
    size = feats // HEADS
    heads = width // size
    scale = LOG2E * size ** (-0.5)

    seqs = docs.shape[0]

    def body(t_ref, doc_ref, vec, *rest):
        dr = doc_ref[seq : seq + 1, :].astype(F32)
        x_refs, (w_ref, wo_ref), rest = rest[:4], rest[4:6], rest[6:]
        p_refs, (saved, lse_out), rest = rest[-17:-13], rest[-13:-11], rest[-11:]
        xs, w, wov, qkv, att, lse, ps, in_sem, p_sem, c_sem, o_sem = rest
        t = t_ref[0]
        load_w = move(w_ref, w, in_sem.at[4])
        for r in range(parts):
            at = lax.bitwise_xor(jnp.int32(r), t)
            move(x_refs[r], xs.at[at], in_sem.at[at])
        load_wo = move(wo_ref, wov, in_sem.at[5])
        pending = []

        def project(i):
            pltpu.make_async_copy(x_refs[0], xs.at[i], in_sem.at[i]).wait()
            rel = lax.bitwise_xor(jnp.int32(i), t)
            pending.append(move(xs.at[i], saved.at[seq, block_at(rel, rows), pl.ds(0, feats)], c_sem.at[i]))
            x = xs[i]
            at = slice(i * rows, (i + 1) * rows)
            qkv[0, at, :] = (dot(x, w[0]) + vec[:, :width]).astype(BF16)
            qkv[1, at, :] = dot(x, w[1]).astype(BF16)
            qkv[2, at, :] = (dot(x, w[2]) + vec[:, width:]).astype(BF16)

        load_w.wait()
        project(0)
        load_wo.wait()
        for i in range(parts):
            if i + 1 < parts:
                project(i + 1)
            span = (i + 1) * rows
            own = slice(i * rows, span)
            same = column(dr[:, own]) == dr[:, :span]
            before = lax.broadcasted_iota(jnp.int32, (rows, span), 0) + i * rows >= lax.broadcasted_iota(
                jnp.int32, (rows, span), 1
            )
            allowed = same & before
            logs = []
            for hd in range(heads):
                cols = slice(hd * size, (hd + 1) * size)
                s = jnp.where(allowed, dot(qkv[0, own, cols], qkv[1, :span, cols], NT) * scale, NEGATIVE)
                top = jnp.max(s, axis=-1, keepdims=True)
                e = jnp.exp2(s - top)
                total = jnp.sum(e, axis=-1, keepdims=True)
                att[i, :, cols] = (dot(e.astype(BF16), qkv[2, :span, cols]) / total).astype(BF16)
                logs.append(top + jnp.log2(total))
            lse[own, :] = lane_pair(logs[0], logs[-1], rows)
            ps[i] = dot(att[i], wov[...]).astype(BF16)
            rel = lax.bitwise_xor(jnp.int32(i), t)
            send_block(p_refs, rel, ps.at[i], p_sem)
            pending.append(
                move(att.at[i], saved.at[seq, block_at(rel, rows), pl.ds(feats + 3 * width, width)], o_sem.at[i])
            )
        for c in range(3):
            pending.append(move(qkv.at[c], saved.at[seq, :, pl.ds(feats + c * width, width)], o_sem.at[parts + c]))
        pending.append(move(lse, lse_out, in_sem.at[5]))
        for copy in pending:
            copy.wait()
        wait_blocks(p_refs, ps.at[0], p_sem)

    extra = [] if previous is None else [previous]
    return kernel_call(
        body,
        (
            *[struct((rows, feats), BF16)] * 4,
            struct((2 * seqs, length, feats + 4 * width), BF16),
            struct((length, 128), F32),
        ),
        (ANY,) * 4 + (HBM,) * 2,
        [SMEM, whole(docs.shape), whole(vecs.shape)]
        + [ANY] * 4
        + [HBM] * (2 + len(extra)),
        scratch=[
            VMEM((parts, rows, feats), BF16),
            VMEM(wqkv.shape, BF16),
            VMEM(wo.shape, BF16),
            VMEM((3, length, width), BF16),
            VMEM((parts, rows, width), BF16),
            VMEM((length, 128), F32),
            VMEM((parts, rows, feats), BF16),
            DMA((6,)),
            DMA((4,)),
            DMA((4,)),
            DMA((7,)),
        ],
        flops=2 * length * feats * width * 4 + 5 * length * length * width,
        nbytes=length * feats * 8,
        trans=length * length * heads // 2,
        aliases={9: 4} if extra else None,
        name="attend_forward",
    )(place, docs, vecs, *blocks, wqkv, wo, *extra)


def attend_backward(seq, place, docs, blocks, saved, lse, wqkv, wo, previous):
    rows, feats = blocks[0].shape
    parts = len(blocks)
    length = rows * parts
    width = wqkv.shape[2]
    size = feats // HEADS
    heads = width // size
    root = size ** (-0.5)
    scale = LOG2E * root

    seqs = docs.shape[0]

    def body(t_ref, doc_ref, *rest):
        dr = doc_ref[seq : seq + 1, :].astype(F32)
        x_refs, (saved_ref, lse_ref, w_ref, wo_ref), rest = rest[:4], rest[4:8], rest[8:]
        p_refs, (out, sums), rest = rest[-20:-16], rest[-16:-14], rest[-14:]
        xs, w, wov, qkvv, attv, lsev, gk, gv, ga, low, ps, in_sem, p_sem, o_sem = rest
        t = t_ref[0]
        load_wo = move(wo_ref, wov, in_sem.at[4])
        for r in (3, 2, 1, 0):
            at = lax.bitwise_xor(jnp.int32(r), t)
            move(x_refs[r], xs.at[at], in_sem.at[at])
        loads = [move(lse_ref, lsev, in_sem.at[6])]
        for c in range(3):
            loads.append(move(saved_ref.at[seq, :, pl.ds(feats + c * width, width)], qkvv.at[c], in_sem.at[12 + c]))
        for i in range(parts):
            rel = lax.bitwise_xor(jnp.int32(i), t)
            att_ref = saved_ref.at[seq, block_at(rel, rows), pl.ds(feats + 3 * width, width)]
            loads.append(move(att_ref, attv.at[i], in_sem.at[8 + i]))
        load_w = move(w_ref, w, in_sem.at[7])
        pending = []

        def project(i):
            pltpu.make_async_copy(x_refs[0], xs.at[i], in_sem.at[i]).wait()
            rel = lax.bitwise_xor(jnp.int32(i), t)
            pending.append(move(xs.at[i], out.at[seq, block_at(rel, rows), pl.ds(0, feats)], o_sem.at[i]))
            ga[i] = dot(xs[i], wov[...], NT).astype(BF16)

        load_wo.wait()
        project(parts - 1)
        for copy in loads:
            copy.wait()
        load_w.wait()
        q_sum = jnp.zeros((1, width), F32)
        v_sum = jnp.zeros((1, width), F32)
        for i in reversed(range(parts)):
            if i:
                project(i - 1)
            span = (i + 1) * rows
            own = slice(i * rows, span)
            same = column(dr[:, own]) == dr[:, :span]
            before = lax.broadcasted_iota(jnp.int32, (rows, span), 0) + i * rows >= lax.broadcasted_iota(
                jnp.int32, (rows, span), 1
            )
            allowed = same & before
            for hd in range(heads):
                cols = slice(hd * size, (hd + 1) * size)
                q = qkvv[0, own, cols]
                k = qkvv[1, :span, cols]
                g = ga[i, :, cols]
                s = dot(q, k, NT) * scale - lsev[own, hd : hd + 1]
                p = jnp.exp2(jnp.where(allowed, s, NEGATIVE))
                gp = dot(g, qkvv[2, :span, cols], NT)
                row = jnp.sum(g.astype(F32) * attv[i, :, cols].astype(F32), axis=-1, keepdims=True)
                gs = (p * (gp - row)).astype(BF16)
                low[0, own, cols] = (dot(gs, k) * root).astype(BF16)
                new_k = dot(gs, q, TN)
                new_v = dot(p.astype(BF16), g, TN)
                if i == parts - 1:
                    gk[:span, cols] = new_k
                    gv[:span, cols] = new_v
                else:
                    gk[:span, cols] += new_k
                    gv[:span, cols] += new_v
            low[1, own, :] = (gk[own, :] * root).astype(BF16)
            low[2, own, :] = gv[own, :].astype(BF16)
            q_sum += jnp.sum(low[0, own, :].astype(F32), axis=0, keepdims=True)
            v_sum += jnp.sum(low[2, own, :].astype(F32), axis=0, keepdims=True)
            ps[i] = (
                dot(low[0, own, :], w[0], NT) + dot(low[1, own, :], w[1], NT) + dot(low[2, own, :], w[2], NT)
            ).astype(BF16)
            rel = lax.bitwise_xor(jnp.int32(i), t)
            send_block(p_refs, rel, ps.at[i], p_sem)
            for c in range(3):
                dst = out.at[seq, block_at(rel, rows), pl.ds(feats + c * width, width)]
                pending.append(move(low.at[c, own], dst, o_sem.at[4 + 3 * i + c]))
        sums[0:1, :] = q_sum
        sums[1:2, :] = v_sum
        for copy in pending:
            copy.wait()
        wait_blocks(p_refs, ps.at[0], p_sem)

    extra = [] if previous is None else [previous]
    return kernel_call(
        body,
        (
            *[struct((rows, feats), BF16)] * 4,
            struct((2 * seqs, length, feats + 4 * width), BF16),
            struct((2, width), F32),
        ),
        (ANY,) * 4 + (HBM, whole((2, width))),
        [SMEM, whole(docs.shape)] + [ANY] * 4 + [HBM] * (4 + len(extra)),
        scratch=[
            VMEM((parts, rows, feats), BF16),
            VMEM(wqkv.shape, BF16),
            VMEM(wo.shape, BF16),
            VMEM((3, length, width), BF16),
            VMEM((parts, rows, width), BF16),
            VMEM((length, 128), F32),
            VMEM((length, width), F32),
            VMEM((length, width), F32),
            VMEM((parts, rows, width), BF16),
            VMEM((3, length, width), BF16),
            VMEM((parts, rows, feats), BF16),
            DMA((15,)),
            DMA((4,)),
            DMA((16,)),
        ],
        flops=2 * length * feats * width * 4 + 10 * length * length * width,
        nbytes=length * feats * 8,
        trans=length * length * heads // 2,
        aliases={10: 4} if extra else None,
        name="attend_backward",
    )(place, docs, *blocks, saved, lse, wqkv, wo, *extra)


ORDER = (3, 1, 2, 0)


ROWS, ACT, SLOPE, GRAD = range(4)


def feed_forward(seq, seqs, blocks, vecs, w_up, w_down, previous):
    rows, feats = blocks[0].shape
    parts = len(blocks)
    length = rows * parts
    units = w_up.shape[1]
    root = math.sqrt(2.0 / math.pi)

    def body(vec, *rest):
        x_refs, (up_ref, down_ref), rest = rest[:4], rest[4:6], rest[6:]
        p_refs, saved, rest = rest[-15:-11], rest[-11], rest[-10:]
        xs, up, down, u, act, slope, ps, in_sem, p_sem, o_sem = rest
        load_up = move(up_ref, up, in_sem.at[4])
        loads = {r: move(x_refs[r], xs.at[r], in_sem.at[r]) for r in ORDER}
        load_down = move(down_ref, down, in_sem.at[5])
        pending = []

        def project(k):
            r = ORDER[k]
            loads[r].wait()
            pending.append(move(xs.at[r], saved.at[ROWS, seq, pl.ds(r * rows, rows)], o_sem.at[r]))
            u[k % 2] = dot(xs[r], up[...]) + vec[...]

        load_up.wait()
        project(0)
        load_down.wait()
        for k, r in enumerate(ORDER):
            if k + 1 < parts:
                project(k + 1)
            v = u[k % 2]
            sq = v * v
            th = jnp.tanh(v * (root + (root * 0.044715) * sq))
            half = 0.5 + 0.5 * th
            g = (v * half).astype(BF16)
            act[r] = g
            slope[r] = (half + v * (1.0 - th * th) * (0.5 * root + (1.5 * 0.044715 * root) * sq)).astype(BF16)
            ps[r] = dot(g, down[...]).astype(BF16)
            at = pl.ds(r * rows, rows)
            pending.append(move(ps.at[r], p_refs[r], p_sem.at[r]))
            pending.append(move(act.at[r], saved.at[ACT, seq, at], o_sem.at[4 + r]))
            pending.append(move(slope.at[r], saved.at[SLOPE, seq, at], o_sem.at[8 + r]))
        for copy in pending:
            copy.wait()

    extra = [] if previous is None else [previous]
    return kernel_call(
        body,
        (
            *[struct((rows, feats), BF16)] * 4,
            struct((4, seqs, length, units), BF16),
        ),
        (ANY,) * 4 + (HBM,),
        [whole(vecs.shape)] + [ANY] * 4 + [HBM] * (2 + len(extra)),
        scratch=[
            VMEM((parts, rows, feats), BF16),
            VMEM(w_up.shape, BF16),
            VMEM(w_down.shape, BF16),
            VMEM((2, rows, units), F32),
            VMEM((parts, rows, units), BF16),
            VMEM((parts, rows, units), BF16),
            VMEM((parts, rows, feats), BF16),
            DMA((6,)),
            DMA((4,)),
            DMA((12,)),
        ],
        flops=4 * length * feats * units,
        nbytes=length * feats * 14,
        trans=length * units,
        aliases={7: 4} if extra else None,
        name="feed_forward",
    )(vecs, *blocks, w_up, w_down, *extra)


def feed_backward(seq, own, got, saved, w_up, w_down, earlier):
    rows, feats = own.shape[1:]
    parts = 4
    length = rows * parts
    units = w_up.shape[1]
    seqs = saved.shape[1]

    def body(own_ref, got_ref, saved_ref, up_ref, down_ref, *rest):
        p_refs, (grad_out, sums), rest = rest[-16:-12], rest[-12:-10], rest[-10:]
        ys, up, down, slopes, u, grad, ps, in_sem, p_sem, o_sem = rest
        load_down = move(down_ref, down, in_sem.at[4])
        loads, slope_loads = {}, {}
        for r in ORDER:
            loads[r] = move((got_ref if r % 2 else own_ref).at[r // 2], ys.at[r], in_sem.at[r])
            slope_loads[r] = move(saved_ref.at[SLOPE, seq, pl.ds(r * rows, rows)], slopes.at[r], in_sem.at[6 + r])
        load_up = move(up_ref, up, in_sem.at[5])
        pending = []

        def project(k):
            r = ORDER[k]
            loads[r].wait()
            slope_loads[r].wait()
            u[k % 2] = dot(ys[r], down[...], NT)

        load_down.wait()
        project(0)
        load_up.wait()
        total = jnp.zeros((8, units), F32)
        for k, r in enumerate(ORDER):
            if k + 1 < parts:
                project(k + 1)
            gu = (u[k % 2] * slopes[r].astype(F32)).astype(BF16)
            grad[r] = gu
            total += jnp.sum(gu.astype(F32).reshape(rows // 8, 8, units), axis=0)
            ps[r] = dot(gu, up[...], NT).astype(BF16)
            pending.append(move(ps.at[r], p_refs[r], p_sem.at[r]))
            pending.append(move(grad.at[r], grad_out.at[GRAD, seq, pl.ds(r * rows, rows)], o_sem.at[4 + r]))
        sums[...] = jnp.sum(total, axis=0, keepdims=True)
        for copy in pending:
            copy.wait()

    return kernel_call(
        body,
        (
            *[struct((rows, feats), BF16)] * 4,
            struct((4, seqs, length, units), BF16),
            struct((1, units), F32),
        ),
        (ANY,) * 4 + (HBM, whole((1, units))),
        [ANY] * 2 + [HBM] * 3 + [ANY] * len(earlier),
        scratch=[
            VMEM((parts, rows, feats), BF16),
            VMEM(w_up.shape, BF16),
            VMEM(w_down.shape, BF16),
            VMEM((parts, rows, units), BF16),
            VMEM((2, rows, units), F32),
            VMEM((parts, rows, units), BF16),
            VMEM((parts, rows, feats), BF16),
            DMA((10,)),
            DMA((4,)),
            DMA((8,)),
        ],
        flops=4 * length * feats * units,
        nbytes=length * feats * 14,
        aliases={2: 4},
        name="feed_backward",
    )(own, got, saved, w_up, w_down, *earlier)


def entries(ref, seq, part, place, rows):
    at = lax.bitwise_xor(jnp.int32(part), place) * rows
    return ref[seq : seq + 1, pl.ds(pl.multiple_of(at, rows), rows)].astype(F32)


def contrast_scores(place, ends, docs, labels, units):
    rows, feats = units[0].shape[0] - EXTRA, units[0].shape[1]
    factor = CONTRAST_SCALE / feats * LOG2E
    count = len(units)
    seqs = count // 4

    def body(t_ref, end_ref, doc_ref, lab_ref, *rest):
        refs, rest = rest[:count], rest[count:]
        exp_out, col_out, row_out, loss_out, both, exps, sums, in_sem, out_sem = rest
        t = t_ref[0]
        loads = [move(refs[k].at[pl.ds(0, rows)], both.at[k], in_sem.at[k]) for k in range(count)]
        for copy in loads:
            copy.wait()
        pending = []
        for s in range(4):
            seq, part = s // 2, s % 2 * 2
            own_lab = column(entries(lab_ref, seq, part, t, rows))

            def block(k, own_doc, seq=seq, part=part, s=s, own_lab=own_lab):
                e = jnp.exp2(dot(both[seq * 4 + part], both[k], NT) * factor)
                if own_doc is not None:
                    e = jnp.where(own_doc != entries(doc_ref, seq, k % 4, t, rows), e, 0.0)
                exps[s, :, k * rows : (k + 1) * rows] = e.astype(BF16)
                picked = jnp.where(own_lab == entries(lab_ref, k // 4, k % 4, t, rows), e, 0.0)
                lanes = [slice(c * 128, (c + 1) * 128) for c in range(rows // 128)]
                fold = lambda v: functools.reduce(jnp.add, [v[:, lane] for lane in lanes])
                return fold(e), fold(picked)

            terms = [block(k, None) for k in range(count) if k // 4 != seq]
            sums[0] = functools.reduce(jnp.add, [a for a, _ in terms])
            sums[1] = functools.reduce(jnp.add, [b for _, b in terms])
            single = end_ref[seq, 0] == end_ref[seq, 1]
            inner = slice(seq * 4 * rows, (seq + 1) * 4 * rows)

            @pl.when(single)
            def _(s=s, inner=inner):
                exps[s, :, inner] = jnp.zeros((rows, 4 * rows), BF16)

            @pl.when(jnp.logical_not(single))
            def _(seq=seq, part=part, block=block):
                own_doc = column(entries(doc_ref, seq, part, t, rows))
                for k in range(seq * 4, seq * 4 + 4):
                    a, b = block(k, own_doc)
                    sums[0] += a
                    sums[1] += b

            pending.append(move(exps.at[s], exp_out.at[s], out_sem.at[s]))
            wide = lane_pair(
                jnp.sum(sums[0], axis=-1, keepdims=True), jnp.sum(sums[1], axis=-1, keepdims=True), rows
            )
            col_out[s * rows : (s + 1) * rows, :] = wide
            flat = jnp.transpose(wide)[:8, :]
            row_out[:, s * rows : (s + 1) * rows] = flat
            if part == 0:
                logs = jnp.log(flat)
                loss_out[seq : seq + 1, :] = logs[0:1] - logs[1:2]
        for copy in pending:
            copy.wait()

    return kernel_call(
        body,
        (
            struct((16, rows, count * rows), BF16),
            struct((4 * rows, 128), F32),
            struct((8, 4 * rows), F32),
            struct((seqs, rows), F32),
        ),
        (HBM, whole((4 * rows, 128)), whole((8, 4 * rows)), whole((seqs, rows))),
        [SMEM, SMEM, whole(docs.shape), whole(labels.shape)] + [ANY] * count,
        scratch=[
            VMEM((count, rows, feats), BF16),
            VMEM((4, rows, count * rows), BF16),
            VMEM((2, rows, 128), F32),
            DMA((count,)),
            DMA((4,)),
        ],
        flops=2 * 4 * rows * count * rows * feats,
        nbytes=count * rows * feats * 4,
        trans=4 * rows * count * rows,
        name="contrast_scores",
    )(place, ends, docs, labels, *units)


def contrast_grads(seq, place, ends, labels, units, exps, col_sums, row_own, row_got, cot, cot_got):
    rows, feats = units[0].shape[0] - EXTRA, units[0].shape[1]
    factor = CONTRAST_SCALE / feats
    count = len(units)
    span = 4 * rows

    def body(t_ref, end_ref, lab_ref, col, own, got, *rest):
        refs, (e_ref, cot_ref, other_ref), rest = rest[:count], rest[count : count + 3], rest[count + 3 :]
        full, low, both, exps, scales, cots, grad, gn, full_v, low_v, in_sem, e_sem, q_sem, c_sem, o_sem = rest
        t = t_ref[0]
        order = [k for k in range(count) if k // 4 != seq] + [k for k in range(count) if k // 4 == seq]
        e_loads = [move(e_ref.at[2 * seq + h], exps.at[h], e_sem.at[h]) for h in range(2)]
        loads = {
            k: move(refs[k].at[pl.ds(0, rows)], both.at[pl.ds(k * rows, rows)], in_sem.at[k]) for k in order
        }
        small = [
            (
                move(refs[seq * 4 + h * 2].at[pl.ds(rows, EXTRA)], scales.at[h], q_sem.at[h]),
                move(other_ref if h else cot_ref.at[seq], cots.at[h], c_sem.at[h]),
            )
            for h in range(2)
        ]
        single = end_ref[seq, 0] == end_ref[seq, 1]

        def weigh(h, blocks):
            s = 2 * seq + h
            own_lab = column(entries(lab_ref, seq, h * 2, t, rows))
            inv = CONTRAST_WEIGHT / col[s * rows : (s + 1) * rows, :]
            all_i, pos_i = inv[:, 0:1], inv[:, 1:2]
            for k in blocks:
                other, piece = k // 4, k % 4
                source = own if piece % 2 == 0 else got
                at = (other * 2 + piece // 2) * rows
                inv_j = CONTRAST_WEIGHT / source[0:2, at : at + rows]
                same = own_lab == entries(lab_ref, other, piece, t, rows)
                coef = (all_i + inv_j[0:1]) - jnp.where(same, pos_i + inv_j[1:2], 0.0)
                cols = slice(k * rows, (k + 1) * rows)
                grad[h, :, cols] = (exps[h, :, cols].astype(F32) * coef).astype(BF16)

        outer = slice((1 - seq) * span, (2 - seq) * span)
        inner = slice(seq * span, (seq + 1) * span)
        for h in range(2):
            e_loads[h].wait()
        weigh(0, order[:4])
        for k in order:
            loads[k].wait()
        for h in range(2):
            if h == 0:
                weigh(1, order[:4])
            gn[h] = dot(grad[h, :, outer], both[outer, :])

        @pl.when(jnp.logical_not(single))
        def _():
            for h in range(2):
                weigh(h, order[4:])
                gn[h] += dot(grad[h, :, inner], both[inner, :])

        pending = []
        for h in range(2):
            first = (seq * 4 + h * 2) * rows
            n = both[first : first + rows, :].astype(F32)
            g = gn[h] * factor
            change = g - n * jnp.mean(g * n, axis=-1, keepdims=True)
            for copy in small[h]:
                copy.wait()
            pieces = scales[h, :, :rows].astype(F32)
            gy = cots[h].astype(F32) + column(pieces[0:1] + pieces[1:2]) * change
            low_v[h] = gy.astype(BF16)
            pending.append(move(low_v.at[h], low.at[h], o_sem.at[h]))
            if h == 0:
                full_v[...] = gy
                pending.append(move(full_v, full, o_sem.at[2]))
        for copy in pending:
            copy.wait()

    return kernel_call(
        body,
        (struct((rows, feats), F32), struct((2, rows, feats), BF16)),
        (ANY,) * 2,
        [
            SMEM,
            SMEM,
            whole(labels.shape),
            whole((4 * rows, 128)),
            whole((8, 4 * rows)),
            whole((8, 4 * rows)),
        ]
        + [ANY] * count
        + [HBM] * 2
        + [ANY],
        scratch=[
            VMEM((count * rows, feats), BF16),
            VMEM((2, rows, count * rows), BF16),
            VMEM((2, EXTRA, feats), BF16),
            VMEM((2, rows, feats), BF16),
            VMEM((2, rows, count * rows), BF16),
            VMEM((2, rows, feats), F32),
            VMEM((rows, feats), F32),
            VMEM((2, rows, feats), BF16),
            DMA((count,)),
            DMA((2,)),
            DMA((2,)),
            DMA((2,)),
            DMA((3,)),
        ],
        flops=4 * rows * count * rows * feats,
        nbytes=count * rows * feats * 4,
        name="contrast_grads",
    )(place, ends, labels, col_sums, row_own, row_got, *units, exps, cot, cot_got)


def down_grad(saved, own, got):
    seqs, length, units = saved.shape[1:]
    rows, feats = own[0].shape[1:]
    tiles = units // TILE

    def body(a_ref, *rest):
        own_refs, got_refs = rest[:seqs], rest[seqs : 2 * seqs]
        out_ref, a, b, out, a_sem, b_sem, o_sem = rest[2 * seqs :]
        b_loads = []
        for s in range(seqs):
            for r in range(4):
                src = (got_refs if r % 2 else own_refs)[s].at[r // 2]
                b_loads.append(move(src, b.at[s, pl.ds(r * rows, rows)], b_sem.at[4 * s + r]))
        columns = [pl.ds(i * TILE, TILE) for i in range(tiles)]
        a_loads = [move(a_ref.at[ACT, :, :, columns[i]], a.at[i], a_sem.at[i]) for i in range(tiles)]
        for copy in b_loads:
            copy.wait()
        stores = []
        for i in range(tiles):
            a_loads[i].wait()
            out[i] = functools.reduce(jnp.add, [dot(a[i, s], b[s], TN) for s in range(seqs)]).astype(BF16)
            stores.append(move(out.at[i], out_ref.at[columns[i]], o_sem.at[i]))
        for copy in stores:
            copy.wait()

    return kernel_call(
        body,
        struct((units, feats), BF16),
        ANY,
        [HBM] + [ANY] * (2 * seqs),
        scratch=[
            VMEM((tiles, seqs, length, TILE), BF16),
            VMEM((seqs, length, feats), BF16),
            VMEM((tiles, TILE, feats), BF16),
            DMA((tiles,)),
            DMA((4 * seqs,)),
            DMA((tiles,)),
        ],
        flops=2 * seqs * length * units * feats,
        nbytes=4 * seqs * length * feats,
        name="down_grad",
    )(saved, *own, *got)


TILE = 256


def send_half(tile, tiles, high, src, to_other, kept, at, sem):
    upper = tile >= tiles // 2
    rows = pl.ds((tile % (tiles // 2)) * TILE, TILE)

    @pl.when(high == int(upper))
    def _():
        pltpu.make_async_copy(src, kept.at[rows, at], sem).start()

    @pl.when(high != int(upper))
    def _():
        pltpu.make_async_copy(src, to_other.at[rows, at], sem).start()

    return pltpu.make_async_copy(src, kept.at[rows, at], sem)


def weight_grad(saved, flags, bit):
    seqs, length, out_rows = saved.shape[1:]
    cols = out_rows
    tiles = out_rows // TILE

    def body(flag, s_ref, other_ref, kept_ref, a, b, out, a_sem, b_sem, o_sem):
        b_loads = [move(s_ref.at[GRAD, s], b.at[s], b_sem.at[s]) for s in range(seqs)]
        columns = [pl.ds(i * TILE, TILE) for i in range(tiles)]
        a_loads = [move(s_ref.at[ROWS, :, :, columns[i]], a.at[i], a_sem.at[i]) for i in range(tiles)]
        for copy in b_loads:
            copy.wait()
        stores = []
        for i in range(tiles):
            a_loads[i].wait()
            out[i] = functools.reduce(jnp.add, [dot(a[i, s], b[s], TN) for s in range(seqs)]).astype(BF16)
            stores.append(
                send_half(i, tiles, flag[bit], out.at[i], other_ref, kept_ref, pl.ds(0, cols), o_sem.at[i])
            )
        for copy in stores:
            copy.wait()

    return kernel_call(
        body,
        (struct((out_rows // 2, cols), BF16),) * 2,
        (ANY,) * 2,
        [pl.BlockSpec(memory_space=pltpu.SMEM)] + [HBM],
        scratch=[
            VMEM((tiles, seqs, length, TILE), BF16),
            VMEM((seqs, length, cols), BF16),
            VMEM((tiles, TILE, cols), BF16),
            DMA((tiles,)),
            DMA((seqs,)),
            DMA((tiles,)),
        ],
        flops=2 * seqs * length * out_rows * cols,
        nbytes=4 * seqs * length * cols,
        name="weight_grad",
    )(flags, saved)


def head_grads(saved, grads, seqs, feats, flags, bits):
    length = saved.shape[1]
    width = (saved.shape[2] - feats) // 4
    tiles = feats // width

    def body(*refs):
        flag, s_ref, h_ref = refs[:3]
        first_refs, second_refs = refs[3:5], refs[5:7]
        a, g, r, first, second, a_sem, g_sem, r_sem, o_sem = refs[7:]
        both = pl.ds(0, seqs)
        columns = [pl.ds(i * width, width) for i in range(tiles)]
        g_loads = []
        for n, ref in enumerate((h_ref, h_ref, h_ref, s_ref)):
            g_loads.append(move(ref.at[both, :, pl.ds(feats + n * width, width)], g.at[n], g_sem.at[n]))
        a_loads, r_loads = [], []
        for i in range(tiles):
            a_loads.append(move(s_ref.at[both, :, columns[i]], a.at[i], a_sem.at[i]))
            r_loads.append(move(h_ref.at[both, :, columns[i]], r.at[i], r_sem.at[i]))
        for copy in g_loads:
            copy.wait()

        def total(x, y):
            return functools.reduce(jnp.add, [dot(x[s], y[s], TN) for s in range(seqs)]).astype(BF16)

        stores = []
        for i in range(tiles):
            a_loads[i].wait()
            first[i, :, :width] = total(a[i], g[0])
            first[i, :, width:] = total(a[i], g[1])
            second[i, :, :width] = total(a[i], g[2])
            r_loads[i].wait()
            second[i, :, width:] = total(g[3], r[i])
            for n, (src, outs) in enumerate(((first, first_refs), (second, second_refs))):
                stores.append(
                    send_half(i, tiles, flag[bits[n]], src.at[i], *outs, pl.ds(0, 2 * width), o_sem.at[2 * i + n])
                )
        for copy in stores:
            copy.wait()

    return kernel_call(
        body,
        (struct((feats // 2, 2 * width), BF16),) * 4,
        (ANY,) * 4,
        [pl.BlockSpec(memory_space=pltpu.SMEM)] + [HBM] * 2,
        scratch=[
            VMEM((tiles, seqs, length, width), BF16),
            VMEM((4, seqs, length, width), BF16),
            VMEM((tiles, seqs, length, width), BF16),
            VMEM((tiles, width, 2 * width), BF16),
            VMEM((tiles, width, 2 * width), BF16),
            DMA((tiles,)),
            DMA((4,)),
            DMA((tiles,)),
            DMA((2 * tiles,)),
        ],
        flops=2 * seqs * length * feats * width * 4,
        nbytes=4 * seqs * length * feats,
        name="head_grads",
    )(flags, saved, grads)


def halve_step(flags, bit, keep, got):
    rows, cols = keep.shape
    half = rows // 2

    def body(flag, k_ref, g_ref, *outs):
        if bit is None:
            outs[0][...] = (k_ref[...].astype(F32) + g_ref[...].astype(F32)).astype(BF16)
            return
        for high in (0, 1):

            @pl.when(flag[bit] == high)
            def _(high=high):
                for out, upper in ((outs[0], 1 - high), (outs[1], high)):
                    at = slice(upper * half, (upper + 1) * half)
                    out[...] = (k_ref[at, :].astype(F32) + g_ref[at, :].astype(F32)).astype(BF16)

    shape = (rows, cols) if bit is None else (half, cols)
    return kernel_call(
        body,
        (struct(shape, BF16),) * (1 if bit is None else 2),
        (whole(shape),) * (1 if bit is None else 2),
        [pl.BlockSpec(memory_space=pltpu.SMEM)] + [whole((rows, cols))] * 2,
        nbytes=rows * cols * 6,
        limit=SMALL,
        name="halve_step",
    )(flags, keep, got)


def join_step(flags, bit, own, got, dtype):
    rows, cols = own.shape
    steps = 2 if dtype == F32 else 1
    part = rows // steps

    def body(flag, own_ref, got_ref, out):
        for high in (0, 1):

            @pl.when(flag[bit] == high)
            def _(high=high):
                out[high] = own_ref[...].astype(dtype)
                out[1 - high] = got_ref[...].astype(dtype)

    block = pl.BlockSpec((part, cols), lambda i: (i, 0))
    return kernel_call(
        body,
        struct((2, rows, cols), dtype),
        pl.BlockSpec((2, part, cols), lambda i: (0, i, 0)),
        [pl.BlockSpec(memory_space=pltpu.SMEM), block, block],
        grid=(steps,),
        nbytes=rows * cols * 8,
        limit=SMALL,
        name="join_step",
    )(flags, own, got).reshape(2 * rows, cols)


def part_outputs(parts, order):
    rows, cols = parts.shape
    step = rows >> len(order)

    def place(i):
        return functools.reduce(
            jnp.add, [((i >> bit) & 1) << (len(order) - 1 - n) for n, bit in enumerate(order)]
        )

    def body(part, out):
        out[...] = part[...].astype(F32)

    return kernel_call(
        body,
        struct((rows, cols), F32),
        pl.BlockSpec((step, cols), lambda i: (place(i), 0)),
        [pl.BlockSpec((step, cols), lambda i: (i, 0))],
        grid=(1 << len(order),),
        nbytes=6 * rows * cols,
        limit=SMALL,
        name="part_outputs",
    )(parts)


def head_outputs(flags, bits, first, second):
    feats = 2 * first[0].shape[0]
    width = first[0].shape[1] // 2
    tile = width

    def body(h_ref, a_ref, b_ref, c_ref, d_ref, qkv, out):
        mine = (lax.div(pl.program_id(0) * tile, feats // 2) == h_ref[bits[0]])

        for case, x in ((True, a_ref), (False, b_ref)):
            @pl.when(mine == case)
            def _(x=x):
                qkv[0] = x[:, :width].astype(F32)
                qkv[1] = x[:, width:].astype(F32)

        mine_two = (lax.div(pl.program_id(0) * tile, feats // 2) == h_ref[bits[1]])
        for case, y in ((True, c_ref), (False, d_ref)):
            @pl.when(mine_two == case)
            def _(y=y):
                qkv[2] = y[:, :width].astype(F32)
                out[...] = y[:, width:].astype(F32)

    half = pl.BlockSpec((tile, 2 * width), lambda i, h: (lax.rem(i, feats // 2 // tile), 0))
    return kernel_call(
        body,
        (struct((3, feats, width), F32), struct((width, feats), F32)),
        (pl.BlockSpec((3, tile, width), lambda i, h: (0, i, 0)), pl.BlockSpec((width, tile), lambda i, h: (0, i))),
        [half] * 4,
        grid=(feats // tile,),
        nbytes=10 * feats * width * 4,
        prefetch=1,
        limit=SMALL,
        name="head_outputs",
    )(flags, *first, *second)


def swap(value, axis, size, bit):
    return lax.ppermute(value, axis, [(i, i ^ bit) for i in range(size)])


CORE, CROSS = 1, 2


def tensor_swap(value, bit):
    return swap(value, "tensor", 4, bit)


def tie(value, *earlier):
    return lax.optimization_barrier((value, *earlier))[0] if earlier else value


class Gather:
    def __init__(self, value):
        self.value = value
        self.cross = tensor_swap(value, CROSS)
        self.core = tensor_swap(value, CORE)

    def blocks(self, *earlier):
        return [self.value, self.core, self.cross, tensor_swap(tie(self.cross, *earlier), CORE)]


class Scatter:
    def __init__(self, blocks):
        self.own, self.other = blocks[0], blocks[2]
        self.core_other = tensor_swap(blocks[3], CORE)
        self.core_own = tensor_swap(blocks[1], CORE)
        self.mark = blocks[3]

    def cross(self, *earlier):
        block = (tie(self.other, *earlier).astype(F32) + self.core_other.astype(F32)).astype(BF16)
        self.parts = (self.own, self.core_own, tensor_swap(block, CROSS))
        return block


class DpSum:
    def __init__(self, send, keep, flags, size, order):
        self.send, self.value, self.flags, self.size = send, keep, flags, size
        self.left = [(bit, True) for bit in order] + [(bit, False) for bit in reversed(order)]
        self.got, self.now = None, None

    def advance(self, *earlier):
        if self.now is not None and self.now[1]:
            more = self.left and self.left[0][1]
            parts = halve_step(self.flags, self.left[0][0] if more else None, tie(self.value, *earlier), self.got)
            self.send, self.value = parts if more else (parts[0], parts[0])
        elif self.now is not None:
            self.send = self.value = join_step(self.flags, self.now[0], tie(self.value, *earlier), self.got, BF16)
        self.now = self.left.pop(0)
        self.got = swap(self.send, "dp", self.size, 1 << self.now[0])
        return self.send

    def halves(self):
        return self.value, self.got


def shards(
    dp_size,
    tokens,
    doc_ids,
    targets,
    cotangent,
    ln1_gain,
    ln1_bias,
    qkv_weight,
    query_bias,
    value_bias,
    output_weight,
    out_bias,
    ln2_gain,
    ln2_bias,
    up_weight,
    up_bias,
    down_weight,
    down_bias,
):
    seqs, rows, feats = tokens.shape
    length = doc_ids.shape[1]
    parts = length // rows
    me = lax.axis_index("tensor")
    place = me.reshape(1).astype(jnp.int32)
    vec = lambda v: v.astype(F32).reshape(1, -1)
    gain_one, shift_one, gain_two, shift_two = vec(ln1_gain), vec(ln1_bias), vec(ln2_gain), vec(ln2_bias)
    out_offset, down_offset, up_shift = vec(out_bias), vec(down_bias), vec(up_bias)
    head_shift = vec(jnp.concatenate([query_bias, value_bias]))
    ends = doc_ids[:, :: length - 1]

    fine = 16
    paired = (jnp.arange(feats, dtype=jnp.int32) // 2).astype(F32)
    freq = jnp.exp(paired * (-2.0 * math.log(10000.0) / feats))[None, :]
    odd = (jnp.arange(feats, dtype=jnp.int32) % 2 == 1)[None, :]
    coarse_at = (me * rows + fine * jnp.arange(rows // fine, dtype=jnp.int32)).astype(F32)[:, None] * freq
    fine_at = jnp.arange(fine, dtype=jnp.int32).astype(F32)[:, None] * freq
    sin_a, cos_a = jnp.sin(coarse_at), jnp.cos(coarse_at)
    tables = (jnp.where(odd, cos_a, sin_a), jnp.where(odd, -sin_a, cos_a), jnp.cos(fine_at), jnp.sin(fine_at))

    hidden, stream, grad_r = [None] * 2, [None] * 2, [None] * 2
    kept, up_sums, head_sums, sums_one, sums_two = [None] * 2, [None] * 2, [None] * 2, [None] * 2, [None] * 2
    shared = {"attend": None, "feed": None, "act": None, "heads": None, "input": None}

    def attend(s, gathered, *earlier):
        *blocks, shared["attend"], kept[s] = attend_forward(
            s, tie(place, *earlier), doc_ids, head_shift, gathered, qkv_weight, output_weight, shared["attend"]
        )
        return Scatter(blocks)

    def middle_rows(s, scatter, *earlier):
        stream[s], normed = second_norm(hidden[s], scatter.parts, tie(out_offset, *earlier), gain_two, shift_two)
        return normed, Gather(normed)

    def feed(s, gathered, *earlier):
        *blocks, shared["feed"] = feed_forward(
            s, seqs, gathered, tie(up_shift, *earlier), up_weight, down_weight, shared["feed"]
        )
        return Scatter(blocks)

    def last_rows(s, scatter, *earlier):
        shared["act"], unit = output_rows(
            s, seqs, stream[s], scatter.parts, tie(down_offset, *earlier), shared["act"]
        )
        return unit, Gather(unit)

    hidden[0], normed_a = first_norm(0, tokens, tables, gain_one, shift_one)
    rows_a = Gather(normed_a)
    hidden[1], normed_b = first_norm(1, tie(tokens, normed_a), tables, gain_one, shift_one)
    rows_b = Gather(normed_b)
    at_a = attend(0, rows_a.blocks(normed_b))
    block = at_a.cross(rows_b.cross)
    at_b = attend(1, rows_b.blocks(), block)
    normed, rows_a = middle_rows(0, at_a, at_b.mark)
    block = at_b.cross(normed)
    ff_a = feed(0, rows_a.blocks(), block)
    normed, rows_b = middle_rows(1, at_b, ff_a.mark)
    block = ff_a.cross(normed)
    ff_b = feed(1, rows_b.blocks(), block)
    unit, units_a = last_rows(0, ff_a, ff_b.mark)
    block = ff_b.cross(unit)
    unit, units_b = last_rows(1, ff_b, block)
    cots = [tensor_swap(tie(cotangent[s], unit), CROSS) for s in range(2)]

    units = units_a.blocks() + units_b.blocks()
    exps, col_sums, row_sums, loss = contrast_scores(place, ends, doc_ids, targets, units)
    row_got = tensor_swap(row_sums, CORE)
    grad_y, low_y, got_y = [None] * 2, [None] * 2, [None] * 2
    for s in range(2):
        grad_y[s], low_y[s] = contrast_grads(
            s, tie(place, *low_y[:s]), ends, targets, units, exps, col_sums, row_sums, row_got, cotangent, cots[s]
        )
        got_y[s] = tensor_swap(tie(low_y[s], cots[1]), CORE)

    def feed_back(s, *earlier):
        *blocks, shared["feed"], up_sums[s] = feed_backward(
            s, low_y[s], got_y[s], shared["feed"], up_weight, down_weight, earlier
        )
        return Scatter(blocks)

    def middle_back(s, scatter, *earlier):
        grad_r[s], low, sums_two[s] = norm_backward(
            s, seqs, stream[s], scatter.parts, tie(gain_two, *earlier), grad_y[s], False, None
        )
        return low, Gather(low)

    def attend_back(s, gathered, *earlier):
        *blocks, shared["heads"], head_sums[s] = attend_backward(
            s, tie(place, *earlier), doc_ids, gathered, shared["attend"], kept[s], qkv_weight, output_weight,
            shared["heads"],
        )
        return Scatter(blocks)

    def first_back(s, scatter, *earlier):
        shared["input"], sums_one[s] = norm_backward(
            s, seqs, hidden[s], scatter.parts, tie(gain_one, *earlier), grad_r[s], True, shared["input"]
        )
        return sums_one[s]

    bits = list(range(dp_size.bit_length() - 1))
    other_bits = bits[1::-1] + bits[2:]
    flags = (lax.axis_index("dp") >> jnp.arange(len(bits), dtype=jnp.int32)) & 1
    grad_down_w = down_grad(shared["feed"], low_y, got_y)
    down_part = lax.psum_scatter(grad_down_w, "dp", scatter_dimension=0, tiled=True)
    fb_a = feed_back(0, grad_down_w)
    fb_b = feed_back(1, fb_a.cross())
    low, rows_a = middle_back(0, fb_a, fb_b.mark)
    block = fb_b.cross(low)
    up_sum = DpSum(*weight_grad(tie(shared["feed"], block), flags, bits[0]), flags, dp_size, bits)
    sent = up_sum.advance()
    ab_a = attend_back(0, rows_a.blocks(sent), sent)
    low, rows_b = middle_back(1, fb_b, ab_a.mark)
    block = ab_a.cross(low)
    sent = up_sum.advance(block)
    ab_b = attend_back(1, rows_b.blocks(sent), sent, down_part)
    down_all = lax.all_gather(tie(down_part, sent), "dp", axis=0, tiled=True)
    sent = up_sum.advance(ab_b.mark)
    sums = first_back(0, ab_a, sent)
    block = ab_b.cross(sums)
    first_send, first_keep, second_send, second_keep = head_grads(
        tie(shared["attend"], block), shared["heads"], seqs, feats, flags, (bits[0], other_bits[0])
    )
    first = DpSum(first_send, first_keep, flags, dp_size, bits)
    second = DpSum(second_send, second_keep, flags, dp_size, other_bits)
    sent = (first.advance(), second.advance())
    sums = first_back(1, ab_b, *sent)
    sent = (sums,)

    total = lambda items: functools.reduce(jnp.add, items)
    heads_sum = total(head_sums)
    heads_row = jnp.pad(heads_sum.reshape(1, -1), ((0, 0), (0, feats - heads_sum.size)))
    small = jnp.concatenate([total(sums_one)[:2], total(sums_two), total(up_sums), heads_row])
    swaps = [("dp", dp_size, 1 << bit) for bit in bits] + [("tensor", 4, CORE), ("tensor", 4, CROSS)]
    local = None
    while swaps or first.left:
        if swaps:
            axis, size, bit = swaps.pop(0)
            if axis == "tensor" and local is None:
                local, small = small[6:], small[:6]
            small = small + swap(tie(small, *sent), axis, size, bit)
        sent = (small,)
        if up_sum.left:
            sent += (up_sum.advance(*sent),)
        if first.left:
            sent = (first.advance(*sent), second.advance(*sent))
        if len(first.left) == 2:
            grad_down_w = tie(down_all, *sent).astype(F32)
            sent += (grad_down_w,)
    own, got = up_sum.halves()
    grad_up_w = join_step(flags, bits[0], tie(own, *sent), got, F32)
    grad_qkv_w, grad_out_w = head_outputs(flags, (bits[0], other_bits[0]), first.halves(), second.halves())
    return (
        shared["act"],
        loss,
        shared["input"],
        small[0],
        small[1],
        grad_qkv_w,
        local[1, : heads_sum.shape[1]],
        local[1, heads_sum.shape[1] : 2 * heads_sum.shape[1]],
        grad_out_w,
        small[4],
        small[2],
        small[3],
        grad_up_w,
        local[0],
        grad_down_w,
        small[5],
    )


def solution(mesh):
    in_specs = (
        P("dp", "tensor", None),
        P("dp", None),
        P("dp", None),
        P("dp", "tensor", None),
        P(),
        P(),
        P(None, None, "tensor"),
        P("tensor"),
        P("tensor"),
        P("tensor", None),
        P(),
        P(),
        P(),
        P(None, "tensor"),
        P("tensor"),
        P("tensor", None),
        P(),
    )
    out_specs = (
        P("dp", "tensor", None),
        P("dp", "tensor"),
        P("dp", "tensor", None),
        P(),
        P(),
        P(None, None, "tensor"),
        P("tensor"),
        P("tensor"),
        P("tensor", None),
        P(),
        P(),
        P(),
        P(None, "tensor"),
        P("tensor"),
        P("tensor", None),
        P(),
    )
    return jax.shard_map(
        functools.partial(shards, mesh.shape["dp"]),
        mesh=mesh,
        in_specs=in_specs,
        out_specs=out_specs,
        check_vma=False,
    )
```

```python
import functools
import math

import jax
import jax.numpy as jnp
from jax import lax
from jax.experimental import pallas as pl
from jax.experimental.pallas import tpu as pltpu
from jax.sharding import PartitionSpec as P

HEADS = 8
NORM_EPS = 1e-05
CONTRAST_SCALE = 32.0
CONTRAST_WEIGHT = 64.0
NEGATIVE = -1e30
LOG2E = math.log2(math.e)
F32 = jnp.float32
BF16 = jnp.bfloat16
MIB = 1 << 20
LIMIT, SMALL = 52, 14
COST = 0.02
NN = (((1,), (0,)), ((), ()))
NT = (((1,), (1,)), ((), ()))
TN = (((0,), (0,)), ((), ()))
VMEM = pltpu.VMEM


def dot(a, b, dims=NN):
    return lax.dot_general(a, b, dims, preferred_element_type=F32)


def whole(shape):
    return pl.BlockSpec(shape, lambda *_: (0,) * len(shape))


def kernel_call(body, outs, out_specs, in_specs, grid=(1,), scratch=(), flops=0, nbytes=0, trans=0,
                limit=LIMIT, aliases=None, prefetch=0, name=None):
    return pl.pallas_call(
        body,
        out_shape=outs,
        grid_spec=pltpu.PrefetchScalarGridSpec(
            num_scalar_prefetch=prefetch,
            grid=grid,
            in_specs=in_specs,
            out_specs=out_specs,
            scratch_shapes=scratch,
        ),
        name=name,
        input_output_aliases=aliases or {},
        cost_estimate=pl.CostEstimate(
            flops=int(flops * COST), bytes_accessed=int(nbytes * COST), transcendentals=int(trans * COST)
        ),
        compiler_params=pltpu.CompilerParams(vmem_limit_bytes=limit * MIB),
    )


def struct(shape, dtype):
    return jax.ShapeDtypeStruct(shape, dtype)


ANY = pl.BlockSpec(memory_space=pl.ANY)
HBM = pl.BlockSpec(memory_space=pltpu.HBM)
SMEM = pl.BlockSpec(memory_space=pltpu.SMEM)
DMA = pltpu.SemaphoreType.DMA


def move(src, dst, sem):
    copy = pltpu.make_async_copy(src, dst, sem)
    copy.start()
    return copy


def column(row):
    return jnp.transpose(jnp.broadcast_to(row, (8, row.shape[1])))[:, :1]


def norm_stats(v):
    centered = v - jnp.mean(v, axis=-1, keepdims=True)
    rstd = lax.rsqrt(jnp.mean(centered * centered, axis=-1, keepdims=True) + NORM_EPS)
    return centered * rstd, rstd


ROW_STEPS = 4


def row_blocks(rows, cols):
    return pl.BlockSpec((rows // ROW_STEPS, cols), lambda i: (i, 0))


def first_norm(seq, tokens, tables, gain, shift):
    rows, feats = tokens.shape[1:]
    fine = tables[2].shape[0]
    step = rows // ROW_STEPS

    def body(tok, pa, qa, cb, sb, g, b, h_out, a_out):
        i = pl.program_id(0)
        for c in range(step // fine):
            at = pl.ds(c * fine, fine)
            row = pl.ds(i * (step // fine) + c, 1)
            pos = pa[row, :] * cb[...] + qa[row, :] * sb[...]
            h = tok[0, at, :].astype(F32) + pos
            h_out[at, :] = h
            z, _ = norm_stats(h)
            a_out[at, :] = (z * g[...] + b[...]).astype(BF16)

    return kernel_call(
        body,
        (struct((rows, feats), F32), struct((rows, feats), BF16)),
        (row_blocks(rows, feats), row_blocks(rows, feats)),
        [pl.BlockSpec((1, step, feats), lambda i: (seq, i, 0))]
        + [whole(t.shape) for t in tables]
        + [whole((1, feats))] * 2,
        grid=(ROW_STEPS,),
        nbytes=rows * feats * 8,
        limit=SMALL,
        name="first_norm",
    )(tokens, *tables, gain, shift)


def joined(parts, at):
    return functools.reduce(jnp.add, [p[at, :].astype(F32) for p in parts])


def second_norm(h, parts, offset, gain, shift):
    rows, feats = h.shape
    chunk = 32
    step = rows // ROW_STEPS

    def body(h_ref, k_ref, c_ref, x_ref, o_ref, g, b, r_out, n_out):
        for c in range(step // chunk):
            at = pl.ds(c * chunk, chunk)
            r = h_ref[at, :] + joined((k_ref, c_ref, x_ref), at) + o_ref[...]
            r_out[at, :] = r
            z, _ = norm_stats(r)
            n_out[at, :] = (z * g[...] + b[...]).astype(BF16)

    block = row_blocks(rows, feats)
    return kernel_call(
        body,
        (struct((rows, feats), F32), struct((rows, feats), BF16)),
        (block, block),
        [block] * 4 + [whole((1, feats))] * 3,
        grid=(ROW_STEPS,),
        nbytes=rows * feats * 16,
        limit=SMALL,
        name="second_norm",
    )(h, *parts, offset, gain, shift)


EXTRA = 16


def output_rows(seq, seqs, r1, parts, offset, previous):
    rows, feats = r1.shape
    step, chunk = 128, 32

    def body(r_ref, k_ref, c_ref, x_ref, o_ref, *rest):
        act_out, n_out, q_all = rest[-3:]
        i = pl.program_id(0)
        for c in range(step // chunk):
            at = pl.ds(c * chunk, chunk)
            y = r_ref[at, :] + joined((k_ref, c_ref, x_ref), at) + o_ref[...]
            act_out[0, at, :] = y.astype(BF16)
            q = lax.rsqrt(jnp.mean(y * y, axis=-1, keepdims=True) + NORM_EPS)
            n_out[pl.ds(pl.multiple_of(i * step + c * chunk, chunk), chunk), :] = (y * q).astype(BF16)
            q_all[at, :] = jnp.broadcast_to(q, (chunk, step))

        @pl.when(i == 0)
        def _():
            n_out[rows:, :] = jnp.zeros((EXTRA, feats), BF16)

        row = jnp.transpose(q_all[...])[:EXTRA, :]
        high = row.astype(BF16).astype(F32)
        which = lax.broadcasted_iota(jnp.int32, (EXTRA, step), 0)
        lanes = pl.ds(pl.multiple_of(i * step, step), step)
        n_out[rows:, lanes] = jnp.where(which == 0, high, jnp.where(which == 1, row - high, 0.0)).astype(BF16)

    block = pl.BlockSpec((step, feats), lambda i: (i, 0))
    extra = [] if previous is None else [previous]
    return kernel_call(
        body,
        (struct((seqs, rows, feats), BF16), struct((rows + EXTRA, feats), BF16)),
        (pl.BlockSpec((1, step, feats), lambda i: (seq, i, 0)), whole((rows + EXTRA, feats))),
        [block] * 4 + [whole((1, feats))] + [ANY] * len(extra),
        grid=(rows // step,),
        scratch=[VMEM((step, step), F32)],
        nbytes=rows * feats * 14,
        aliases={5: 0} if extra else None,
        limit=SMALL,
        name="output_rows",
    )(r1, *parts, offset, *extra)


def norm_backward(seq, seqs, v, parts, gain, base, final, previous):
    rows, feats = v.shape
    chunk = 16
    step = rows // ROW_STEPS

    def body(v_ref, k_ref, c_ref, x_ref, g, base_ref, *rest):
        if final:
            out, sums = rest[-2:]
        else:
            out, low, sums = rest[-3:]
        acc = [jnp.zeros((8, feats), F32) for _ in range(2 if final else 4)]
        for c in range(step // chunk):
            at = pl.ds(c * chunk, chunk)
            got = joined((k_ref, c_ref, x_ref), at)
            z, rstd = norm_stats(v_ref[at, :])
            w = got * g[...]
            inner = rstd * (w - jnp.mean(w, axis=-1, keepdims=True) - z * jnp.mean(w * z, axis=-1, keepdims=True))
            old = base_ref[at, :]
            new = old + inner
            if final:
                out[0, at, :] = new
            else:
                out[at, :] = new
                low[at, :] = new.astype(BF16)
            terms = [got * z, got] + ([] if final else [new, old])
            for k, term in enumerate(terms):
                acc[k] = acc[k] + jnp.sum(term.reshape(chunk // 8, 8, feats), axis=0)

        @pl.when(pl.program_id(0) == 0)
        def _():
            sums[...] = jnp.zeros_like(sums)

        for k, term in enumerate(acc):
            sums[k : k + 1, :] += jnp.sum(term, axis=0, keepdims=True)

    block = row_blocks(rows, feats)
    extra = [] if previous is None else [previous]
    seq_block = pl.BlockSpec((1, step, feats), lambda i: (seq, i, 0))
    if final:
        outs, specs = (struct((seqs, rows, feats), F32), struct((4, feats), F32)), (seq_block, whole((4, feats)))
    else:
        outs = (struct((rows, feats), F32), struct((rows, feats), BF16), struct((4, feats), F32))
        specs = (block, block, whole((4, feats)))
    return kernel_call(
        body,
        outs,
        specs,
        [block] * 4 + [whole((1, feats)), block] + [ANY] * len(extra),
        grid=(ROW_STEPS,),
        nbytes=rows * feats * 20,
        aliases={6: 0} if extra else None,
        limit=SMALL,
        name="norm_backward",
    )(v, *parts, gain, base, *extra)


def send_block(refs, rel, src, sems):
    for r, ref in enumerate(refs):

        @pl.when(rel == r)
        def _(r=r, ref=ref):
            pltpu.make_async_copy(src, ref, sems.at[r]).start()


def wait_blocks(refs, src, sems):
    for r, ref in enumerate(refs):
        pltpu.make_async_copy(src, ref, sems.at[r]).wait()


def block_at(rel, rows):
    return pl.ds(pl.multiple_of(rel * rows, rows), rows)


def lane_pair(first, second, rows):
    lanes = lax.broadcasted_iota(jnp.int32, (rows, 128), 1)
    return jnp.where(lanes == 0, first, second)


def attend_forward(seq, place, docs, vecs, blocks, wqkv, wo, previous):
    rows, feats = blocks[0].shape
    parts = len(blocks)
    length = rows * parts
    width = wqkv.shape[2]
    size = feats // HEADS
    heads = width // size
    scale = LOG2E * size ** (-0.5)

    seqs = docs.shape[0]

    def body(t_ref, doc_ref, vec, *rest):
        dr = doc_ref[seq : seq + 1, :].astype(F32)
        x_refs, (w_ref, wo_ref), rest = rest[:4], rest[4:6], rest[6:]
        p_refs, (saved, lse_out), rest = rest[-17:-13], rest[-13:-11], rest[-11:]
        xs, w, wov, qkv, att, lse, ps, in_sem, p_sem, c_sem, o_sem = rest
        t = t_ref[0]
        load_w = move(w_ref, w, in_sem.at[4])
        for r in range(parts):
            at = lax.bitwise_xor(jnp.int32(r), t)
            move(x_refs[r], xs.at[at], in_sem.at[at])
        load_wo = move(wo_ref, wov, in_sem.at[5])
        pending = []

        def project(i):
            pltpu.make_async_copy(x_refs[0], xs.at[i], in_sem.at[i]).wait()
            rel = lax.bitwise_xor(jnp.int32(i), t)
            pending.append(move(xs.at[i], saved.at[seq, block_at(rel, rows), pl.ds(0, feats)], c_sem.at[i]))
            x = xs[i]
            at = slice(i * rows, (i + 1) * rows)
            qkv[0, at, :] = (dot(x, w[0]) + vec[:, :width]).astype(BF16)
            qkv[1, at, :] = dot(x, w[1]).astype(BF16)
            qkv[2, at, :] = (dot(x, w[2]) + vec[:, width:]).astype(BF16)

        load_w.wait()
        project(0)
        load_wo.wait()
        for i in range(parts):
            if i + 1 < parts:
                project(i + 1)
            span = (i + 1) * rows
            own = slice(i * rows, span)
            same = column(dr[:, own]) == dr[:, :span]
            before = lax.broadcasted_iota(jnp.int32, (rows, span), 0) + i * rows >= lax.broadcasted_iota(
                jnp.int32, (rows, span), 1
            )
            allowed = same & before
            logs = []
            for hd in range(heads):
                cols = slice(hd * size, (hd + 1) * size)
                s = jnp.where(allowed, dot(qkv[0, own, cols], qkv[1, :span, cols], NT) * scale, NEGATIVE)
                top = jnp.max(s, axis=-1, keepdims=True)
                e = jnp.exp2(s - top)
                total = jnp.sum(e, axis=-1, keepdims=True)
                att[i, :, cols] = (dot(e.astype(BF16), qkv[2, :span, cols]) / total).astype(BF16)
                logs.append(top + jnp.log2(total))
            lse[own, :] = lane_pair(logs[0], logs[-1], rows)
            ps[i] = dot(att[i], wov[...]).astype(BF16)
            rel = lax.bitwise_xor(jnp.int32(i), t)
            send_block(p_refs, rel, ps.at[i], p_sem)
            pending.append(
                move(att.at[i], saved.at[seq, block_at(rel, rows), pl.ds(feats + 3 * width, width)], o_sem.at[i])
            )
        for c in range(3):
            pending.append(move(qkv.at[c], saved.at[seq, :, pl.ds(feats + c * width, width)], o_sem.at[parts + c]))
        pending.append(move(lse, lse_out, in_sem.at[5]))
        for copy in pending:
            copy.wait()
        wait_blocks(p_refs, ps.at[0], p_sem)

    extra = [] if previous is None else [previous]
    return kernel_call(
        body,
        (
            *[struct((rows, feats), BF16)] * 4,
            struct((2 * seqs, length, feats + 4 * width), BF16),
            struct((length, 128), F32),
        ),
        (ANY,) * 4 + (HBM,) * 2,
        [SMEM, whole(docs.shape), whole(vecs.shape)]
        + [ANY] * 4
        + [HBM] * (2 + len(extra)),
        scratch=[
            VMEM((parts, rows, feats), BF16),
            VMEM(wqkv.shape, BF16),
            VMEM(wo.shape, BF16),
            VMEM((3, length, width), BF16),
            VMEM((parts, rows, width), BF16),
            VMEM((length, 128), F32),
            VMEM((parts, rows, feats), BF16),
            DMA((6,)),
            DMA((4,)),
            DMA((4,)),
            DMA((7,)),
        ],
        flops=2 * length * feats * width * 4 + 5 * length * length * width,
        nbytes=length * feats * 8,
        trans=length * length * heads // 2,
        aliases={9: 4} if extra else None,
        name="attend_forward",
    )(place, docs, vecs, *blocks, wqkv, wo, *extra)


def attend_backward(seq, place, docs, blocks, saved, lse, wqkv, wo, previous):
    rows, feats = blocks[0].shape
    parts = len(blocks)
    length = rows * parts
    width = wqkv.shape[2]
    size = feats // HEADS
    heads = width // size
    root = size ** (-0.5)
    scale = LOG2E * root

    seqs = docs.shape[0]

    def body(t_ref, doc_ref, *rest):
        dr = doc_ref[seq : seq + 1, :].astype(F32)
        x_refs, (saved_ref, lse_ref, w_ref, wo_ref), rest = rest[:4], rest[4:8], rest[8:]
        p_refs, (out, sums), rest = rest[-20:-16], rest[-16:-14], rest[-14:]
        xs, w, wov, qkvv, attv, lsev, gk, gv, ga, low, ps, in_sem, p_sem, o_sem = rest
        t = t_ref[0]
        load_wo = move(wo_ref, wov, in_sem.at[4])
        for r in (3, 2, 1, 0):
            at = lax.bitwise_xor(jnp.int32(r), t)
            move(x_refs[r], xs.at[at], in_sem.at[at])
        loads = [move(lse_ref, lsev, in_sem.at[6])]
        for c in range(3):
            loads.append(move(saved_ref.at[seq, :, pl.ds(feats + c * width, width)], qkvv.at[c], in_sem.at[12 + c]))
        for i in range(parts):
            rel = lax.bitwise_xor(jnp.int32(i), t)
            att_ref = saved_ref.at[seq, block_at(rel, rows), pl.ds(feats + 3 * width, width)]
            loads.append(move(att_ref, attv.at[i], in_sem.at[8 + i]))
        load_w = move(w_ref, w, in_sem.at[7])
        pending = []

        def project(i):
            pltpu.make_async_copy(x_refs[0], xs.at[i], in_sem.at[i]).wait()
            rel = lax.bitwise_xor(jnp.int32(i), t)
            pending.append(move(xs.at[i], out.at[seq, block_at(rel, rows), pl.ds(0, feats)], o_sem.at[i]))
            ga[i] = dot(xs[i], wov[...], NT).astype(BF16)

        load_wo.wait()
        project(parts - 1)
        for copy in loads:
            copy.wait()
        load_w.wait()
        q_sum = jnp.zeros((1, width), F32)
        v_sum = jnp.zeros((1, width), F32)
        for i in reversed(range(parts)):
            if i:
                project(i - 1)
            span = (i + 1) * rows
            own = slice(i * rows, span)
            same = column(dr[:, own]) == dr[:, :span]
            before = lax.broadcasted_iota(jnp.int32, (rows, span), 0) + i * rows >= lax.broadcasted_iota(
                jnp.int32, (rows, span), 1
            )
            allowed = same & before
            for hd in range(heads):
                cols = slice(hd * size, (hd + 1) * size)
                q = qkvv[0, own, cols]
                k = qkvv[1, :span, cols]
                g = ga[i, :, cols]
                s = dot(q, k, NT) * scale - lsev[own, hd : hd + 1]
                p = jnp.exp2(jnp.where(allowed, s, NEGATIVE))
                gp = dot(g, qkvv[2, :span, cols], NT)
                row = jnp.sum(g.astype(F32) * attv[i, :, cols].astype(F32), axis=-1, keepdims=True)
                gs = (p * (gp - row)).astype(BF16)
                low[0, own, cols] = (dot(gs, k) * root).astype(BF16)
                new_k = dot(gs, q, TN)
                new_v = dot(p.astype(BF16), g, TN)
                if i == parts - 1:
                    gk[:span, cols] = new_k
                    gv[:span, cols] = new_v
                else:
                    gk[:span, cols] += new_k
                    gv[:span, cols] += new_v
            low[1, own, :] = (gk[own, :] * root).astype(BF16)
            low[2, own, :] = gv[own, :].astype(BF16)
            q_sum += jnp.sum(low[0, own, :].astype(F32), axis=0, keepdims=True)
            v_sum += jnp.sum(low[2, own, :].astype(F32), axis=0, keepdims=True)
            ps[i] = (
                dot(low[0, own, :], w[0], NT) + dot(low[1, own, :], w[1], NT) + dot(low[2, own, :], w[2], NT)
            ).astype(BF16)
            rel = lax.bitwise_xor(jnp.int32(i), t)
            send_block(p_refs, rel, ps.at[i], p_sem)
            for c in range(3):
                dst = out.at[seq, block_at(rel, rows), pl.ds(feats + c * width, width)]
                pending.append(move(low.at[c, own], dst, o_sem.at[4 + 3 * i + c]))
        sums[0:1, :] = q_sum
        sums[1:2, :] = v_sum
        for copy in pending:
            copy.wait()
        wait_blocks(p_refs, ps.at[0], p_sem)

    extra = [] if previous is None else [previous]
    return kernel_call(
        body,
        (
            *[struct((rows, feats), BF16)] * 4,
            struct((2 * seqs, length, feats + 4 * width), BF16),
            struct((2, width), F32),
        ),
        (ANY,) * 4 + (HBM, whole((2, width))),
        [SMEM, whole(docs.shape)] + [ANY] * 4 + [HBM] * (4 + len(extra)),
        scratch=[
            VMEM((parts, rows, feats), BF16),
            VMEM(wqkv.shape, BF16),
            VMEM(wo.shape, BF16),
            VMEM((3, length, width), BF16),
            VMEM((parts, rows, width), BF16),
            VMEM((length, 128), F32),
            VMEM((length, width), F32),
            VMEM((length, width), F32),
            VMEM((parts, rows, width), BF16),
            VMEM((3, length, width), BF16),
            VMEM((parts, rows, feats), BF16),
            DMA((15,)),
            DMA((4,)),
            DMA((16,)),
        ],
        flops=2 * length * feats * width * 4 + 10 * length * length * width,
        nbytes=length * feats * 8,
        trans=length * length * heads // 2,
        aliases={10: 4} if extra else None,
        name="attend_backward",
    )(place, docs, *blocks, saved, lse, wqkv, wo, *extra)


ORDER = (3, 1, 2, 0)


ROWS, ACT, SLOPE, GRAD = range(4)


def feed_forward(seq, seqs, blocks, vecs, w_up, w_down, previous):
    rows, feats = blocks[0].shape
    parts = len(blocks)
    length = rows * parts
    units = w_up.shape[1]
    root = math.sqrt(2.0 / math.pi)

    def body(vec, *rest):
        x_refs, (up_ref, down_ref), rest = rest[:4], rest[4:6], rest[6:]
        p_refs, saved, rest = rest[-15:-11], rest[-11], rest[-10:]
        xs, up, down, u, act, slope, ps, in_sem, p_sem, o_sem = rest
        load_up = move(up_ref, up, in_sem.at[4])
        loads = {r: move(x_refs[r], xs.at[r], in_sem.at[r]) for r in ORDER}
        load_down = move(down_ref, down, in_sem.at[5])
        pending = []

        def project(k):
            r = ORDER[k]
            loads[r].wait()
            pending.append(move(xs.at[r], saved.at[ROWS, seq, pl.ds(r * rows, rows)], o_sem.at[r]))
            u[k % 2] = dot(xs[r], up[...]) + vec[...]

        load_up.wait()
        project(0)
        load_down.wait()
        for k, r in enumerate(ORDER):
            if k + 1 < parts:
                project(k + 1)
            v = u[k % 2]
            sq = v * v
            th = jnp.tanh(v * (root + (root * 0.044715) * sq))
            half = 0.5 + 0.5 * th
            g = (v * half).astype(BF16)
            act[r] = g
            slope[r] = (half + v * (1.0 - th * th) * (0.5 * root + (1.5 * 0.044715 * root) * sq)).astype(BF16)
            ps[r] = dot(g, down[...]).astype(BF16)
            at = pl.ds(r * rows, rows)
            pending.append(move(ps.at[r], p_refs[r], p_sem.at[r]))
            pending.append(move(act.at[r], saved.at[ACT, seq, at], o_sem.at[4 + r]))
            pending.append(move(slope.at[r], saved.at[SLOPE, seq, at], o_sem.at[8 + r]))
        for copy in pending:
            copy.wait()

    extra = [] if previous is None else [previous]
    return kernel_call(
        body,
        (
            *[struct((rows, feats), BF16)] * 4,
            struct((4, seqs, length, units), BF16),
        ),
        (ANY,) * 4 + (HBM,),
        [whole(vecs.shape)] + [ANY] * 4 + [HBM] * (2 + len(extra)),
        scratch=[
            VMEM((parts, rows, feats), BF16),
            VMEM(w_up.shape, BF16),
            VMEM(w_down.shape, BF16),
            VMEM((2, rows, units), F32),
            VMEM((parts, rows, units), BF16),
            VMEM((parts, rows, units), BF16),
            VMEM((parts, rows, feats), BF16),
            DMA((6,)),
            DMA((4,)),
            DMA((12,)),
        ],
        flops=4 * length * feats * units,
        nbytes=length * feats * 14,
        trans=length * units,
        aliases={7: 4} if extra else None,
        name="feed_forward",
    )(vecs, *blocks, w_up, w_down, *extra)


def feed_backward(seq, own, got, saved, w_up, w_down, earlier):
    rows, feats = own.shape[1:]
    parts = 4
    length = rows * parts
    units = w_up.shape[1]
    seqs = saved.shape[1]

    def body(own_ref, got_ref, saved_ref, up_ref, down_ref, *rest):
        p_refs, (grad_out, sums), rest = rest[-16:-12], rest[-12:-10], rest[-10:]
        ys, up, down, slopes, u, grad, ps, in_sem, p_sem, o_sem = rest
        load_down = move(down_ref, down, in_sem.at[4])
        loads, slope_loads = {}, {}
        for r in ORDER:
            loads[r] = move((got_ref if r % 2 else own_ref).at[r // 2], ys.at[r], in_sem.at[r])
            slope_loads[r] = move(saved_ref.at[SLOPE, seq, pl.ds(r * rows, rows)], slopes.at[r], in_sem.at[6 + r])
        load_up = move(up_ref, up, in_sem.at[5])
        pending = []

        def project(k):
            r = ORDER[k]
            loads[r].wait()
            slope_loads[r].wait()
            u[k % 2] = dot(ys[r], down[...], NT)

        load_down.wait()
        project(0)
        load_up.wait()
        total = jnp.zeros((8, units), F32)
        for k, r in enumerate(ORDER):
            if k + 1 < parts:
                project(k + 1)
            gu = (u[k % 2] * slopes[r].astype(F32)).astype(BF16)
            grad[r] = gu
            total += jnp.sum(gu.astype(F32).reshape(rows // 8, 8, units), axis=0)
            ps[r] = dot(gu, up[...], NT).astype(BF16)
            pending.append(move(ps.at[r], p_refs[r], p_sem.at[r]))
            pending.append(move(grad.at[r], grad_out.at[GRAD, seq, pl.ds(r * rows, rows)], o_sem.at[4 + r]))
        sums[...] = jnp.sum(total, axis=0, keepdims=True)
        for copy in pending:
            copy.wait()

    return kernel_call(
        body,
        (
            *[struct((rows, feats), BF16)] * 4,
            struct((4, seqs, length, units), BF16),
            struct((1, units), F32),
        ),
        (ANY,) * 4 + (HBM, whole((1, units))),
        [ANY] * 2 + [HBM] * 3 + [ANY] * len(earlier),
        scratch=[
            VMEM((parts, rows, feats), BF16),
            VMEM(w_up.shape, BF16),
            VMEM(w_down.shape, BF16),
            VMEM((parts, rows, units), BF16),
            VMEM((2, rows, units), F32),
            VMEM((parts, rows, units), BF16),
            VMEM((parts, rows, feats), BF16),
            DMA((10,)),
            DMA((4,)),
            DMA((8,)),
        ],
        flops=4 * length * feats * units,
        nbytes=length * feats * 14,
        aliases={2: 4},
        name="feed_backward",
    )(own, got, saved, w_up, w_down, *earlier)


def entries(ref, seq, part, place, rows):
    at = lax.bitwise_xor(jnp.int32(part), place) * rows
    return ref[seq : seq + 1, pl.ds(pl.multiple_of(at, rows), rows)].astype(F32)


def contrast_scores(place, ends, docs, labels, units):
    rows, feats = units[0].shape[0] - EXTRA, units[0].shape[1]
    factor = CONTRAST_SCALE / feats * LOG2E
    count = len(units)
    seqs = count // 4

    def body(t_ref, end_ref, doc_ref, lab_ref, *rest):
        refs, rest = rest[:count], rest[count:]
        exp_out, col_out, row_out, loss_out, both, exps, sums, in_sem, out_sem = rest
        t = t_ref[0]
        loads = [move(refs[k].at[pl.ds(0, rows)], both.at[k], in_sem.at[k]) for k in range(count)]
        for copy in loads:
            copy.wait()
        pending = []
        for s in range(4):
            seq, part = s // 2, s % 2 * 2
            own_lab = column(entries(lab_ref, seq, part, t, rows))

            def block(k, own_doc, seq=seq, part=part, s=s, own_lab=own_lab):
                e = jnp.exp2(dot(both[seq * 4 + part], both[k], NT) * factor)
                if own_doc is not None:
                    e = jnp.where(own_doc != entries(doc_ref, seq, k % 4, t, rows), e, 0.0)
                exps[s, :, k * rows : (k + 1) * rows] = e.astype(BF16)
                picked = jnp.where(own_lab == entries(lab_ref, k // 4, k % 4, t, rows), e, 0.0)
                lanes = [slice(c * 128, (c + 1) * 128) for c in range(rows // 128)]
                fold = lambda v: functools.reduce(jnp.add, [v[:, lane] for lane in lanes])
                return fold(e), fold(picked)

            terms = [block(k, None) for k in range(count) if k // 4 != seq]
            sums[0] = functools.reduce(jnp.add, [a for a, _ in terms])
            sums[1] = functools.reduce(jnp.add, [b for _, b in terms])
            single = end_ref[seq, 0] == end_ref[seq, 1]
            inner = slice(seq * 4 * rows, (seq + 1) * 4 * rows)

            @pl.when(single)
            def _(s=s, inner=inner):
                exps[s, :, inner] = jnp.zeros((rows, 4 * rows), BF16)

            @pl.when(jnp.logical_not(single))
            def _(seq=seq, part=part, block=block):
                own_doc = column(entries(doc_ref, seq, part, t, rows))
                for k in range(seq * 4, seq * 4 + 4):
                    a, b = block(k, own_doc)
                    sums[0] += a
                    sums[1] += b

            pending.append(move(exps.at[s], exp_out.at[s], out_sem.at[s]))
            wide = lane_pair(
                jnp.sum(sums[0], axis=-1, keepdims=True), jnp.sum(sums[1], axis=-1, keepdims=True), rows
            )
            col_out[s * rows : (s + 1) * rows, :] = wide
            flat = jnp.transpose(wide)[:8, :]
            row_out[:, s * rows : (s + 1) * rows] = flat
            if part == 0:
                logs = jnp.log(flat)
                loss_out[seq : seq + 1, :] = logs[0:1] - logs[1:2]
        for copy in pending:
            copy.wait()

    return kernel_call(
        body,
        (
            struct((16, rows, count * rows), BF16),
            struct((4 * rows, 128), F32),
            struct((8, 4 * rows), F32),
            struct((seqs, rows), F32),
        ),
        (HBM, whole((4 * rows, 128)), whole((8, 4 * rows)), whole((seqs, rows))),
        [SMEM, SMEM, whole(docs.shape), whole(labels.shape)] + [ANY] * count,
        scratch=[
            VMEM((count, rows, feats), BF16),
            VMEM((4, rows, count * rows), BF16),
            VMEM((2, rows, 128), F32),
            DMA((count,)),
            DMA((4,)),
        ],
        flops=2 * 4 * rows * count * rows * feats,
        nbytes=count * rows * feats * 4,
        trans=4 * rows * count * rows,
        name="contrast_scores",
    )(place, ends, docs, labels, *units)


def contrast_grads(seq, place, ends, labels, units, exps, col_sums, row_own, row_got, cot, cot_got):
    rows, feats = units[0].shape[0] - EXTRA, units[0].shape[1]
    factor = CONTRAST_SCALE / feats
    count = len(units)
    span = 4 * rows

    def body(t_ref, end_ref, lab_ref, col, own, got, *rest):
        refs, (e_ref, cot_ref, other_ref), rest = rest[:count], rest[count : count + 3], rest[count + 3 :]
        full, low, both, exps, scales, cots, grad, gn, full_v, low_v, in_sem, e_sem, q_sem, c_sem, o_sem = rest
        t = t_ref[0]
        order = [k for k in range(count) if k // 4 != seq] + [k for k in range(count) if k // 4 == seq]
        e_loads = [move(e_ref.at[2 * seq + h], exps.at[h], e_sem.at[h]) for h in range(2)]
        loads = {
            k: move(refs[k].at[pl.ds(0, rows)], both.at[pl.ds(k * rows, rows)], in_sem.at[k]) for k in order
        }
        small = [
            (
                move(refs[seq * 4 + h * 2].at[pl.ds(rows, EXTRA)], scales.at[h], q_sem.at[h]),
                move(other_ref if h else cot_ref.at[seq], cots.at[h], c_sem.at[h]),
            )
            for h in range(2)
        ]
        single = end_ref[seq, 0] == end_ref[seq, 1]

        def weigh(h, blocks):
            s = 2 * seq + h
            own_lab = column(entries(lab_ref, seq, h * 2, t, rows))
            inv = CONTRAST_WEIGHT / col[s * rows : (s + 1) * rows, :]
            all_i, pos_i = inv[:, 0:1], inv[:, 1:2]
            for k in blocks:
                other, piece = k // 4, k % 4
                source = own if piece % 2 == 0 else got
                at = (other * 2 + piece // 2) * rows
                inv_j = CONTRAST_WEIGHT / source[0:2, at : at + rows]
                same = own_lab == entries(lab_ref, other, piece, t, rows)
                coef = (all_i + inv_j[0:1]) - jnp.where(same, pos_i + inv_j[1:2], 0.0)
                cols = slice(k * rows, (k + 1) * rows)
                grad[h, :, cols] = (exps[h, :, cols].astype(F32) * coef).astype(BF16)

        outer = slice((1 - seq) * span, (2 - seq) * span)
        inner = slice(seq * span, (seq + 1) * span)
        for h in range(2):
            e_loads[h].wait()
        weigh(0, order[:4])
        for k in order:
            loads[k].wait()
        for h in range(2):
            if h == 0:
                weigh(1, order[:4])
            gn[h] = dot(grad[h, :, outer], both[outer, :])

        @pl.when(jnp.logical_not(single))
        def _():
            for h in range(2):
                weigh(h, order[4:])
                gn[h] += dot(grad[h, :, inner], both[inner, :])

        pending = []
        for h in range(2):
            first = (seq * 4 + h * 2) * rows
            n = both[first : first + rows, :].astype(F32)
            g = gn[h] * factor
            change = g - n * jnp.mean(g * n, axis=-1, keepdims=True)
            for copy in small[h]:
                copy.wait()
            pieces = scales[h, :, :rows].astype(F32)
            gy = cots[h].astype(F32) + column(pieces[0:1] + pieces[1:2]) * change
            low_v[h] = gy.astype(BF16)
            pending.append(move(low_v.at[h], low.at[h], o_sem.at[h]))
            if h == 0:
                full_v[...] = gy
                pending.append(move(full_v, full, o_sem.at[2]))
        for copy in pending:
            copy.wait()

    return kernel_call(
        body,
        (struct((rows, feats), F32), struct((2, rows, feats), BF16)),
        (ANY,) * 2,
        [
            SMEM,
            SMEM,
            whole(labels.shape),
            whole((4 * rows, 128)),
            whole((8, 4 * rows)),
            whole((8, 4 * rows)),
        ]
        + [ANY] * count
        + [HBM] * 2
        + [ANY],
        scratch=[
            VMEM((count * rows, feats), BF16),
            VMEM((2, rows, count * rows), BF16),
            VMEM((2, EXTRA, feats), BF16),
            VMEM((2, rows, feats), BF16),
            VMEM((2, rows, count * rows), BF16),
            VMEM((2, rows, feats), F32),
            VMEM((rows, feats), F32),
            VMEM((2, rows, feats), BF16),
            DMA((count,)),
            DMA((2,)),
            DMA((2,)),
            DMA((2,)),
            DMA((3,)),
        ],
        flops=4 * rows * count * rows * feats,
        nbytes=count * rows * feats * 4,
        name="contrast_grads",
    )(place, ends, labels, col_sums, row_own, row_got, *units, exps, cot, cot_got)


def down_grad(saved, own, got):
    seqs, length, units = saved.shape[1:]
    rows, feats = own[0].shape[1:]
    tiles = units // TILE

    def body(a_ref, *rest):
        own_refs, got_refs = rest[:seqs], rest[seqs : 2 * seqs]
        out_ref, a, b, out, a_sem, b_sem, o_sem = rest[2 * seqs :]
        b_loads = []
        for s in range(seqs):
            for r in range(4):
                src = (got_refs if r % 2 else own_refs)[s].at[r // 2]
                b_loads.append(move(src, b.at[s, pl.ds(r * rows, rows)], b_sem.at[4 * s + r]))
        columns = [pl.ds(i * TILE, TILE) for i in range(tiles)]
        a_loads = [move(a_ref.at[ACT, :, :, columns[i]], a.at[i], a_sem.at[i]) for i in range(tiles)]
        for copy in b_loads:
            copy.wait()
        stores = []
        for i in range(tiles):
            a_loads[i].wait()
            out[i] = functools.reduce(jnp.add, [dot(a[i, s], b[s], TN) for s in range(seqs)]).astype(BF16)
            stores.append(move(out.at[i], out_ref.at[columns[i]], o_sem.at[i]))
        for copy in stores:
            copy.wait()

    return kernel_call(
        body,
        struct((units, feats), BF16),
        ANY,
        [HBM] + [ANY] * (2 * seqs),
        scratch=[
            VMEM((tiles, seqs, length, TILE), BF16),
            VMEM((seqs, length, feats), BF16),
            VMEM((tiles, TILE, feats), BF16),
            DMA((tiles,)),
            DMA((4 * seqs,)),
            DMA((tiles,)),
        ],
        flops=2 * seqs * length * units * feats,
        nbytes=4 * seqs * length * feats,
        name="down_grad",
    )(saved, *own, *got)


TILE = 256


def send_half(tile, tiles, high, src, to_other, kept, at, sem):
    upper = tile >= tiles // 2
    rows = pl.ds((tile % (tiles // 2)) * TILE, TILE)

    @pl.when(high == int(upper))
    def _():
        pltpu.make_async_copy(src, kept.at[rows, at], sem).start()

    @pl.when(high != int(upper))
    def _():
        pltpu.make_async_copy(src, to_other.at[rows, at], sem).start()

    return pltpu.make_async_copy(src, kept.at[rows, at], sem)


def weight_grad(saved, flags, bit):
    seqs, length, out_rows = saved.shape[1:]
    cols = out_rows
    tiles = out_rows // TILE

    def body(flag, s_ref, other_ref, kept_ref, a, b, out, a_sem, b_sem, o_sem):
        b_loads = [move(s_ref.at[GRAD, s], b.at[s], b_sem.at[s]) for s in range(seqs)]
        columns = [pl.ds(i * TILE, TILE) for i in range(tiles)]
        a_loads = [move(s_ref.at[ROWS, :, :, columns[i]], a.at[i], a_sem.at[i]) for i in range(tiles)]
        for copy in b_loads:
            copy.wait()
        stores = []
        for i in range(tiles):
            a_loads[i].wait()
            out[i] = functools.reduce(jnp.add, [dot(a[i, s], b[s], TN) for s in range(seqs)]).astype(BF16)
            stores.append(
                send_half(i, tiles, flag[bit], out.at[i], other_ref, kept_ref, pl.ds(0, cols), o_sem.at[i])
            )
        for copy in stores:
            copy.wait()

    return kernel_call(
        body,
        (struct((out_rows // 2, cols), BF16),) * 2,
        (ANY,) * 2,
        [pl.BlockSpec(memory_space=pltpu.SMEM)] + [HBM],
        scratch=[
            VMEM((tiles, seqs, length, TILE), BF16),
            VMEM((seqs, length, cols), BF16),
            VMEM((tiles, TILE, cols), BF16),
            DMA((tiles,)),
            DMA((seqs,)),
            DMA((tiles,)),
        ],
        flops=2 * seqs * length * out_rows * cols,
        nbytes=4 * seqs * length * cols,
        name="weight_grad",
    )(flags, saved)


def head_grads(saved, grads, seqs, feats, flags, bits):
    length = saved.shape[1]
    width = (saved.shape[2] - feats) // 4
    tiles = feats // width

    def body(*refs):
        flag, s_ref, h_ref = refs[:3]
        first_refs, second_refs = refs[3:5], refs[5:7]
        a, g, r, first, second, a_sem, g_sem, r_sem, o_sem = refs[7:]
        both = pl.ds(0, seqs)
        columns = [pl.ds(i * width, width) for i in range(tiles)]
        g_loads = []
        for n, ref in enumerate((h_ref, h_ref, h_ref, s_ref)):
            g_loads.append(move(ref.at[both, :, pl.ds(feats + n * width, width)], g.at[n], g_sem.at[n]))
        a_loads, r_loads = [], []
        for i in range(tiles):
            a_loads.append(move(s_ref.at[both, :, columns[i]], a.at[i], a_sem.at[i]))
            r_loads.append(move(h_ref.at[both, :, columns[i]], r.at[i], r_sem.at[i]))
        for copy in g_loads:
            copy.wait()

        def total(x, y):
            return functools.reduce(jnp.add, [dot(x[s], y[s], TN) for s in range(seqs)]).astype(BF16)

        stores = []
        for i in range(tiles):
            a_loads[i].wait()
            first[i, :, :width] = total(a[i], g[0])
            first[i, :, width:] = total(a[i], g[1])
            second[i, :, :width] = total(a[i], g[2])
            r_loads[i].wait()
            second[i, :, width:] = total(g[3], r[i])
            for n, (src, outs) in enumerate(((first, first_refs), (second, second_refs))):
                stores.append(
                    send_half(i, tiles, flag[bits[n]], src.at[i], *outs, pl.ds(0, 2 * width), o_sem.at[2 * i + n])
                )
        for copy in stores:
            copy.wait()

    return kernel_call(
        body,
        (struct((feats // 2, 2 * width), BF16),) * 4,
        (ANY,) * 4,
        [pl.BlockSpec(memory_space=pltpu.SMEM)] + [HBM] * 2,
        scratch=[
            VMEM((tiles, seqs, length, width), BF16),
            VMEM((4, seqs, length, width), BF16),
            VMEM((tiles, seqs, length, width), BF16),
            VMEM((tiles, width, 2 * width), BF16),
            VMEM((tiles, width, 2 * width), BF16),
            DMA((tiles,)),
            DMA((4,)),
            DMA((tiles,)),
            DMA((2 * tiles,)),
        ],
        flops=2 * seqs * length * feats * width * 4,
        nbytes=4 * seqs * length * feats,
        name="head_grads",
    )(flags, saved, grads)


def halve_step(flags, bit, keep, got):
    rows, cols = keep.shape
    half = rows // 2

    def body(flag, k_ref, g_ref, *outs):
        if bit is None:
            outs[0][...] = (k_ref[...].astype(F32) + g_ref[...].astype(F32)).astype(BF16)
            return
        for high in (0, 1):

            @pl.when(flag[bit] == high)
            def _(high=high):
                for out, upper in ((outs[0], 1 - high), (outs[1], high)):
                    at = slice(upper * half, (upper + 1) * half)
                    out[...] = (k_ref[at, :].astype(F32) + g_ref[at, :].astype(F32)).astype(BF16)

    shape = (rows, cols) if bit is None else (half, cols)
    return kernel_call(
        body,
        (struct(shape, BF16),) * (1 if bit is None else 2),
        (whole(shape),) * (1 if bit is None else 2),
        [pl.BlockSpec(memory_space=pltpu.SMEM)] + [whole((rows, cols))] * 2,
        nbytes=rows * cols * 6,
        limit=SMALL,
        name="halve_step",
    )(flags, keep, got)


def join_step(flags, bit, own, got, dtype):
    rows, cols = own.shape
    steps = 2 if dtype == F32 else 1
    part = rows // steps

    def body(flag, own_ref, got_ref, out):
        for high in (0, 1):

            @pl.when(flag[bit] == high)
            def _(high=high):
                out[high] = own_ref[...].astype(dtype)
                out[1 - high] = got_ref[...].astype(dtype)

    block = pl.BlockSpec((part, cols), lambda i: (i, 0))
    return kernel_call(
        body,
        struct((2, rows, cols), dtype),
        pl.BlockSpec((2, part, cols), lambda i: (0, i, 0)),
        [pl.BlockSpec(memory_space=pltpu.SMEM), block, block],
        grid=(steps,),
        nbytes=rows * cols * 8,
        limit=SMALL,
        name="join_step",
    )(flags, own, got).reshape(2 * rows, cols)


def part_outputs(parts, order):
    rows, cols = parts.shape
    step = rows >> len(order)

    def place(i):
        return functools.reduce(
            jnp.add, [((i >> bit) & 1) << (len(order) - 1 - n) for n, bit in enumerate(order)]
        )

    def body(part, out):
        out[...] = part[...].astype(F32)

    return kernel_call(
        body,
        struct((rows, cols), F32),
        pl.BlockSpec((step, cols), lambda i: (place(i), 0)),
        [pl.BlockSpec((step, cols), lambda i: (i, 0))],
        grid=(1 << len(order),),
        nbytes=6 * rows * cols,
        limit=SMALL,
        name="part_outputs",
    )(parts)


def head_outputs(flags, bits, first, second):
    feats = 2 * first[0].shape[0]
    width = first[0].shape[1] // 2
    tile = width

    def body(h_ref, a_ref, b_ref, c_ref, d_ref, qkv, out):
        mine = (lax.div(pl.program_id(0) * tile, feats // 2) == h_ref[bits[0]])

        for case, x in ((True, a_ref), (False, b_ref)):
            @pl.when(mine == case)
            def _(x=x):
                qkv[0] = x[:, :width].astype(F32)
                qkv[1] = x[:, width:].astype(F32)

        mine_two = (lax.div(pl.program_id(0) * tile, feats // 2) == h_ref[bits[1]])
        for case, y in ((True, c_ref), (False, d_ref)):
            @pl.when(mine_two == case)
            def _(y=y):
                qkv[2] = y[:, :width].astype(F32)
                out[...] = y[:, width:].astype(F32)

    half = pl.BlockSpec((tile, 2 * width), lambda i, h: (lax.rem(i, feats // 2 // tile), 0))
    return kernel_call(
        body,
        (struct((3, feats, width), F32), struct((width, feats), F32)),
        (pl.BlockSpec((3, tile, width), lambda i, h: (0, i, 0)), pl.BlockSpec((width, tile), lambda i, h: (0, i))),
        [half] * 4,
        grid=(feats // tile,),
        nbytes=10 * feats * width * 4,
        prefetch=1,
        limit=SMALL,
        name="head_outputs",
    )(flags, *first, *second)


def swap(value, axis, size, bit):
    return lax.ppermute(value, axis, [(i, i ^ bit) for i in range(size)])


CORE, CROSS = 1, 2


def tensor_swap(value, bit):
    return swap(value, "tensor", 4, bit)


def tie(value, *earlier):
    return lax.optimization_barrier((value, *earlier))[0] if earlier else value


class Gather:
    def __init__(self, value):
        self.value = value
        self.cross = tensor_swap(value, CROSS)
        self.core = tensor_swap(value, CORE)

    def blocks(self, *earlier):
        return [self.value, self.core, self.cross, tensor_swap(tie(self.cross, *earlier), CORE)]


class Scatter:
    def __init__(self, blocks):
        self.own, self.other = blocks[0], blocks[2]
        self.core_other = tensor_swap(blocks[3], CORE)
        self.core_own = tensor_swap(blocks[1], CORE)
        self.mark = blocks[3]

    def cross(self, *earlier):
        block = (tie(self.other, *earlier).astype(F32) + self.core_other.astype(F32)).astype(BF16)
        self.parts = (self.own, self.core_own, tensor_swap(block, CROSS))
        return block


class DpSum:
    def __init__(self, send, keep, flags, size, order):
        self.send, self.value, self.flags, self.size = send, keep, flags, size
        self.left = [(bit, True) for bit in order] + [(bit, False) for bit in reversed(order)]
        self.got, self.now = None, None

    def advance(self, *earlier):
        if self.now is not None and self.now[1]:
            more = self.left and self.left[0][1]
            parts = halve_step(self.flags, self.left[0][0] if more else None, tie(self.value, *earlier), self.got)
            self.send, self.value = parts if more else (parts[0], parts[0])
        elif self.now is not None:
            self.send = self.value = join_step(self.flags, self.now[0], tie(self.value, *earlier), self.got, BF16)
        self.now = self.left.pop(0)
        self.got = swap(self.send, "dp", self.size, 1 << self.now[0])
        return self.send

    def halves(self):
        return self.value, self.got


def shards(
    dp_size,
    tokens,
    doc_ids,
    targets,
    cotangent,
    ln1_gain,
    ln1_bias,
    qkv_weight,
    query_bias,
    value_bias,
    output_weight,
    out_bias,
    ln2_gain,
    ln2_bias,
    up_weight,
    up_bias,
    down_weight,
    down_bias,
):
    seqs, rows, feats = tokens.shape
    length = doc_ids.shape[1]
    parts = length // rows
    me = lax.axis_index("tensor")
    place = me.reshape(1).astype(jnp.int32)
    vec = lambda v: v.astype(F32).reshape(1, -1)
    gain_one, shift_one, gain_two, shift_two = vec(ln1_gain), vec(ln1_bias), vec(ln2_gain), vec(ln2_bias)
    out_offset, down_offset, up_shift = vec(out_bias), vec(down_bias), vec(up_bias)
    head_shift = vec(jnp.concatenate([query_bias, value_bias]))
    ends = doc_ids[:, :: length - 1]

    fine = 16
    paired = (jnp.arange(feats, dtype=jnp.int32) // 2).astype(F32)
    freq = jnp.exp(paired * (-2.0 * math.log(10000.0) / feats))[None, :]
    odd = (jnp.arange(feats, dtype=jnp.int32) % 2 == 1)[None, :]
    coarse_at = (me * rows + fine * jnp.arange(rows // fine, dtype=jnp.int32)).astype(F32)[:, None] * freq
    fine_at = jnp.arange(fine, dtype=jnp.int32).astype(F32)[:, None] * freq
    sin_a, cos_a = jnp.sin(coarse_at), jnp.cos(coarse_at)
    tables = (jnp.where(odd, cos_a, sin_a), jnp.where(odd, -sin_a, cos_a), jnp.cos(fine_at), jnp.sin(fine_at))

    hidden, stream, grad_r = [None] * 2, [None] * 2, [None] * 2
    kept, up_sums, head_sums, sums_one, sums_two = [None] * 2, [None] * 2, [None] * 2, [None] * 2, [None] * 2
    shared = {"attend": None, "feed": None, "act": None, "heads": None, "input": None}

    def attend(s, gathered, *earlier):
        *blocks, shared["attend"], kept[s] = attend_forward(
            s, tie(place, *earlier), doc_ids, head_shift, gathered, qkv_weight, output_weight, shared["attend"]
        )
        return Scatter(blocks)

    def middle_rows(s, scatter, *earlier):
        stream[s], normed = second_norm(hidden[s], scatter.parts, tie(out_offset, *earlier), gain_two, shift_two)
        return normed, Gather(normed)

    def feed(s, gathered, *earlier):
        *blocks, shared["feed"] = feed_forward(
            s, seqs, gathered, tie(up_shift, *earlier), up_weight, down_weight, shared["feed"]
        )
        return Scatter(blocks)

    def last_rows(s, scatter, *earlier):
        shared["act"], unit = output_rows(
            s, seqs, stream[s], scatter.parts, tie(down_offset, *earlier), shared["act"]
        )
        return unit, Gather(unit)

    hidden[0], normed_a = first_norm(0, tokens, tables, gain_one, shift_one)
    rows_a = Gather(normed_a)
    hidden[1], normed_b = first_norm(1, tie(tokens, normed_a), tables, gain_one, shift_one)
    rows_b = Gather(normed_b)
    at_a = attend(0, rows_a.blocks(normed_b))
    block = at_a.cross(rows_b.cross)
    at_b = attend(1, rows_b.blocks(), block)
    normed, rows_a = middle_rows(0, at_a, at_b.mark)
    block = at_b.cross(normed)
    ff_a = feed(0, rows_a.blocks(), block)
    normed, rows_b = middle_rows(1, at_b, ff_a.mark)
    block = ff_a.cross(normed)
    ff_b = feed(1, rows_b.blocks(), block)
    unit, units_a = last_rows(0, ff_a, ff_b.mark)
    block = ff_b.cross(unit)
    unit, units_b = last_rows(1, ff_b, block)
    cots = [tensor_swap(tie(cotangent[s], unit), CROSS) for s in range(2)]

    units = units_a.blocks() + units_b.blocks()
    exps, col_sums, row_sums, loss = contrast_scores(place, ends, doc_ids, targets, units)
    row_got = tensor_swap(row_sums, CORE)
    grad_y, low_y, got_y = [None] * 2, [None] * 2, [None] * 2
    for s in range(2):
        grad_y[s], low_y[s] = contrast_grads(
            s, tie(place, *low_y[:s]), ends, targets, units, exps, col_sums, row_sums, row_got, cotangent, cots[s]
        )
        got_y[s] = tensor_swap(tie(low_y[s], cots[1]), CORE)

    def feed_back(s, *earlier):
        *blocks, shared["feed"], up_sums[s] = feed_backward(
            s, low_y[s], got_y[s], shared["feed"], up_weight, down_weight, earlier
        )
        return Scatter(blocks)

    def middle_back(s, scatter, *earlier):
        grad_r[s], low, sums_two[s] = norm_backward(
            s, seqs, stream[s], scatter.parts, tie(gain_two, *earlier), grad_y[s], False, None
        )
        return low, Gather(low)

    def attend_back(s, gathered, *earlier):
        *blocks, shared["heads"], head_sums[s] = attend_backward(
            s, tie(place, *earlier), doc_ids, gathered, shared["attend"], kept[s], qkv_weight, output_weight,
            shared["heads"],
        )
        return Scatter(blocks)

    def first_back(s, scatter, *earlier):
        shared["input"], sums_one[s] = norm_backward(
            s, seqs, hidden[s], scatter.parts, tie(gain_one, *earlier), grad_r[s], True, shared["input"]
        )
        return sums_one[s]

    bits = list(range(dp_size.bit_length() - 1))
    other_bits = bits[1::-1] + bits[2:]
    flags = (lax.axis_index("dp") >> jnp.arange(len(bits), dtype=jnp.int32)) & 1
    grad_down_w = down_grad(shared["feed"], low_y, got_y)
    down_part = lax.psum_scatter(grad_down_w, "dp", scatter_dimension=0, tiled=True)
    fb_a = feed_back(0, grad_down_w)
    fb_b = feed_back(1, fb_a.cross())
    low, rows_a = middle_back(0, fb_a, fb_b.mark)
    block = fb_b.cross(low)
    up_sum = DpSum(*weight_grad(tie(shared["feed"], block), flags, bits[0]), flags, dp_size, bits)
    sent = up_sum.advance()
    ab_a = attend_back(0, rows_a.blocks(sent), sent)
    low, rows_b = middle_back(1, fb_b, ab_a.mark)
    block = ab_a.cross(low)
    sent = up_sum.advance(block, rows_b.cross)
    ab_b = attend_back(1, rows_b.blocks(sent), sent, down_part)
    down_all = lax.all_gather(tie(down_part, sent), "dp", axis=0, tiled=True)
    sent = up_sum.advance(ab_b.mark)
    sums = first_back(0, ab_a, sent)
    block = ab_b.cross(sums)
    first_send, first_keep, second_send, second_keep = head_grads(
        tie(shared["attend"], block), shared["heads"], seqs, feats, flags, (bits[0], other_bits[0])
    )
    first = DpSum(first_send, first_keep, flags, dp_size, bits)
    second = DpSum(second_send, second_keep, flags, dp_size, other_bits)
    sent = (first.advance(), second.advance())
    sent = up_sum.advance(*sent)
    sums = first_back(1, ab_b, sent)
    sent = (sums,)

    total = lambda items: functools.reduce(jnp.add, items)
    heads_sum = total(head_sums)
    heads_row = jnp.pad(heads_sum.reshape(1, -1), ((0, 0), (0, feats - heads_sum.size)))
    small = jnp.concatenate([total(sums_one)[:2], total(sums_two), total(up_sums), heads_row])
    swaps = [("dp", dp_size, 1 << bit) for bit in bits] + [("tensor", 4, CORE), ("tensor", 4, CROSS)]
    local = None
    axis, size, bit = swaps.pop(0)
    arriving = swap(small, axis, size, bit)
    sent = ()
    while first.left or arriving is not None or up_sum.left:
        if first.left:
            sent = (first.advance(*sent),)
            sent = (second.advance(*sent),)
        if len(first.left) == 2:
            grad_down_w = tie(down_all, *sent).astype(F32)
            sent += (grad_down_w,)
        small = tie(small, *sent)
        if arriving is not None:
            small = small + arriving
        arriving = None
        if swaps:
            axis, size, bit = swaps.pop(0)
            if axis == "tensor" and local is None:
                local, small = small[6:], small[:6]
            arriving = swap(small, axis, size, bit)
        sent = (small,)
        if up_sum.left:
            sent += (up_sum.advance(*sent),)
    own, got = up_sum.halves()
    grad_up_w = join_step(flags, bits[0], tie(own, *sent), got, F32)
    own, got = first.halves()
    grad_qkv_w, grad_out_w = head_outputs(
        flags, (bits[0], other_bits[0]), (tie(own, grad_up_w), got), second.halves()
    )
    return (
        shared["act"],
        loss,
        shared["input"],
        small[0],
        small[1],
        grad_qkv_w,
        local[1, : heads_sum.shape[1]],
        local[1, heads_sum.shape[1] : 2 * heads_sum.shape[1]],
        grad_out_w,
        small[4],
        small[2],
        small[3],
        grad_up_w,
        local[0],
        grad_down_w,
        small[5],
    )


def solution(mesh):
    in_specs = (
        P("dp", "tensor", None),
        P("dp", None),
        P("dp", None),
        P("dp", "tensor", None),
        P(),
        P(),
        P(None, None, "tensor"),
        P("tensor"),
        P("tensor"),
        P("tensor", None),
        P(),
        P(),
        P(),
        P(None, "tensor"),
        P("tensor"),
        P("tensor", None),
        P(),
    )
    out_specs = (
        P("dp", "tensor", None),
        P("dp", "tensor"),
        P("dp", "tensor", None),
        P(),
        P(),
        P(None, None, "tensor"),
        P("tensor"),
        P("tensor"),
        P("tensor", None),
        P(),
        P(),
        P(),
        P(None, "tensor"),
        P("tensor"),
        P("tensor", None),
        P(),
    )
    return jax.shard_map(
        functools.partial(shards, mesh.shape["dp"]),
        mesh=mesh,
        in_specs=in_specs,
        out_specs=out_specs,
        check_vma=False,
    )
```

```python
import functools
import math

import jax
import jax.numpy as jnp
from jax import lax
from jax.experimental import pallas as pl
from jax.experimental.pallas import tpu as pltpu
from jax.sharding import PartitionSpec as P

HEADS = 8
NORM_EPS = 1e-05
CONTRAST_SCALE = 32.0
CONTRAST_WEIGHT = 64.0
NEGATIVE = -1e30
LOG2E = math.log2(math.e)
F32 = jnp.float32
BF16 = jnp.bfloat16
MIB = 1 << 20
LIMIT, SMALL = 52, 14
COST = 0.02
NN = (((1,), (0,)), ((), ()))
NT = (((1,), (1,)), ((), ()))
TN = (((0,), (0,)), ((), ()))
VMEM = pltpu.VMEM


def dot(a, b, dims=NN):
    return lax.dot_general(a, b, dims, preferred_element_type=F32)


def whole(shape):
    return pl.BlockSpec(shape, lambda *_: (0,) * len(shape))


def kernel_call(body, outs, out_specs, in_specs, grid=(1,), scratch=(), flops=0, nbytes=0, trans=0,
                limit=LIMIT, aliases=None, prefetch=0, name=None):
    return pl.pallas_call(
        body,
        out_shape=outs,
        grid_spec=pltpu.PrefetchScalarGridSpec(
            num_scalar_prefetch=prefetch,
            grid=grid,
            in_specs=in_specs,
            out_specs=out_specs,
            scratch_shapes=scratch,
        ),
        name=name,
        input_output_aliases=aliases or {},
        cost_estimate=pl.CostEstimate(
            flops=int(flops * COST), bytes_accessed=int(nbytes * COST), transcendentals=int(trans * COST)
        ),
        compiler_params=pltpu.CompilerParams(vmem_limit_bytes=limit * MIB),
    )


def struct(shape, dtype):
    return jax.ShapeDtypeStruct(shape, dtype)


ANY = pl.BlockSpec(memory_space=pl.ANY)
HBM = pl.BlockSpec(memory_space=pltpu.HBM)
SMEM = pl.BlockSpec(memory_space=pltpu.SMEM)
DMA = pltpu.SemaphoreType.DMA


def move(src, dst, sem):
    copy = pltpu.make_async_copy(src, dst, sem)
    copy.start()
    return copy


def column(row):
    return jnp.transpose(jnp.broadcast_to(row, (8, row.shape[1])))[:, :1]


def norm_stats(v):
    centered = v - jnp.mean(v, axis=-1, keepdims=True)
    rstd = lax.rsqrt(jnp.mean(centered * centered, axis=-1, keepdims=True) + NORM_EPS)
    return centered * rstd, rstd


ROW_STEPS = 4


def row_blocks(rows, cols):
    return pl.BlockSpec((rows // ROW_STEPS, cols), lambda i: (i, 0))


def first_norm(seq, tokens, tables, gain, shift):
    rows, feats = tokens.shape[1:]
    fine = tables[2].shape[0]
    step = rows // ROW_STEPS

    def body(tok, pa, qa, cb, sb, g, b, h_out, a_out):
        i = pl.program_id(0)
        for c in range(step // fine):
            at = pl.ds(c * fine, fine)
            row = pl.ds(i * (step // fine) + c, 1)
            pos = pa[row, :] * cb[...] + qa[row, :] * sb[...]
            h = tok[0, at, :].astype(F32) + pos
            h_out[at, :] = h
            z, _ = norm_stats(h)
            a_out[at, :] = (z * g[...] + b[...]).astype(BF16)

    return kernel_call(
        body,
        (struct((rows, feats), F32), struct((rows, feats), BF16)),
        (row_blocks(rows, feats), row_blocks(rows, feats)),
        [pl.BlockSpec((1, step, feats), lambda i: (seq, i, 0))]
        + [whole(t.shape) for t in tables]
        + [whole((1, feats))] * 2,
        grid=(ROW_STEPS,),
        nbytes=rows * feats * 8,
        limit=SMALL,
        name="first_norm",
    )(tokens, *tables, gain, shift)


def joined(parts, at):
    return functools.reduce(jnp.add, [p[at, :].astype(F32) for p in parts])


def second_norm(h, parts, offset, gain, shift):
    rows, feats = h.shape
    chunk = 32
    step = rows // ROW_STEPS

    def body(h_ref, k_ref, c_ref, x_ref, o_ref, g, b, r_out, n_out):
        for c in range(step // chunk):
            at = pl.ds(c * chunk, chunk)
            r = h_ref[at, :] + joined((k_ref, c_ref, x_ref), at) + o_ref[...]
            r_out[at, :] = r
            z, _ = norm_stats(r)
            n_out[at, :] = (z * g[...] + b[...]).astype(BF16)

    block = row_blocks(rows, feats)
    return kernel_call(
        body,
        (struct((rows, feats), F32), struct((rows, feats), BF16)),
        (block, block),
        [block] * 4 + [whole((1, feats))] * 3,
        grid=(ROW_STEPS,),
        nbytes=rows * feats * 16,
        limit=SMALL,
        name="second_norm",
    )(h, *parts, offset, gain, shift)


EXTRA = 16


def output_rows(seq, seqs, r1, parts, offset, previous):
    rows, feats = r1.shape
    step, chunk = 128, 32

    def body(r_ref, k_ref, c_ref, x_ref, o_ref, *rest):
        act_out, n_out, q_all = rest[-3:]
        i = pl.program_id(0)
        for c in range(step // chunk):
            at = pl.ds(c * chunk, chunk)
            y = r_ref[at, :] + joined((k_ref, c_ref, x_ref), at) + o_ref[...]
            act_out[0, at, :] = y.astype(BF16)
            q = lax.rsqrt(jnp.mean(y * y, axis=-1, keepdims=True) + NORM_EPS)
            n_out[pl.ds(pl.multiple_of(i * step + c * chunk, chunk), chunk), :] = (y * q).astype(BF16)
            q_all[at, :] = jnp.broadcast_to(q, (chunk, step))

        @pl.when(i == 0)
        def _():
            n_out[rows:, :] = jnp.zeros((EXTRA, feats), BF16)

        row = jnp.transpose(q_all[...])[:EXTRA, :]
        high = row.astype(BF16).astype(F32)
        which = lax.broadcasted_iota(jnp.int32, (EXTRA, step), 0)
        lanes = pl.ds(pl.multiple_of(i * step, step), step)
        n_out[rows:, lanes] = jnp.where(which == 0, high, jnp.where(which == 1, row - high, 0.0)).astype(BF16)

    block = pl.BlockSpec((step, feats), lambda i: (i, 0))
    extra = [] if previous is None else [previous]
    return kernel_call(
        body,
        (struct((seqs, rows, feats), BF16), struct((rows + EXTRA, feats), BF16)),
        (pl.BlockSpec((1, step, feats), lambda i: (seq, i, 0)), whole((rows + EXTRA, feats))),
        [block] * 4 + [whole((1, feats))] + [ANY] * len(extra),
        grid=(rows // step,),
        scratch=[VMEM((step, step), F32)],
        nbytes=rows * feats * 14,
        aliases={5: 0} if extra else None,
        limit=SMALL,
        name="output_rows",
    )(r1, *parts, offset, *extra)


def norm_backward(seq, seqs, v, parts, gain, base, final, previous):
    rows, feats = v.shape
    chunk = 16
    step = rows // ROW_STEPS

    def body(v_ref, k_ref, c_ref, x_ref, g, base_ref, *rest):
        if final:
            out, sums = rest[-2:]
        else:
            out, low, sums = rest[-3:]
        acc = [jnp.zeros((8, feats), F32) for _ in range(2 if final else 4)]
        for c in range(step // chunk):
            at = pl.ds(c * chunk, chunk)
            got = joined((k_ref, c_ref, x_ref), at)
            z, rstd = norm_stats(v_ref[at, :])
            w = got * g[...]
            inner = rstd * (w - jnp.mean(w, axis=-1, keepdims=True) - z * jnp.mean(w * z, axis=-1, keepdims=True))
            old = base_ref[at, :]
            new = old + inner
            if final:
                out[0, at, :] = new
            else:
                out[at, :] = new
                low[at, :] = new.astype(BF16)
            terms = [got * z, got] + ([] if final else [new, old])
            for k, term in enumerate(terms):
                acc[k] = acc[k] + jnp.sum(term.reshape(chunk // 8, 8, feats), axis=0)

        @pl.when(pl.program_id(0) == 0)
        def _():
            sums[...] = jnp.zeros_like(sums)

        for k, term in enumerate(acc):
            sums[k : k + 1, :] += jnp.sum(term, axis=0, keepdims=True)

    block = row_blocks(rows, feats)
    extra = [] if previous is None else [previous]
    seq_block = pl.BlockSpec((1, step, feats), lambda i: (seq, i, 0))
    if final:
        outs, specs = (struct((seqs, rows, feats), F32), struct((4, feats), F32)), (seq_block, whole((4, feats)))
    else:
        outs = (struct((rows, feats), F32), struct((rows, feats), BF16), struct((4, feats), F32))
        specs = (block, block, whole((4, feats)))
    return kernel_call(
        body,
        outs,
        specs,
        [block] * 4 + [whole((1, feats)), block] + [ANY] * len(extra),
        grid=(ROW_STEPS,),
        nbytes=rows * feats * 20,
        aliases={6: 0} if extra else None,
        limit=SMALL,
        name="norm_backward",
    )(v, *parts, gain, base, *extra)


def send_block(refs, rel, src, sems):
    for r, ref in enumerate(refs):

        @pl.when(rel == r)
        def _(r=r, ref=ref):
            pltpu.make_async_copy(src, ref, sems.at[r]).start()


def wait_blocks(refs, src, sems):
    for r, ref in enumerate(refs):
        pltpu.make_async_copy(src, ref, sems.at[r]).wait()


def block_at(rel, rows):
    return pl.ds(pl.multiple_of(rel * rows, rows), rows)


def lane_pair(first, second, rows):
    lanes = lax.broadcasted_iota(jnp.int32, (rows, 128), 1)
    return jnp.where(lanes == 0, first, second)


def attend_forward(seq, place, docs, vecs, blocks, wqkv, wo, previous):
    rows, feats = blocks[0].shape
    parts = len(blocks)
    length = rows * parts
    width = wqkv.shape[2]
    size = feats // HEADS
    heads = width // size
    scale = LOG2E * size ** (-0.5)

    seqs = docs.shape[0]

    def body(t_ref, doc_ref, vec, *rest):
        dr = doc_ref[seq : seq + 1, :].astype(F32)
        x_refs, (w_ref, wo_ref), rest = rest[:4], rest[4:6], rest[6:]
        p_refs, (saved, lse_out), rest = rest[-17:-13], rest[-13:-11], rest[-11:]
        xs, w, wov, qkv, att, lse, ps, in_sem, p_sem, c_sem, o_sem = rest
        t = t_ref[0]
        load_w = move(w_ref, w, in_sem.at[4])
        for r in range(parts):
            at = lax.bitwise_xor(jnp.int32(r), t)
            move(x_refs[r], xs.at[at], in_sem.at[at])
        load_wo = move(wo_ref, wov, in_sem.at[5])
        pending = []

        def project(i):
            pltpu.make_async_copy(x_refs[0], xs.at[i], in_sem.at[i]).wait()
            rel = lax.bitwise_xor(jnp.int32(i), t)
            pending.append(move(xs.at[i], saved.at[seq, block_at(rel, rows), pl.ds(0, feats)], c_sem.at[i]))
            x = xs[i]
            at = slice(i * rows, (i + 1) * rows)
            qkv[0, at, :] = (dot(x, w[0]) + vec[:, :width]).astype(BF16)
            qkv[1, at, :] = dot(x, w[1]).astype(BF16)
            qkv[2, at, :] = (dot(x, w[2]) + vec[:, width:]).astype(BF16)

        load_w.wait()
        project(0)
        load_wo.wait()
        for i in range(parts):
            if i + 1 < parts:
                project(i + 1)
            span = (i + 1) * rows
            own = slice(i * rows, span)
            same = column(dr[:, own]) == dr[:, :span]
            before = lax.broadcasted_iota(jnp.int32, (rows, span), 0) + i * rows >= lax.broadcasted_iota(
                jnp.int32, (rows, span), 1
            )
            allowed = same & before
            logs = []
            for hd in range(heads):
                cols = slice(hd * size, (hd + 1) * size)
                s = jnp.where(allowed, dot(qkv[0, own, cols], qkv[1, :span, cols], NT) * scale, NEGATIVE)
                top = jnp.max(s, axis=-1, keepdims=True)
                e = jnp.exp2(s - top)
                total = jnp.sum(e, axis=-1, keepdims=True)
                att[i, :, cols] = (dot(e.astype(BF16), qkv[2, :span, cols]) / total).astype(BF16)
                logs.append(top + jnp.log2(total))
            lse[own, :] = lane_pair(logs[0], logs[-1], rows)
            ps[i] = dot(att[i], wov[...]).astype(BF16)
            rel = lax.bitwise_xor(jnp.int32(i), t)
            send_block(p_refs, rel, ps.at[i], p_sem)
            pending.append(
                move(att.at[i], saved.at[seq, block_at(rel, rows), pl.ds(feats + 3 * width, width)], o_sem.at[i])
            )
        for c in range(3):
            pending.append(move(qkv.at[c], saved.at[seq, :, pl.ds(feats + c * width, width)], o_sem.at[parts + c]))
        pending.append(move(lse, lse_out, in_sem.at[5]))
        for copy in pending:
            copy.wait()
        wait_blocks(p_refs, ps.at[0], p_sem)

    extra = [] if previous is None else [previous]
    return kernel_call(
        body,
        (
            *[struct((rows, feats), BF16)] * 4,
            struct((2 * seqs, length, feats + 4 * width), BF16),
            struct((length, 128), F32),
        ),
        (ANY,) * 4 + (HBM,) * 2,
        [SMEM, whole(docs.shape), whole(vecs.shape)]
        + [ANY] * 4
        + [HBM] * (2 + len(extra)),
        scratch=[
            VMEM((parts, rows, feats), BF16),
            VMEM(wqkv.shape, BF16),
            VMEM(wo.shape, BF16),
            VMEM((3, length, width), BF16),
            VMEM((parts, rows, width), BF16),
            VMEM((length, 128), F32),
            VMEM((parts, rows, feats), BF16),
            DMA((6,)),
            DMA((4,)),
            DMA((4,)),
            DMA((7,)),
        ],
        flops=2 * length * feats * width * 4 + 5 * length * length * width,
        nbytes=length * feats * 8,
        trans=length * length * heads // 2,
        aliases={9: 4} if extra else None,
        name="attend_forward",
    )(place, docs, vecs, *blocks, wqkv, wo, *extra)


def attend_backward(seq, place, docs, blocks, saved, lse, wqkv, wo, previous, earlier=()):
    rows, feats = blocks[0].shape
    parts = len(blocks)
    length = rows * parts
    width = wqkv.shape[2]
    size = feats // HEADS
    heads = width // size
    root = size ** (-0.5)
    scale = LOG2E * root

    seqs = docs.shape[0]

    def body(t_ref, doc_ref, *rest):
        dr = doc_ref[seq : seq + 1, :].astype(F32)
        x_refs, (saved_ref, lse_ref, w_ref, wo_ref), rest = rest[:4], rest[4:8], rest[8:]
        p_refs, (out, sums), rest = rest[-20:-16], rest[-16:-14], rest[-14:]
        xs, w, wov, qkvv, attv, lsev, gk, gv, ga, low, ps, in_sem, p_sem, o_sem = rest
        t = t_ref[0]
        load_wo = move(wo_ref, wov, in_sem.at[4])
        for r in (3, 2, 1, 0):
            at = lax.bitwise_xor(jnp.int32(r), t)
            move(x_refs[r], xs.at[at], in_sem.at[at])
        loads = [move(lse_ref, lsev, in_sem.at[6])]
        for c in range(3):
            loads.append(move(saved_ref.at[seq, :, pl.ds(feats + c * width, width)], qkvv.at[c], in_sem.at[12 + c]))
        for i in range(parts):
            rel = lax.bitwise_xor(jnp.int32(i), t)
            att_ref = saved_ref.at[seq, block_at(rel, rows), pl.ds(feats + 3 * width, width)]
            loads.append(move(att_ref, attv.at[i], in_sem.at[8 + i]))
        load_w = move(w_ref, w, in_sem.at[7])
        pending = []

        def project(i):
            pltpu.make_async_copy(x_refs[0], xs.at[i], in_sem.at[i]).wait()
            rel = lax.bitwise_xor(jnp.int32(i), t)
            pending.append(move(xs.at[i], out.at[seq, block_at(rel, rows), pl.ds(0, feats)], o_sem.at[i]))
            ga[i] = dot(xs[i], wov[...], NT).astype(BF16)

        load_wo.wait()
        project(parts - 1)
        for copy in loads:
            copy.wait()
        load_w.wait()
        q_sum = jnp.zeros((1, width), F32)
        v_sum = jnp.zeros((1, width), F32)
        for i in reversed(range(parts)):
            if i:
                project(i - 1)
            span = (i + 1) * rows
            own = slice(i * rows, span)
            same = column(dr[:, own]) == dr[:, :span]
            before = lax.broadcasted_iota(jnp.int32, (rows, span), 0) + i * rows >= lax.broadcasted_iota(
                jnp.int32, (rows, span), 1
            )
            allowed = same & before
            for hd in range(heads):
                cols = slice(hd * size, (hd + 1) * size)
                q = qkvv[0, own, cols]
                k = qkvv[1, :span, cols]
                g = ga[i, :, cols]
                s = dot(q, k, NT) * scale - lsev[own, hd : hd + 1]
                p = jnp.exp2(jnp.where(allowed, s, NEGATIVE))
                gp = dot(g, qkvv[2, :span, cols], NT)
                row = jnp.sum(g.astype(F32) * attv[i, :, cols].astype(F32), axis=-1, keepdims=True)
                gs = (p * (gp - row)).astype(BF16)
                low[0, own, cols] = (dot(gs, k) * root).astype(BF16)
                new_k = dot(gs, q, TN)
                new_v = dot(p.astype(BF16), g, TN)
                if i == parts - 1:
                    gk[:span, cols] = new_k
                    gv[:span, cols] = new_v
                else:
                    gk[:span, cols] += new_k
                    gv[:span, cols] += new_v
            low[1, own, :] = (gk[own, :] * root).astype(BF16)
            low[2, own, :] = gv[own, :].astype(BF16)
            q_sum += jnp.sum(low[0, own, :].astype(F32), axis=0, keepdims=True)
            v_sum += jnp.sum(low[2, own, :].astype(F32), axis=0, keepdims=True)
            ps[i] = (
                dot(low[0, own, :], w[0], NT) + dot(low[1, own, :], w[1], NT) + dot(low[2, own, :], w[2], NT)
            ).astype(BF16)
            rel = lax.bitwise_xor(jnp.int32(i), t)
            send_block(p_refs, rel, ps.at[i], p_sem)
            for c in range(3):
                dst = out.at[seq, block_at(rel, rows), pl.ds(feats + c * width, width)]
                pending.append(move(low.at[c, own], dst, o_sem.at[4 + 3 * i + c]))
        sums[0:1, :] = q_sum
        sums[1:2, :] = v_sum
        for copy in pending:
            copy.wait()
        wait_blocks(p_refs, ps.at[0], p_sem)

    extra = [] if previous is None else [previous]
    return kernel_call(
        body,
        (
            *[struct((rows, feats), BF16)] * 4,
            struct((2 * seqs, length, feats + 4 * width), BF16),
            struct((2, width), F32),
        ),
        (ANY,) * 4 + (HBM, whole((2, width))),
        [SMEM, whole(docs.shape)] + [ANY] * 4 + [HBM] * (4 + len(extra)) + [ANY] * len(earlier),
        scratch=[
            VMEM((parts, rows, feats), BF16),
            VMEM(wqkv.shape, BF16),
            VMEM(wo.shape, BF16),
            VMEM((3, length, width), BF16),
            VMEM((parts, rows, width), BF16),
            VMEM((length, 128), F32),
            VMEM((length, width), F32),
            VMEM((length, width), F32),
            VMEM((parts, rows, width), BF16),
            VMEM((3, length, width), BF16),
            VMEM((parts, rows, feats), BF16),
            DMA((15,)),
            DMA((4,)),
            DMA((16,)),
        ],
        flops=2 * length * feats * width * 4 + 10 * length * length * width,
        nbytes=length * feats * 8,
        trans=length * length * heads // 2,
        aliases={10: 4} if extra else None,
        name="attend_backward",
    )(place, docs, *blocks, saved, lse, wqkv, wo, *extra, *earlier)


ORDER = (3, 1, 2, 0)


ROWS, ACT, SLOPE, GRAD = range(4)


def feed_forward(seq, seqs, blocks, vecs, w_up, w_down, previous):
    rows, feats = blocks[0].shape
    parts = len(blocks)
    length = rows * parts
    units = w_up.shape[1]
    root = math.sqrt(2.0 / math.pi)

    def body(vec, *rest):
        x_refs, (up_ref, down_ref), rest = rest[:4], rest[4:6], rest[6:]
        p_refs, saved, rest = rest[-15:-11], rest[-11], rest[-10:]
        xs, up, down, u, act, slope, ps, in_sem, p_sem, o_sem = rest
        load_up = move(up_ref, up, in_sem.at[4])
        loads = {r: move(x_refs[r], xs.at[r], in_sem.at[r]) for r in ORDER}
        load_down = move(down_ref, down, in_sem.at[5])
        pending = []

        def project(k):
            r = ORDER[k]
            loads[r].wait()
            pending.append(move(xs.at[r], saved.at[ROWS, seq, pl.ds(r * rows, rows)], o_sem.at[r]))
            u[k % 2] = dot(xs[r], up[...]) + vec[...]

        load_up.wait()
        project(0)
        load_down.wait()
        for k, r in enumerate(ORDER):
            if k + 1 < parts:
                project(k + 1)
            v = u[k % 2]
            sq = v * v
            th = jnp.tanh(v * (root + (root * 0.044715) * sq))
            half = 0.5 + 0.5 * th
            g = (v * half).astype(BF16)
            act[r] = g
            slope[r] = (half + v * (1.0 - th * th) * (0.5 * root + (1.5 * 0.044715 * root) * sq)).astype(BF16)
            ps[r] = dot(g, down[...]).astype(BF16)
            at = pl.ds(r * rows, rows)
            pending.append(move(ps.at[r], p_refs[r], p_sem.at[r]))
            pending.append(move(act.at[r], saved.at[ACT, seq, at], o_sem.at[4 + r]))
            pending.append(move(slope.at[r], saved.at[SLOPE, seq, at], o_sem.at[8 + r]))
        for copy in pending:
            copy.wait()

    extra = [] if previous is None else [previous]
    return kernel_call(
        body,
        (
            *[struct((rows, feats), BF16)] * 4,
            struct((4, seqs, length, units), BF16),
        ),
        (ANY,) * 4 + (HBM,),
        [whole(vecs.shape)] + [ANY] * 4 + [HBM] * (2 + len(extra)),
        scratch=[
            VMEM((parts, rows, feats), BF16),
            VMEM(w_up.shape, BF16),
            VMEM(w_down.shape, BF16),
            VMEM((2, rows, units), F32),
            VMEM((parts, rows, units), BF16),
            VMEM((parts, rows, units), BF16),
            VMEM((parts, rows, feats), BF16),
            DMA((6,)),
            DMA((4,)),
            DMA((12,)),
        ],
        flops=4 * length * feats * units,
        nbytes=length * feats * 14,
        trans=length * units,
        aliases={7: 4} if extra else None,
        name="feed_forward",
    )(vecs, *blocks, w_up, w_down, *extra)


def feed_backward(seq, own, got, saved, w_up, w_down, earlier):
    rows, feats = own.shape[1:]
    parts = 4
    length = rows * parts
    units = w_up.shape[1]
    seqs = saved.shape[1]

    def body(own_ref, got_ref, saved_ref, up_ref, down_ref, *rest):
        p_refs, (grad_out, sums), rest = rest[-16:-12], rest[-12:-10], rest[-10:]
        ys, up, down, slopes, u, grad, ps, in_sem, p_sem, o_sem = rest
        load_down = move(down_ref, down, in_sem.at[4])
        loads, slope_loads = {}, {}
        for r in ORDER:
            loads[r] = move((got_ref if r % 2 else own_ref).at[r // 2], ys.at[r], in_sem.at[r])
            slope_loads[r] = move(saved_ref.at[SLOPE, seq, pl.ds(r * rows, rows)], slopes.at[r], in_sem.at[6 + r])
        load_up = move(up_ref, up, in_sem.at[5])
        pending = []

        def project(k):
            r = ORDER[k]
            loads[r].wait()
            slope_loads[r].wait()
            u[k % 2] = dot(ys[r], down[...], NT)

        load_down.wait()
        project(0)
        load_up.wait()
        total = jnp.zeros((8, units), F32)
        for k, r in enumerate(ORDER):
            if k + 1 < parts:
                project(k + 1)
            gu = (u[k % 2] * slopes[r].astype(F32)).astype(BF16)
            grad[r] = gu
            total += jnp.sum(gu.astype(F32).reshape(rows // 8, 8, units), axis=0)
            ps[r] = dot(gu, up[...], NT).astype(BF16)
            pending.append(move(ps.at[r], p_refs[r], p_sem.at[r]))
            pending.append(move(grad.at[r], grad_out.at[GRAD, seq, pl.ds(r * rows, rows)], o_sem.at[4 + r]))
        sums[...] = jnp.sum(total, axis=0, keepdims=True)
        for copy in pending:
            copy.wait()

    return kernel_call(
        body,
        (
            *[struct((rows, feats), BF16)] * 4,
            struct((4, seqs, length, units), BF16),
            struct((1, units), F32),
        ),
        (ANY,) * 4 + (HBM, whole((1, units))),
        [ANY] * 2 + [HBM] * 3 + [ANY] * len(earlier),
        scratch=[
            VMEM((parts, rows, feats), BF16),
            VMEM(w_up.shape, BF16),
            VMEM(w_down.shape, BF16),
            VMEM((parts, rows, units), BF16),
            VMEM((2, rows, units), F32),
            VMEM((parts, rows, units), BF16),
            VMEM((parts, rows, feats), BF16),
            DMA((10,)),
            DMA((4,)),
            DMA((8,)),
        ],
        flops=4 * length * feats * units,
        nbytes=length * feats * 14,
        aliases={2: 4},
        name="feed_backward",
    )(own, got, saved, w_up, w_down, *earlier)


def entries(ref, seq, part, place, rows):
    at = lax.bitwise_xor(jnp.int32(part), place) * rows
    return ref[seq : seq + 1, pl.ds(pl.multiple_of(at, rows), rows)].astype(F32)


def contrast_scores(place, ends, docs, labels, units):
    rows, feats = units[0].shape[0] - EXTRA, units[0].shape[1]
    factor = CONTRAST_SCALE / feats * LOG2E
    count = len(units)
    seqs = count // 4

    def body(t_ref, end_ref, doc_ref, lab_ref, *rest):
        refs, rest = rest[:count], rest[count:]
        exp_out, col_out, row_out, loss_out, both, exps, sums, in_sem, out_sem = rest
        t = t_ref[0]
        loads = [move(refs[k].at[pl.ds(0, rows)], both.at[k], in_sem.at[k]) for k in range(count)]
        for copy in loads:
            copy.wait()
        pending = []
        for s in range(4):
            seq, part = s // 2, s % 2 * 2
            own_lab = column(entries(lab_ref, seq, part, t, rows))

            def block(k, own_doc, seq=seq, part=part, s=s, own_lab=own_lab):
                e = jnp.exp2(dot(both[seq * 4 + part], both[k], NT) * factor)
                if own_doc is not None:
                    e = jnp.where(own_doc != entries(doc_ref, seq, k % 4, t, rows), e, 0.0)
                exps[s, :, k * rows : (k + 1) * rows] = e.astype(BF16)
                picked = jnp.where(own_lab == entries(lab_ref, k // 4, k % 4, t, rows), e, 0.0)
                lanes = [slice(c * 128, (c + 1) * 128) for c in range(rows // 128)]
                fold = lambda v: functools.reduce(jnp.add, [v[:, lane] for lane in lanes])
                return fold(e), fold(picked)

            terms = [block(k, None) for k in range(count) if k // 4 != seq]
            sums[0] = functools.reduce(jnp.add, [a for a, _ in terms])
            sums[1] = functools.reduce(jnp.add, [b for _, b in terms])
            single = end_ref[seq, 0] == end_ref[seq, 1]
            inner = slice(seq * 4 * rows, (seq + 1) * 4 * rows)

            @pl.when(single)
            def _(s=s, inner=inner):
                exps[s, :, inner] = jnp.zeros((rows, 4 * rows), BF16)

            @pl.when(jnp.logical_not(single))
            def _(seq=seq, part=part, block=block):
                own_doc = column(entries(doc_ref, seq, part, t, rows))
                for k in range(seq * 4, seq * 4 + 4):
                    a, b = block(k, own_doc)
                    sums[0] += a
                    sums[1] += b

            pending.append(move(exps.at[s], exp_out.at[s], out_sem.at[s]))
            wide = lane_pair(
                jnp.sum(sums[0], axis=-1, keepdims=True), jnp.sum(sums[1], axis=-1, keepdims=True), rows
            )
            col_out[s * rows : (s + 1) * rows, :] = wide
            flat = jnp.transpose(wide)[:8, :]
            row_out[:, s * rows : (s + 1) * rows] = flat
            if part == 0:
                logs = jnp.log(flat)
                loss_out[seq : seq + 1, :] = logs[0:1] - logs[1:2]
        for copy in pending:
            copy.wait()

    return kernel_call(
        body,
        (
            struct((16, rows, count * rows), BF16),
            struct((4 * rows, 128), F32),
            struct((8, 4 * rows), F32),
            struct((seqs, rows), F32),
        ),
        (HBM, whole((4 * rows, 128)), whole((8, 4 * rows)), whole((seqs, rows))),
        [SMEM, SMEM, whole(docs.shape), whole(labels.shape)] + [ANY] * count,
        scratch=[
            VMEM((count, rows, feats), BF16),
            VMEM((4, rows, count * rows), BF16),
            VMEM((2, rows, 128), F32),
            DMA((count,)),
            DMA((4,)),
        ],
        flops=2 * 4 * rows * count * rows * feats,
        nbytes=count * rows * feats * 4,
        trans=4 * rows * count * rows,
        name="contrast_scores",
    )(place, ends, docs, labels, *units)


def contrast_grads(seq, place, ends, labels, units, exps, col_sums, row_own, row_got, cot, cot_got):
    rows, feats = units[0].shape[0] - EXTRA, units[0].shape[1]
    factor = CONTRAST_SCALE / feats
    count = len(units)
    span = 4 * rows

    def body(t_ref, end_ref, lab_ref, col, own, got, *rest):
        refs, (e_ref, cot_ref, other_ref), rest = rest[:count], rest[count : count + 3], rest[count + 3 :]
        full, low, both, exps, scales, cots, grad, gn, full_v, low_v, in_sem, e_sem, q_sem, c_sem, o_sem = rest
        t = t_ref[0]
        order = [k for k in range(count) if k // 4 != seq] + [k for k in range(count) if k // 4 == seq]
        e_loads = [move(e_ref.at[2 * seq + h], exps.at[h], e_sem.at[h]) for h in range(2)]
        loads = {
            k: move(refs[k].at[pl.ds(0, rows)], both.at[pl.ds(k * rows, rows)], in_sem.at[k]) for k in order
        }
        small = [
            (
                move(refs[seq * 4 + h * 2].at[pl.ds(rows, EXTRA)], scales.at[h], q_sem.at[h]),
                move(other_ref if h else cot_ref.at[seq], cots.at[h], c_sem.at[h]),
            )
            for h in range(2)
        ]
        single = end_ref[seq, 0] == end_ref[seq, 1]

        def weigh(h, blocks):
            s = 2 * seq + h
            own_lab = column(entries(lab_ref, seq, h * 2, t, rows))
            inv = CONTRAST_WEIGHT / col[s * rows : (s + 1) * rows, :]
            all_i, pos_i = inv[:, 0:1], inv[:, 1:2]
            for k in blocks:
                other, piece = k // 4, k % 4
                source = own if piece % 2 == 0 else got
                at = (other * 2 + piece // 2) * rows
                inv_j = CONTRAST_WEIGHT / source[0:2, at : at + rows]
                same = own_lab == entries(lab_ref, other, piece, t, rows)
                coef = (all_i + inv_j[0:1]) - jnp.where(same, pos_i + inv_j[1:2], 0.0)
                cols = slice(k * rows, (k + 1) * rows)
                grad[h, :, cols] = (exps[h, :, cols].astype(F32) * coef).astype(BF16)

        outer = slice((1 - seq) * span, (2 - seq) * span)
        inner = slice(seq * span, (seq + 1) * span)
        for h in range(2):
            e_loads[h].wait()
        weigh(0, order[:4])
        for k in order:
            loads[k].wait()
        for h in range(2):
            if h == 0:
                weigh(1, order[:4])
            gn[h] = dot(grad[h, :, outer], both[outer, :])

        @pl.when(jnp.logical_not(single))
        def _():
            for h in range(2):
                weigh(h, order[4:])
                gn[h] += dot(grad[h, :, inner], both[inner, :])

        pending = []
        for h in range(2):
            first = (seq * 4 + h * 2) * rows
            n = both[first : first + rows, :].astype(F32)
            g = gn[h] * factor
            change = g - n * jnp.mean(g * n, axis=-1, keepdims=True)
            for copy in small[h]:
                copy.wait()
            pieces = scales[h, :, :rows].astype(F32)
            gy = cots[h].astype(F32) + column(pieces[0:1] + pieces[1:2]) * change
            low_v[h] = gy.astype(BF16)
            pending.append(move(low_v.at[h], low.at[h], o_sem.at[h]))
            if h == 0:
                full_v[...] = gy
                pending.append(move(full_v, full, o_sem.at[2]))
        for copy in pending:
            copy.wait()

    return kernel_call(
        body,
        (struct((rows, feats), F32), struct((2, rows, feats), BF16)),
        (ANY,) * 2,
        [
            SMEM,
            SMEM,
            whole(labels.shape),
            whole((4 * rows, 128)),
            whole((8, 4 * rows)),
            whole((8, 4 * rows)),
        ]
        + [ANY] * count
        + [HBM] * 2
        + [ANY],
        scratch=[
            VMEM((count * rows, feats), BF16),
            VMEM((2, rows, count * rows), BF16),
            VMEM((2, EXTRA, feats), BF16),
            VMEM((2, rows, feats), BF16),
            VMEM((2, rows, count * rows), BF16),
            VMEM((2, rows, feats), F32),
            VMEM((rows, feats), F32),
            VMEM((2, rows, feats), BF16),
            DMA((count,)),
            DMA((2,)),
            DMA((2,)),
            DMA((2,)),
            DMA((3,)),
        ],
        flops=4 * rows * count * rows * feats,
        nbytes=count * rows * feats * 4,
        name="contrast_grads",
    )(place, ends, labels, col_sums, row_own, row_got, *units, exps, cot, cot_got)


def down_grad(saved, own, got):
    seqs, length, units = saved.shape[1:]
    rows, feats = own[0].shape[1:]
    tiles = units // TILE

    def body(a_ref, *rest):
        own_refs, got_refs = rest[:seqs], rest[seqs : 2 * seqs]
        out_ref, a, b, out, a_sem, b_sem, o_sem = rest[2 * seqs :]
        b_loads = []
        for s in range(seqs):
            for r in range(4):
                src = (got_refs if r % 2 else own_refs)[s].at[r // 2]
                b_loads.append(move(src, b.at[s, pl.ds(r * rows, rows)], b_sem.at[4 * s + r]))
        columns = [pl.ds(i * TILE, TILE) for i in range(tiles)]
        a_loads = [move(a_ref.at[ACT, :, :, columns[i]], a.at[i], a_sem.at[i]) for i in range(tiles)]
        for copy in b_loads:
            copy.wait()
        stores = []
        for i in range(tiles):
            a_loads[i].wait()
            out[i] = functools.reduce(jnp.add, [dot(a[i, s], b[s], TN) for s in range(seqs)]).astype(BF16)
            stores.append(move(out.at[i], out_ref.at[columns[i]], o_sem.at[i]))
        for copy in stores:
            copy.wait()

    return kernel_call(
        body,
        struct((units, feats), BF16),
        ANY,
        [HBM] + [ANY] * (2 * seqs),
        scratch=[
            VMEM((tiles, seqs, length, TILE), BF16),
            VMEM((seqs, length, feats), BF16),
            VMEM((tiles, TILE, feats), BF16),
            DMA((tiles,)),
            DMA((4 * seqs,)),
            DMA((tiles,)),
        ],
        flops=2 * seqs * length * units * feats,
        nbytes=4 * seqs * length * feats,
        name="down_grad",
    )(saved, *own, *got)


TILE = 256


def send_half(tile, tiles, high, src, to_other, kept, at, sem):
    upper = tile >= tiles // 2
    rows = pl.ds((tile % (tiles // 2)) * TILE, TILE)

    @pl.when(high == int(upper))
    def _():
        pltpu.make_async_copy(src, kept.at[rows, at], sem).start()

    @pl.when(high != int(upper))
    def _():
        pltpu.make_async_copy(src, to_other.at[rows, at], sem).start()

    return pltpu.make_async_copy(src, kept.at[rows, at], sem)


def weight_grad(saved, flags, bit):
    seqs, length, out_rows = saved.shape[1:]
    cols = out_rows
    tiles = out_rows // TILE

    def body(flag, s_ref, other_ref, kept_ref, a, b, out, a_sem, b_sem, o_sem):
        b_loads = [move(s_ref.at[GRAD, s], b.at[s], b_sem.at[s]) for s in range(seqs)]
        columns = [pl.ds(i * TILE, TILE) for i in range(tiles)]
        a_loads = [move(s_ref.at[ROWS, :, :, columns[i]], a.at[i], a_sem.at[i]) for i in range(tiles)]
        for copy in b_loads:
            copy.wait()
        stores = []
        for i in range(tiles):
            a_loads[i].wait()
            out[i] = functools.reduce(jnp.add, [dot(a[i, s], b[s], TN) for s in range(seqs)]).astype(BF16)
            stores.append(
                send_half(i, tiles, flag[bit], out.at[i], other_ref, kept_ref, pl.ds(0, cols), o_sem.at[i])
            )
        for copy in stores:
            copy.wait()

    return kernel_call(
        body,
        (struct((out_rows // 2, cols), BF16),) * 2,
        (ANY,) * 2,
        [pl.BlockSpec(memory_space=pltpu.SMEM)] + [HBM],
        scratch=[
            VMEM((tiles, seqs, length, TILE), BF16),
            VMEM((seqs, length, cols), BF16),
            VMEM((tiles, TILE, cols), BF16),
            DMA((tiles,)),
            DMA((seqs,)),
            DMA((tiles,)),
        ],
        flops=2 * seqs * length * out_rows * cols,
        nbytes=4 * seqs * length * cols,
        name="weight_grad",
    )(flags, saved)


def head_terms(seq, s_ref, h_ref, feats, width, a, g, r, a_sem, g_sem, r_sem):
    tiles = feats // width
    columns = [pl.ds(i * width, width) for i in range(tiles)]
    a_load = lambda i: move(s_ref.at[seq, :, columns[i]], a.at[i], a_sem.at[i])
    r_load = lambda i: move(h_ref.at[seq, :, columns[i]], r.at[i], r_sem.at[i])
    g_load = lambda n: move(
        (s_ref if n == 3 else h_ref).at[seq, :, pl.ds(feats + n * width, width)], g.at[n], g_sem.at[n]
    )
    a_loads = [a_load(0)]
    g_loads = [g_load(n) for n in range(4)]
    r_loads = [r_load(0)]
    for i in range(1, tiles):
        a_loads.append(a_load(i))
        r_loads.append(r_load(i))

    def tile(i):
        a_loads[i].wait()
        values = []
        for n in range(3):
            if i == 0:
                g_loads[n].wait()
            values.append(dot(a[i], g[n], TN))
        if i == 0:
            g_loads[3].wait()
        r_loads[i].wait()
        values.append(dot(g[3], r[i], TN))
        return values

    return tile, columns


def head_scratch(length, feats, width):
    tiles = feats // width
    return [
        VMEM((tiles, length, width), BF16),
        VMEM((4, length, width), BF16),
        VMEM((tiles, length, width), BF16),
        DMA((tiles,)),
        DMA((4,)),
        DMA((tiles,)),
    ]


def head_part(saved, grads, feats):
    length = saved.shape[1]
    width = (saved.shape[2] - feats) // 4
    tiles = feats // width

    def body(s_ref, h_ref, out_ref, a, g, r, a_sem, g_sem, r_sem, out, o_sem):
        tile, _ = head_terms(0, s_ref, h_ref, feats, width, a, g, r, a_sem, g_sem, r_sem)
        stores = []
        for i in range(tiles):
            for n, value in enumerate(tile(i)):
                out[i, :, n * width : (n + 1) * width] = value
            stores.append(move(out.at[i], out_ref.at[i], o_sem.at[i]))
        for copy in stores:
            copy.wait()

    return kernel_call(
        body,
        struct((tiles, width, 4 * width), F32),
        ANY,
        [HBM] * 2,
        scratch=head_scratch(length, feats, width) + [VMEM((tiles, width, 4 * width), F32), DMA((tiles,))],
        flops=8 * length * feats * width,
        nbytes=4 * length * feats,
        name="head_part",
    )(saved, grads)


def head_grads(saved, grads, part, feats, flags, bits):
    length = saved.shape[1]
    width = (saved.shape[2] - feats) // 4
    tiles = feats // width

    def body(flag, s_ref, h_ref, part_ref, *refs):
        first_refs, second_refs = refs[:2], refs[2:4]
        a, g, r, a_sem, g_sem, r_sem, old, first, second, p_sem, o_sem = refs[4:]
        tile, columns = head_terms(1, s_ref, h_ref, feats, width, a, g, r, a_sem, g_sem, r_sem)
        p_loads = [move(part_ref.at[i], old.at[i], p_sem.at[i]) for i in range(tiles)]
        stores = []
        for i in range(tiles):
            values = tile(i)
            p_loads[i].wait()
            for n, value in enumerate(values):
                total = value + old[i, :, n * width : (n + 1) * width]
                (first, second)[n // 2][i, :, n % 2 * width : (n % 2 + 1) * width] = total.astype(BF16)
            for n, (src, outs) in enumerate(((first, first_refs), (second, second_refs))):
                stores.append(
                    send_half(i, tiles, flag[bits[n]], src.at[i], *outs, pl.ds(0, 2 * width), o_sem.at[2 * i + n])
                )
        for copy in stores:
            copy.wait()

    return kernel_call(
        body,
        (struct((feats // 2, 2 * width), BF16),) * 4,
        (ANY,) * 4,
        [SMEM] + [HBM] * 2 + [ANY],
        scratch=head_scratch(length, feats, width)
        + [
            VMEM((tiles, width, 4 * width), F32),
            VMEM((tiles, width, 2 * width), BF16),
            VMEM((tiles, width, 2 * width), BF16),
            DMA((tiles,)),
            DMA((2 * tiles,)),
        ],
        flops=8 * length * feats * width,
        nbytes=4 * length * feats,
        name="head_grads",
    )(flags, saved, grads, part)


def halve_step(flags, bit, keep, got):
    rows, cols = keep.shape
    half = rows // 2

    def body(flag, k_ref, g_ref, *outs):
        if bit is None:
            outs[0][...] = (k_ref[...].astype(F32) + g_ref[...].astype(F32)).astype(BF16)
            return
        for high in (0, 1):

            @pl.when(flag[bit] == high)
            def _(high=high):
                for out, upper in ((outs[0], 1 - high), (outs[1], high)):
                    at = slice(upper * half, (upper + 1) * half)
                    out[...] = (k_ref[at, :].astype(F32) + g_ref[at, :].astype(F32)).astype(BF16)

    shape = (rows, cols) if bit is None else (half, cols)
    return kernel_call(
        body,
        (struct(shape, BF16),) * (1 if bit is None else 2),
        (whole(shape),) * (1 if bit is None else 2),
        [pl.BlockSpec(memory_space=pltpu.SMEM)] + [whole((rows, cols))] * 2,
        nbytes=rows * cols * 6,
        limit=SMALL,
        name="halve_step",
    )(flags, keep, got)


def join_step(flags, bit, own, got, dtype):
    rows, cols = own.shape
    steps = 2 if dtype == F32 else 1
    part = rows // steps

    def body(flag, own_ref, got_ref, out):
        for high in (0, 1):

            @pl.when(flag[bit] == high)
            def _(high=high):
                out[high] = own_ref[...].astype(dtype)
                out[1 - high] = got_ref[...].astype(dtype)

    block = pl.BlockSpec((part, cols), lambda i: (i, 0))
    return kernel_call(
        body,
        struct((2, rows, cols), dtype),
        pl.BlockSpec((2, part, cols), lambda i: (0, i, 0)),
        [pl.BlockSpec(memory_space=pltpu.SMEM), block, block],
        grid=(steps,),
        nbytes=rows * cols * 8,
        limit=SMALL,
        name="join_step",
    )(flags, own, got).reshape(2 * rows, cols)


def part_outputs(parts, order):
    rows, cols = parts.shape
    step = rows >> len(order)

    def place(i):
        return functools.reduce(
            jnp.add, [((i >> bit) & 1) << (len(order) - 1 - n) for n, bit in enumerate(order)]
        )

    def body(part, out):
        out[...] = part[...].astype(F32)

    return kernel_call(
        body,
        struct((rows, cols), F32),
        pl.BlockSpec((step, cols), lambda i: (place(i), 0)),
        [pl.BlockSpec((step, cols), lambda i: (i, 0))],
        grid=(1 << len(order),),
        nbytes=6 * rows * cols,
        limit=SMALL,
        name="part_outputs",
    )(parts)


def head_outputs(flags, bits, first, second):
    feats = 2 * first[0].shape[0]
    width = first[0].shape[1] // 2
    tile = width

    def body(h_ref, a_ref, b_ref, c_ref, d_ref, qkv, out):
        mine = (lax.div(pl.program_id(0) * tile, feats // 2) == h_ref[bits[0]])

        for case, x in ((True, a_ref), (False, b_ref)):
            @pl.when(mine == case)
            def _(x=x):
                qkv[0] = x[:, :width].astype(F32)
                qkv[1] = x[:, width:].astype(F32)

        mine_two = (lax.div(pl.program_id(0) * tile, feats // 2) == h_ref[bits[1]])
        for case, y in ((True, c_ref), (False, d_ref)):
            @pl.when(mine_two == case)
            def _(y=y):
                qkv[2] = y[:, :width].astype(F32)
                out[...] = y[:, width:].astype(F32)

    half = pl.BlockSpec((tile, 2 * width), lambda i, h: (lax.rem(i, feats // 2 // tile), 0))
    return kernel_call(
        body,
        (struct((3, feats, width), F32), struct((width, feats), F32)),
        (pl.BlockSpec((3, tile, width), lambda i, h: (0, i, 0)), pl.BlockSpec((width, tile), lambda i, h: (0, i))),
        [half] * 4,
        grid=(feats // tile,),
        nbytes=10 * feats * width * 4,
        prefetch=1,
        limit=SMALL,
        name="head_outputs",
    )(flags, *first, *second)


def swap(value, axis, size, bit):
    return lax.ppermute(value, axis, [(i, i ^ bit) for i in range(size)])


CORE, CROSS = 1, 2


def tensor_swap(value, bit):
    return swap(value, "tensor", 4, bit)


def tie(value, *earlier):
    return lax.optimization_barrier((value, *earlier))[0] if earlier else value


class Gather:
    def __init__(self, value):
        self.value = value
        self.cross = tensor_swap(value, CROSS)
        self.core = tensor_swap(value, CORE)

    def blocks(self, *earlier):
        return [self.value, self.core, self.cross, tensor_swap(tie(self.cross, *earlier), CORE)]


class Scatter:
    def __init__(self, blocks):
        self.own, self.other = blocks[0], blocks[2]
        self.core_other = tensor_swap(blocks[3], CORE)
        self.core_own = tensor_swap(blocks[1], CORE)
        self.mark = blocks[3]

    def cross(self, *earlier):
        block = (tie(self.other, *earlier).astype(F32) + self.core_other.astype(F32)).astype(BF16)
        self.parts = (self.own, self.core_own, tensor_swap(block, CROSS))
        return block


class DpSum:
    def __init__(self, send, keep, flags, size, order):
        self.send, self.value, self.flags, self.size = send, keep, flags, size
        self.left = [(bit, True) for bit in order] + [(bit, False) for bit in reversed(order)]
        self.got, self.now = None, None

    def advance(self, *earlier):
        if self.now is not None and self.now[1]:
            more = self.left and self.left[0][1]
            parts = halve_step(self.flags, self.left[0][0] if more else None, tie(self.value, *earlier), self.got)
            self.send, self.value = parts if more else (parts[0], parts[0])
        elif self.now is not None:
            self.send = self.value = join_step(self.flags, self.now[0], tie(self.value, *earlier), self.got, BF16)
        self.now = self.left.pop(0)
        self.got = swap(self.send, "dp", self.size, 1 << self.now[0])
        return self.send

    def halves(self):
        return self.value, self.got


def shards(
    dp_size,
    tokens,
    doc_ids,
    targets,
    cotangent,
    ln1_gain,
    ln1_bias,
    qkv_weight,
    query_bias,
    value_bias,
    output_weight,
    out_bias,
    ln2_gain,
    ln2_bias,
    up_weight,
    up_bias,
    down_weight,
    down_bias,
):
    seqs, rows, feats = tokens.shape
    length = doc_ids.shape[1]
    parts = length // rows
    me = lax.axis_index("tensor")
    place = me.reshape(1).astype(jnp.int32)
    vec = lambda v: v.astype(F32).reshape(1, -1)
    gain_one, shift_one, gain_two, shift_two = vec(ln1_gain), vec(ln1_bias), vec(ln2_gain), vec(ln2_bias)
    out_offset, down_offset, up_shift = vec(out_bias), vec(down_bias), vec(up_bias)
    head_shift = vec(jnp.concatenate([query_bias, value_bias]))
    ends = doc_ids[:, :: length - 1]

    fine = 16
    paired = (jnp.arange(feats, dtype=jnp.int32) // 2).astype(F32)
    freq = jnp.exp(paired * (-2.0 * math.log(10000.0) / feats))[None, :]
    odd = (jnp.arange(feats, dtype=jnp.int32) % 2 == 1)[None, :]
    coarse_at = (me * rows + fine * jnp.arange(rows // fine, dtype=jnp.int32)).astype(F32)[:, None] * freq
    fine_at = jnp.arange(fine, dtype=jnp.int32).astype(F32)[:, None] * freq
    sin_a, cos_a = jnp.sin(coarse_at), jnp.cos(coarse_at)
    tables = (jnp.where(odd, cos_a, sin_a), jnp.where(odd, -sin_a, cos_a), jnp.cos(fine_at), jnp.sin(fine_at))

    hidden, stream, grad_r = [None] * 2, [None] * 2, [None] * 2
    kept, up_sums, head_sums, sums_one, sums_two = [None] * 2, [None] * 2, [None] * 2, [None] * 2, [None] * 2
    shared = {"attend": None, "feed": None, "act": None, "heads": None, "input": None}

    def attend(s, gathered, *earlier):
        *blocks, shared["attend"], kept[s] = attend_forward(
            s, tie(place, *earlier), doc_ids, head_shift, gathered, qkv_weight, output_weight, shared["attend"]
        )
        return Scatter(blocks)

    def middle_rows(s, scatter, *earlier):
        stream[s], normed = second_norm(hidden[s], scatter.parts, tie(out_offset, *earlier), gain_two, shift_two)
        return normed, Gather(normed)

    def feed(s, gathered, *earlier):
        *blocks, shared["feed"] = feed_forward(
            s, seqs, gathered, tie(up_shift, *earlier), up_weight, down_weight, shared["feed"]
        )
        return Scatter(blocks)

    def last_rows(s, scatter, *earlier):
        shared["act"], unit = output_rows(
            s, seqs, stream[s], scatter.parts, tie(down_offset, *earlier), shared["act"]
        )
        return unit, Gather(unit)

    hidden[0], normed_a = first_norm(0, tokens, tables, gain_one, shift_one)
    rows_a = Gather(normed_a)
    hidden[1], normed_b = first_norm(1, tie(tokens, normed_a), tables, gain_one, shift_one)
    rows_b = Gather(normed_b)
    at_a = attend(0, rows_a.blocks(normed_b))
    block = at_a.cross(rows_b.cross)
    at_b = attend(1, rows_b.blocks(), block)
    normed, rows_a = middle_rows(0, at_a, at_b.mark)
    block = at_b.cross(normed)
    ff_a = feed(0, rows_a.blocks(), block)
    normed, rows_b = middle_rows(1, at_b, ff_a.mark)
    block = ff_a.cross(normed)
    ff_b = feed(1, rows_b.blocks(), block)
    unit, units_a = last_rows(0, ff_a, ff_b.mark)
    block = ff_b.cross(unit)
    unit, units_b = last_rows(1, ff_b, block)
    cots = [tensor_swap(tie(cotangent[s], unit), CROSS) for s in range(2)]

    units = units_a.blocks() + units_b.blocks()
    exps, col_sums, row_sums, loss = contrast_scores(place, ends, doc_ids, targets, units)
    row_got = tensor_swap(row_sums, CORE)
    grad_y, low_y, got_y = [None] * 2, [None] * 2, [None] * 2
    for s in range(2):
        grad_y[s], low_y[s] = contrast_grads(
            s, tie(place, *low_y[:s]), ends, targets, units, exps, col_sums, row_sums, row_got, cotangent, cots[s]
        )
        got_y[s] = tensor_swap(tie(low_y[s], cots[1]), CORE)

    def feed_back(s, *earlier):
        *blocks, shared["feed"], up_sums[s] = feed_backward(
            s, low_y[s], got_y[s], shared["feed"], up_weight, down_weight, earlier
        )
        return Scatter(blocks)

    def middle_back(s, scatter, *earlier):
        grad_r[s], low, sums_two[s] = norm_backward(
            s, seqs, stream[s], scatter.parts, tie(gain_two, *earlier), grad_y[s], False, None
        )
        return low, Gather(low)

    def attend_back(s, gathered, *earlier, after=()):
        *blocks, shared["heads"], head_sums[s] = attend_backward(
            s, tie(place, *earlier), doc_ids, gathered, shared["attend"], kept[s], qkv_weight, output_weight,
            shared["heads"], after,
        )
        return Scatter(blocks)

    def first_back(s, scatter, *earlier):
        shared["input"], sums_one[s] = norm_backward(
            s, seqs, hidden[s], scatter.parts, tie(gain_one, *earlier), grad_r[s], True, shared["input"]
        )
        return sums_one[s]

    bits = list(range(dp_size.bit_length() - 1))
    other_bits = bits[1::-1] + bits[2:]
    flags = (lax.axis_index("dp") >> jnp.arange(len(bits), dtype=jnp.int32)) & 1
    grad_down_w = down_grad(shared["feed"], low_y, got_y)
    down_part = lax.psum_scatter(grad_down_w, "dp", scatter_dimension=0, tiled=True)
    fb_a = feed_back(0, grad_down_w)
    fb_b = feed_back(1, fb_a.cross())
    low, rows_a = middle_back(0, fb_a, fb_b.mark)
    block = fb_b.cross(low)
    up_sum = DpSum(*weight_grad(tie(shared["feed"], block), flags, bits[0]), flags, dp_size, bits)
    sent = up_sum.advance()
    ab_a = attend_back(0, rows_a.blocks(sent), sent)
    low, rows_b = middle_back(1, fb_b, ab_a.mark)
    block = ab_a.cross(low)
    part = head_part(tie(shared["attend"], block), shared["heads"], feats)
    sent = up_sum.advance(part, rows_b.cross)
    ab_b = attend_back(1, rows_b.blocks(sent), sent, down_part, after=(part,))
    down_all = lax.all_gather(tie(down_part, sent), "dp", axis=0, tiled=True)
    sent = up_sum.advance(ab_b.mark)
    sums = first_back(0, ab_a, sent)
    block = ab_b.cross(sums)
    first_send, first_keep, second_send, second_keep = head_grads(
        tie(shared["attend"], block), shared["heads"], part, feats, flags, (bits[0], other_bits[0])
    )
    first = DpSum(first_send, first_keep, flags, dp_size, bits)
    second = DpSum(second_send, second_keep, flags, dp_size, other_bits)
    sent = (first.advance(), second.advance())
    sums = first_back(1, ab_b, *sent)
    sent = (sums,)

    total = lambda items: functools.reduce(jnp.add, items)
    heads_sum = total(head_sums)
    heads_row = jnp.pad(heads_sum.reshape(1, -1), ((0, 0), (0, feats - heads_sum.size)))
    small = jnp.concatenate([total(sums_one)[:2], total(sums_two), total(up_sums), heads_row])
    swaps = [("tensor", 4, CROSS)] + [("dp", dp_size, 1 << bit) for bit in bits] + [("tensor", 4, CORE)]
    shared_rows = (jnp.arange(small.shape[0]) < 6).astype(F32)[:, None]
    axis, size, bit = swaps.pop(0)
    arriving = swap(small, axis, size, bit)
    sent = ()
    while first.left or arriving is not None or up_sum.left:
        if first.left:
            sent = (first.advance(*sent),)
        if up_sum.left:
            sent = (up_sum.advance(*sent),)
        if second.left:
            sent = (second.advance(*sent),)
        if len(first.left) == 2:
            grad_down_w = tie(down_all, *sent).astype(F32)
            sent += (grad_down_w,)
        small = tie(small, *sent)
        if arriving is not None:
            small = small + (arriving * shared_rows if axis == "tensor" else arriving)
        arriving = None
        if swaps:
            axis, size, bit = swaps.pop(0)
            arriving = swap(small, axis, size, bit)
        sent = (small,)
    local, small = small[6:], small[:6]
    own, got = up_sum.halves()
    grad_up_w = join_step(flags, bits[0], tie(own, *sent), got, F32)
    own, got = first.halves()
    grad_qkv_w, grad_out_w = head_outputs(
        flags, (bits[0], other_bits[0]), (tie(own, grad_up_w), got), second.halves()
    )
    return (
        shared["act"],
        loss,
        shared["input"],
        small[0],
        small[1],
        grad_qkv_w,
        local[1, : heads_sum.shape[1]],
        local[1, heads_sum.shape[1] : 2 * heads_sum.shape[1]],
        grad_out_w,
        small[4],
        small[2],
        small[3],
        grad_up_w,
        local[0],
        grad_down_w,
        small[5],
    )


def solution(mesh):
    in_specs = (
        P("dp", "tensor", None),
        P("dp", None),
        P("dp", None),
        P("dp", "tensor", None),
        P(),
        P(),
        P(None, None, "tensor"),
        P("tensor"),
        P("tensor"),
        P("tensor", None),
        P(),
        P(),
        P(),
        P(None, "tensor"),
        P("tensor"),
        P("tensor", None),
        P(),
    )
    out_specs = (
        P("dp", "tensor", None),
        P("dp", "tensor"),
        P("dp", "tensor", None),
        P(),
        P(),
        P(None, None, "tensor"),
        P("tensor"),
        P("tensor"),
        P("tensor", None),
        P(),
        P(),
        P(),
        P(None, "tensor"),
        P("tensor"),
        P("tensor", None),
        P(),
    )
    return jax.shard_map(
        functools.partial(shards, mesh.shape["dp"]),
        mesh=mesh,
        in_specs=in_specs,
        out_specs=out_specs,
        check_vma=False,
    )
```

```python
import functools
import math

import jax
import jax.numpy as jnp
from jax import lax
from jax.experimental import pallas as pl
from jax.experimental.pallas import tpu as pltpu
from jax.sharding import PartitionSpec as P

HEADS = 8
NORM_EPS = 1e-05
CONTRAST_SCALE = 32.0
CONTRAST_WEIGHT = 64.0
NEGATIVE = -1e30
LOG2E = math.log2(math.e)
F32 = jnp.float32
BF16 = jnp.bfloat16
MIB = 1 << 20
LIMIT, SMALL = 52, 14
COST = 0.02
NN = (((1,), (0,)), ((), ()))
NT = (((1,), (1,)), ((), ()))
TN = (((0,), (0,)), ((), ()))
VMEM = pltpu.VMEM


def dot(a, b, dims=NN):
    return lax.dot_general(a, b, dims, preferred_element_type=F32)


def whole(shape):
    return pl.BlockSpec(shape, lambda *_: (0,) * len(shape))


def kernel_call(body, outs, out_specs, in_specs, grid=(1,), scratch=(), flops=0, nbytes=0, trans=0,
                limit=LIMIT, aliases=None, prefetch=0, name=None):
    return pl.pallas_call(
        body,
        out_shape=outs,
        grid_spec=pltpu.PrefetchScalarGridSpec(
            num_scalar_prefetch=prefetch,
            grid=grid,
            in_specs=in_specs,
            out_specs=out_specs,
            scratch_shapes=scratch,
        ),
        name=name,
        input_output_aliases=aliases or {},
        cost_estimate=pl.CostEstimate(
            flops=int(flops * COST), bytes_accessed=int(nbytes * COST), transcendentals=int(trans * COST)
        ),
        compiler_params=pltpu.CompilerParams(vmem_limit_bytes=limit * MIB),
    )


def struct(shape, dtype):
    return jax.ShapeDtypeStruct(shape, dtype)


ANY = pl.BlockSpec(memory_space=pl.ANY)
HBM = pl.BlockSpec(memory_space=pltpu.HBM)
SMEM = pl.BlockSpec(memory_space=pltpu.SMEM)
DMA = pltpu.SemaphoreType.DMA


def move(src, dst, sem):
    copy = pltpu.make_async_copy(src, dst, sem)
    copy.start()
    return copy


def column(row):
    return jnp.transpose(jnp.broadcast_to(row, (8, row.shape[1])))[:, :1]


def norm_stats(v):
    centered = v - jnp.mean(v, axis=-1, keepdims=True)
    rstd = lax.rsqrt(jnp.mean(centered * centered, axis=-1, keepdims=True) + NORM_EPS)
    return centered * rstd, rstd


ROW_STEPS = 4


def row_blocks(rows, cols):
    return pl.BlockSpec((rows // ROW_STEPS, cols), lambda i: (i, 0))


def first_norm(seq, tokens, tables, gain, shift):
    rows, feats = tokens.shape[1:]
    fine = tables[2].shape[0]
    step = rows // ROW_STEPS

    def body(tok, pa, qa, cb, sb, g, b, h_out, a_out):
        i = pl.program_id(0)
        for c in range(step // fine):
            at = pl.ds(c * fine, fine)
            row = pl.ds(i * (step // fine) + c, 1)
            pos = pa[row, :] * cb[...] + qa[row, :] * sb[...]
            h = tok[0, at, :].astype(F32) + pos
            h_out[at, :] = h
            z, _ = norm_stats(h)
            a_out[at, :] = (z * g[...] + b[...]).astype(BF16)

    return kernel_call(
        body,
        (struct((rows, feats), F32), struct((rows, feats), BF16)),
        (row_blocks(rows, feats), row_blocks(rows, feats)),
        [pl.BlockSpec((1, step, feats), lambda i: (seq, i, 0))]
        + [whole(t.shape) for t in tables]
        + [whole((1, feats))] * 2,
        grid=(ROW_STEPS,),
        nbytes=rows * feats * 8,
        limit=SMALL,
        name="first_norm",
    )(tokens, *tables, gain, shift)


def joined(parts, at):
    return functools.reduce(jnp.add, [p[at, :].astype(F32) for p in parts])


def second_norm(h, parts, offset, gain, shift):
    rows, feats = h.shape
    chunk = 32
    step = rows // ROW_STEPS

    def body(h_ref, k_ref, c_ref, x_ref, o_ref, g, b, r_out, n_out):
        for c in range(step // chunk):
            at = pl.ds(c * chunk, chunk)
            r = h_ref[at, :] + joined((k_ref, c_ref, x_ref), at) + o_ref[...]
            r_out[at, :] = r
            z, _ = norm_stats(r)
            n_out[at, :] = (z * g[...] + b[...]).astype(BF16)

    block = row_blocks(rows, feats)
    return kernel_call(
        body,
        (struct((rows, feats), F32), struct((rows, feats), BF16)),
        (block, block),
        [block] * 4 + [whole((1, feats))] * 3,
        grid=(ROW_STEPS,),
        nbytes=rows * feats * 16,
        limit=SMALL,
        name="second_norm",
    )(h, *parts, offset, gain, shift)


EXTRA = 16


def output_rows(seq, seqs, r1, parts, offset, previous):
    rows, feats = r1.shape
    step, chunk = 128, 32

    def body(r_ref, k_ref, c_ref, x_ref, o_ref, *rest):
        act_out, n_out, q_all = rest[-3:]
        i = pl.program_id(0)
        for c in range(step // chunk):
            at = pl.ds(c * chunk, chunk)
            y = r_ref[at, :] + joined((k_ref, c_ref, x_ref), at) + o_ref[...]
            act_out[0, at, :] = y.astype(BF16)
            q = lax.rsqrt(jnp.mean(y * y, axis=-1, keepdims=True) + NORM_EPS)
            n_out[pl.ds(pl.multiple_of(i * step + c * chunk, chunk), chunk), :] = (y * q).astype(BF16)
            q_all[at, :] = jnp.broadcast_to(q, (chunk, step))

        @pl.when(i == 0)
        def _():
            n_out[rows:, :] = jnp.zeros((EXTRA, feats), BF16)

        row = jnp.transpose(q_all[...])[:EXTRA, :]
        high = row.astype(BF16).astype(F32)
        which = lax.broadcasted_iota(jnp.int32, (EXTRA, step), 0)
        lanes = pl.ds(pl.multiple_of(i * step, step), step)
        n_out[rows:, lanes] = jnp.where(which == 0, high, jnp.where(which == 1, row - high, 0.0)).astype(BF16)

    block = pl.BlockSpec((step, feats), lambda i: (i, 0))
    extra = [] if previous is None else [previous]
    return kernel_call(
        body,
        (struct((seqs, rows, feats), BF16), struct((rows + EXTRA, feats), BF16)),
        (pl.BlockSpec((1, step, feats), lambda i: (seq, i, 0)), whole((rows + EXTRA, feats))),
        [block] * 4 + [whole((1, feats))] + [ANY] * len(extra),
        grid=(rows // step,),
        scratch=[VMEM((step, step), F32)],
        nbytes=rows * feats * 14,
        aliases={5: 0} if extra else None,
        limit=SMALL,
        name="output_rows",
    )(r1, *parts, offset, *extra)


def norm_backward(seq, seqs, v, parts, gain, base, final, previous):
    rows, feats = v.shape
    chunk = 16
    step = rows // ROW_STEPS

    def body(v_ref, k_ref, c_ref, x_ref, g, base_ref, *rest):
        if final:
            out, sums = rest[-2:]
        else:
            out, low, sums = rest[-3:]
        acc = [jnp.zeros((8, feats), F32) for _ in range(2 if final else 4)]
        for c in range(step // chunk):
            at = pl.ds(c * chunk, chunk)
            got = joined((k_ref, c_ref, x_ref), at)
            z, rstd = norm_stats(v_ref[at, :])
            w = got * g[...]
            inner = rstd * (w - jnp.mean(w, axis=-1, keepdims=True) - z * jnp.mean(w * z, axis=-1, keepdims=True))
            old = base_ref[at, :]
            new = old + inner
            if final:
                out[0, at, :] = new
            else:
                out[at, :] = new
                low[at, :] = new.astype(BF16)
            terms = [got * z, got] + ([] if final else [new, old])
            for k, term in enumerate(terms):
                acc[k] = acc[k] + jnp.sum(term.reshape(chunk // 8, 8, feats), axis=0)

        @pl.when(pl.program_id(0) == 0)
        def _():
            sums[...] = jnp.zeros_like(sums)

        for k, term in enumerate(acc):
            sums[k : k + 1, :] += jnp.sum(term, axis=0, keepdims=True)

    block = row_blocks(rows, feats)
    extra = [] if previous is None else [previous]
    seq_block = pl.BlockSpec((1, step, feats), lambda i: (seq, i, 0))
    if final:
        outs, specs = (struct((seqs, rows, feats), F32), struct((4, feats), F32)), (seq_block, whole((4, feats)))
    else:
        outs = (struct((rows, feats), F32), struct((rows, feats), BF16), struct((4, feats), F32))
        specs = (block, block, whole((4, feats)))
    return kernel_call(
        body,
        outs,
        specs,
        [block] * 4 + [whole((1, feats)), block] + [ANY] * len(extra),
        grid=(ROW_STEPS,),
        nbytes=rows * feats * 20,
        aliases={6: 0} if extra else None,
        limit=SMALL,
        name="norm_backward",
    )(v, *parts, gain, base, *extra)


def send_block(refs, rel, src, sems):
    for r, ref in enumerate(refs):

        @pl.when(rel == r)
        def _(r=r, ref=ref):
            pltpu.make_async_copy(src, ref, sems.at[r]).start()


def wait_blocks(refs, src, sems):
    for r, ref in enumerate(refs):
        pltpu.make_async_copy(src, ref, sems.at[r]).wait()


def block_at(rel, rows):
    return pl.ds(pl.multiple_of(rel * rows, rows), rows)


def lane_pair(first, second, rows):
    lanes = lax.broadcasted_iota(jnp.int32, (rows, 128), 1)
    return jnp.where(lanes == 0, first, second)


def attend_forward(seq, place, docs, vecs, blocks, wqkv, wo, previous):
    rows, feats = blocks[0].shape
    parts = len(blocks)
    length = rows * parts
    width = wqkv.shape[2]
    size = feats // HEADS
    heads = width // size
    scale = LOG2E * size ** (-0.5)

    seqs = docs.shape[0]

    def body(t_ref, doc_ref, vec, *rest):
        dr = doc_ref[seq : seq + 1, :].astype(F32)
        x_refs, (w_ref, wo_ref), rest = rest[:4], rest[4:6], rest[6:]
        p_refs, (saved, lse_out), rest = rest[-17:-13], rest[-13:-11], rest[-11:]
        xs, w, wov, qkv, att, lse, ps, in_sem, p_sem, c_sem, o_sem = rest
        t = t_ref[0]
        load_w = move(w_ref, w, in_sem.at[4])
        for r in range(parts):
            at = lax.bitwise_xor(jnp.int32(r), t)
            move(x_refs[r], xs.at[at], in_sem.at[at])
        load_wo = move(wo_ref, wov, in_sem.at[5])
        pending = []

        def project(i):
            pltpu.make_async_copy(x_refs[0], xs.at[i], in_sem.at[i]).wait()
            rel = lax.bitwise_xor(jnp.int32(i), t)
            pending.append(move(xs.at[i], saved.at[seq, block_at(rel, rows), pl.ds(0, feats)], c_sem.at[i]))
            x = xs[i]
            at = slice(i * rows, (i + 1) * rows)
            qkv[0, at, :] = (dot(x, w[0]) + vec[:, :width]).astype(BF16)
            qkv[1, at, :] = dot(x, w[1]).astype(BF16)
            qkv[2, at, :] = (dot(x, w[2]) + vec[:, width:]).astype(BF16)

        load_w.wait()
        project(0)
        load_wo.wait()
        for i in range(parts):
            if i + 1 < parts:
                project(i + 1)
            span = (i + 1) * rows
            own = slice(i * rows, span)
            same = column(dr[:, own]) == dr[:, :span]
            before = lax.broadcasted_iota(jnp.int32, (rows, span), 0) + i * rows >= lax.broadcasted_iota(
                jnp.int32, (rows, span), 1
            )
            allowed = same & before
            logs = []
            for hd in range(heads):
                cols = slice(hd * size, (hd + 1) * size)
                s = jnp.where(allowed, dot(qkv[0, own, cols], qkv[1, :span, cols], NT) * scale, NEGATIVE)
                top = jnp.max(s, axis=-1, keepdims=True)
                e = jnp.exp2(s - top)
                total = jnp.sum(e, axis=-1, keepdims=True)
                att[i, :, cols] = (dot(e.astype(BF16), qkv[2, :span, cols]) / total).astype(BF16)
                logs.append(top + jnp.log2(total))
            lse[own, :] = lane_pair(logs[0], logs[-1], rows)
            ps[i] = dot(att[i], wov[...]).astype(BF16)
            rel = lax.bitwise_xor(jnp.int32(i), t)
            send_block(p_refs, rel, ps.at[i], p_sem)
            pending.append(
                move(att.at[i], saved.at[seq, block_at(rel, rows), pl.ds(feats + 3 * width, width)], o_sem.at[i])
            )
        for c in range(3):
            pending.append(move(qkv.at[c], saved.at[seq, :, pl.ds(feats + c * width, width)], o_sem.at[parts + c]))
        pending.append(move(lse, lse_out, in_sem.at[5]))
        for copy in pending:
            copy.wait()
        wait_blocks(p_refs, ps.at[0], p_sem)

    extra = [] if previous is None else [previous]
    return kernel_call(
        body,
        (
            *[struct((rows, feats), BF16)] * 4,
            struct((2 * seqs, length, feats + 4 * width), BF16),
            struct((length, 128), F32),
        ),
        (ANY,) * 4 + (HBM,) * 2,
        [SMEM, whole(docs.shape), whole(vecs.shape)]
        + [ANY] * 4
        + [HBM] * (2 + len(extra)),
        scratch=[
            VMEM((parts, rows, feats), BF16),
            VMEM(wqkv.shape, BF16),
            VMEM(wo.shape, BF16),
            VMEM((3, length, width), BF16),
            VMEM((parts, rows, width), BF16),
            VMEM((length, 128), F32),
            VMEM((parts, rows, feats), BF16),
            DMA((6,)),
            DMA((4,)),
            DMA((4,)),
            DMA((7,)),
        ],
        flops=2 * length * feats * width * 4 + 5 * length * length * width,
        nbytes=length * feats * 8,
        trans=length * length * heads // 2,
        aliases={9: 4} if extra else None,
        name="attend_forward",
    )(place, docs, vecs, *blocks, wqkv, wo, *extra)


def attend_backward(seq, place, docs, blocks, saved, lse, wqkv, wo, previous, earlier=()):
    rows, feats = blocks[0].shape
    parts = len(blocks)
    length = rows * parts
    width = wqkv.shape[2]
    size = feats // HEADS
    heads = width // size
    root = size ** (-0.5)
    scale = LOG2E * root

    seqs = docs.shape[0]

    def body(t_ref, doc_ref, *rest):
        dr = doc_ref[seq : seq + 1, :].astype(F32)
        x_refs, (saved_ref, lse_ref, w_ref, wo_ref), rest = rest[:4], rest[4:8], rest[8:]
        p_refs, (out, sums), rest = rest[-20:-16], rest[-16:-14], rest[-14:]
        xs, w, wov, qkvv, attv, lsev, gk, gv, ga, low, ps, in_sem, p_sem, o_sem = rest
        t = t_ref[0]
        load_wo = move(wo_ref, wov, in_sem.at[4])
        for r in (3, 2, 1, 0):
            at = lax.bitwise_xor(jnp.int32(r), t)
            move(x_refs[r], xs.at[at], in_sem.at[at])
        loads = [move(lse_ref, lsev, in_sem.at[6])]
        for c in range(3):
            loads.append(move(saved_ref.at[seq, :, pl.ds(feats + c * width, width)], qkvv.at[c], in_sem.at[12 + c]))
        for i in range(parts):
            rel = lax.bitwise_xor(jnp.int32(i), t)
            att_ref = saved_ref.at[seq, block_at(rel, rows), pl.ds(feats + 3 * width, width)]
            loads.append(move(att_ref, attv.at[i], in_sem.at[8 + i]))
        load_w = move(w_ref, w, in_sem.at[7])
        pending = []

        def project(i):
            pltpu.make_async_copy(x_refs[0], xs.at[i], in_sem.at[i]).wait()
            rel = lax.bitwise_xor(jnp.int32(i), t)
            pending.append(move(xs.at[i], out.at[seq, block_at(rel, rows), pl.ds(0, feats)], o_sem.at[i]))
            ga[i] = dot(xs[i], wov[...], NT).astype(BF16)

        load_wo.wait()
        project(parts - 1)
        for copy in loads:
            copy.wait()
        load_w.wait()
        q_sum = jnp.zeros((1, width), F32)
        v_sum = jnp.zeros((1, width), F32)
        for i in reversed(range(parts)):
            if i:
                project(i - 1)
            span = (i + 1) * rows
            own = slice(i * rows, span)
            same = column(dr[:, own]) == dr[:, :span]
            before = lax.broadcasted_iota(jnp.int32, (rows, span), 0) + i * rows >= lax.broadcasted_iota(
                jnp.int32, (rows, span), 1
            )
            allowed = same & before
            for hd in range(heads):
                cols = slice(hd * size, (hd + 1) * size)
                q = qkvv[0, own, cols]
                k = qkvv[1, :span, cols]
                g = ga[i, :, cols]
                s = dot(q, k, NT) * scale - lsev[own, hd : hd + 1]
                p = jnp.exp2(jnp.where(allowed, s, NEGATIVE))
                gp = dot(g, qkvv[2, :span, cols], NT)
                row = jnp.sum(g.astype(F32) * attv[i, :, cols].astype(F32), axis=-1, keepdims=True)
                gs = (p * (gp - row)).astype(BF16)
                low[0, own, cols] = (dot(gs, k) * root).astype(BF16)
                new_k = dot(gs, q, TN)
                new_v = dot(p.astype(BF16), g, TN)
                if i == parts - 1:
                    gk[:span, cols] = new_k
                    gv[:span, cols] = new_v
                else:
                    gk[:span, cols] += new_k
                    gv[:span, cols] += new_v
            low[1, own, :] = (gk[own, :] * root).astype(BF16)
            low[2, own, :] = gv[own, :].astype(BF16)
            q_sum += jnp.sum(low[0, own, :].astype(F32), axis=0, keepdims=True)
            v_sum += jnp.sum(low[2, own, :].astype(F32), axis=0, keepdims=True)
            ps[i] = (
                dot(low[0, own, :], w[0], NT) + dot(low[1, own, :], w[1], NT) + dot(low[2, own, :], w[2], NT)
            ).astype(BF16)
            rel = lax.bitwise_xor(jnp.int32(i), t)
            send_block(p_refs, rel, ps.at[i], p_sem)
            for c in range(3):
                dst = out.at[seq, block_at(rel, rows), pl.ds(feats + c * width, width)]
                pending.append(move(low.at[c, own], dst, o_sem.at[4 + 3 * i + c]))
        sums[0:1, :] = q_sum
        sums[1:2, :] = v_sum
        for copy in pending:
            copy.wait()
        wait_blocks(p_refs, ps.at[0], p_sem)

    extra = [] if previous is None else [previous]
    return kernel_call(
        body,
        (
            *[struct((rows, feats), BF16)] * 4,
            struct((2 * seqs, length, feats + 4 * width), BF16),
            struct((2, width), F32),
        ),
        (ANY,) * 4 + (HBM, whole((2, width))),
        [SMEM, whole(docs.shape)] + [ANY] * 4 + [HBM] * (4 + len(extra)) + [ANY] * len(earlier),
        scratch=[
            VMEM((parts, rows, feats), BF16),
            VMEM(wqkv.shape, BF16),
            VMEM(wo.shape, BF16),
            VMEM((3, length, width), BF16),
            VMEM((parts, rows, width), BF16),
            VMEM((length, 128), F32),
            VMEM((length, width), F32),
            VMEM((length, width), F32),
            VMEM((parts, rows, width), BF16),
            VMEM((3, length, width), BF16),
            VMEM((parts, rows, feats), BF16),
            DMA((15,)),
            DMA((4,)),
            DMA((16,)),
        ],
        flops=2 * length * feats * width * 4 + 10 * length * length * width,
        nbytes=length * feats * 8,
        trans=length * length * heads // 2,
        aliases={10: 4} if extra else None,
        name="attend_backward",
    )(place, docs, *blocks, saved, lse, wqkv, wo, *extra, *earlier)


ORDER = (3, 1, 2, 0)


ROWS, ACT, SLOPE, GRAD = range(4)


def feed_forward(seq, seqs, blocks, vecs, w_up, w_down, previous):
    rows, feats = blocks[0].shape
    parts = len(blocks)
    length = rows * parts
    units = w_up.shape[1]
    root = math.sqrt(2.0 / math.pi)

    def body(vec, *rest):
        x_refs, (up_ref, down_ref), rest = rest[:4], rest[4:6], rest[6:]
        p_refs, saved, rest = rest[-15:-11], rest[-11], rest[-10:]
        xs, up, down, u, act, slope, ps, in_sem, p_sem, o_sem = rest
        load_up = move(up_ref, up, in_sem.at[4])
        loads = {r: move(x_refs[r], xs.at[r], in_sem.at[r]) for r in ORDER}
        load_down = move(down_ref, down, in_sem.at[5])
        pending = []

        def project(k):
            r = ORDER[k]
            loads[r].wait()
            pending.append(move(xs.at[r], saved.at[ROWS, seq, pl.ds(r * rows, rows)], o_sem.at[r]))
            u[k % 2] = dot(xs[r], up[...]) + vec[...]

        load_up.wait()
        project(0)
        load_down.wait()
        for k, r in enumerate(ORDER):
            if k + 1 < parts:
                project(k + 1)
            v = u[k % 2]
            sq = v * v
            th = jnp.tanh(v * (root + (root * 0.044715) * sq))
            half = 0.5 + 0.5 * th
            g = (v * half).astype(BF16)
            act[r] = g
            slope[r] = (half + v * (1.0 - th * th) * (0.5 * root + (1.5 * 0.044715 * root) * sq)).astype(BF16)
            ps[r] = dot(g, down[...]).astype(BF16)
            at = pl.ds(r * rows, rows)
            pending.append(move(ps.at[r], p_refs[r], p_sem.at[r]))
            pending.append(move(act.at[r], saved.at[ACT, seq, at], o_sem.at[4 + r]))
            pending.append(move(slope.at[r], saved.at[SLOPE, seq, at], o_sem.at[8 + r]))
        for copy in pending:
            copy.wait()

    extra = [] if previous is None else [previous]
    return kernel_call(
        body,
        (
            *[struct((rows, feats), BF16)] * 4,
            struct((4, seqs, length, units), BF16),
        ),
        (ANY,) * 4 + (HBM,),
        [whole(vecs.shape)] + [ANY] * 4 + [HBM] * (2 + len(extra)),
        scratch=[
            VMEM((parts, rows, feats), BF16),
            VMEM(w_up.shape, BF16),
            VMEM(w_down.shape, BF16),
            VMEM((2, rows, units), F32),
            VMEM((parts, rows, units), BF16),
            VMEM((parts, rows, units), BF16),
            VMEM((parts, rows, feats), BF16),
            DMA((6,)),
            DMA((4,)),
            DMA((12,)),
        ],
        flops=4 * length * feats * units,
        nbytes=length * feats * 14,
        trans=length * units,
        aliases={7: 4} if extra else None,
        name="feed_forward",
    )(vecs, *blocks, w_up, w_down, *extra)


def feed_backward(seq, own, got, saved, w_up, w_down, earlier):
    rows, feats = own.shape[1:]
    parts = 4
    length = rows * parts
    units = w_up.shape[1]
    seqs = saved.shape[1]

    def body(own_ref, got_ref, saved_ref, up_ref, down_ref, *rest):
        p_refs, (grad_out, sums), rest = rest[-16:-12], rest[-12:-10], rest[-10:]
        ys, up, down, slopes, u, grad, ps, in_sem, p_sem, o_sem = rest
        load_down = move(down_ref, down, in_sem.at[4])
        loads, slope_loads = {}, {}
        for r in ORDER:
            loads[r] = move((got_ref if r % 2 else own_ref).at[r // 2], ys.at[r], in_sem.at[r])
            slope_loads[r] = move(saved_ref.at[SLOPE, seq, pl.ds(r * rows, rows)], slopes.at[r], in_sem.at[6 + r])
        load_up = move(up_ref, up, in_sem.at[5])
        pending = []

        def project(k):
            r = ORDER[k]
            loads[r].wait()
            slope_loads[r].wait()
            u[k % 2] = dot(ys[r], down[...], NT)

        load_down.wait()
        project(0)
        load_up.wait()
        total = jnp.zeros((8, units), F32)
        for k, r in enumerate(ORDER):
            if k + 1 < parts:
                project(k + 1)
            gu = (u[k % 2] * slopes[r].astype(F32)).astype(BF16)
            grad[r] = gu
            total += jnp.sum(gu.astype(F32).reshape(rows // 8, 8, units), axis=0)
            ps[r] = dot(gu, up[...], NT).astype(BF16)
            pending.append(move(ps.at[r], p_refs[r], p_sem.at[r]))
            pending.append(move(grad.at[r], grad_out.at[GRAD, seq, pl.ds(r * rows, rows)], o_sem.at[4 + r]))
        sums[...] = jnp.sum(total, axis=0, keepdims=True)
        for copy in pending:
            copy.wait()

    return kernel_call(
        body,
        (
            *[struct((rows, feats), BF16)] * 4,
            struct((4, seqs, length, units), BF16),
            struct((1, units), F32),
        ),
        (ANY,) * 4 + (HBM, whole((1, units))),
        [ANY] * 2 + [HBM] * 3 + [ANY] * len(earlier),
        scratch=[
            VMEM((parts, rows, feats), BF16),
            VMEM(w_up.shape, BF16),
            VMEM(w_down.shape, BF16),
            VMEM((parts, rows, units), BF16),
            VMEM((2, rows, units), F32),
            VMEM((parts, rows, units), BF16),
            VMEM((parts, rows, feats), BF16),
            DMA((10,)),
            DMA((4,)),
            DMA((8,)),
        ],
        flops=4 * length * feats * units,
        nbytes=length * feats * 14,
        aliases={2: 4},
        name="feed_backward",
    )(own, got, saved, w_up, w_down, *earlier)


def entries(ref, seq, part, place, rows):
    at = lax.bitwise_xor(jnp.int32(part), place) * rows
    return ref[seq : seq + 1, pl.ds(pl.multiple_of(at, rows), rows)].astype(F32)


def contrast_scores(place, ends, docs, labels, units):
    rows, feats = units[0].shape[0] - EXTRA, units[0].shape[1]
    factor = CONTRAST_SCALE / feats * LOG2E
    count = len(units)
    seqs = count // 4

    def body(t_ref, end_ref, doc_ref, lab_ref, *rest):
        refs, rest = rest[:count], rest[count:]
        exp_out, col_out, row_out, loss_out, both, exps, sums, in_sem, out_sem = rest
        t = t_ref[0]
        loads = [move(refs[k].at[pl.ds(0, rows)], both.at[k], in_sem.at[k]) for k in range(count)]
        for copy in loads:
            copy.wait()
        pending = []
        for s in range(4):
            seq, part = s // 2, s % 2 * 2
            own_lab = column(entries(lab_ref, seq, part, t, rows))

            def block(k, own_doc, seq=seq, part=part, s=s, own_lab=own_lab):
                e = jnp.exp2(dot(both[seq * 4 + part], both[k], NT) * factor)
                if own_doc is not None:
                    e = jnp.where(own_doc != entries(doc_ref, seq, k % 4, t, rows), e, 0.0)
                exps[s, :, k * rows : (k + 1) * rows] = e.astype(BF16)
                picked = jnp.where(own_lab == entries(lab_ref, k // 4, k % 4, t, rows), e, 0.0)
                lanes = [slice(c * 128, (c + 1) * 128) for c in range(rows // 128)]
                fold = lambda v: functools.reduce(jnp.add, [v[:, lane] for lane in lanes])
                return fold(e), fold(picked)

            terms = [block(k, None) for k in range(count) if k // 4 != seq]
            sums[0] = functools.reduce(jnp.add, [a for a, _ in terms])
            sums[1] = functools.reduce(jnp.add, [b for _, b in terms])
            single = end_ref[seq, 0] == end_ref[seq, 1]
            inner = slice(seq * 4 * rows, (seq + 1) * 4 * rows)

            @pl.when(single)
            def _(s=s, inner=inner):
                exps[s, :, inner] = jnp.zeros((rows, 4 * rows), BF16)

            @pl.when(jnp.logical_not(single))
            def _(seq=seq, part=part, block=block):
                own_doc = column(entries(doc_ref, seq, part, t, rows))
                for k in range(seq * 4, seq * 4 + 4):
                    a, b = block(k, own_doc)
                    sums[0] += a
                    sums[1] += b

            pending.append(move(exps.at[s], exp_out.at[s], out_sem.at[s]))
            wide = lane_pair(
                jnp.sum(sums[0], axis=-1, keepdims=True), jnp.sum(sums[1], axis=-1, keepdims=True), rows
            )
            col_out[s * rows : (s + 1) * rows, :] = wide
            flat = jnp.transpose(wide)[:8, :]
            row_out[:, s * rows : (s + 1) * rows] = flat
            if part == 0:
                logs = jnp.log(flat)
                loss_out[seq : seq + 1, :] = logs[0:1] - logs[1:2]
        for copy in pending:
            copy.wait()

    return kernel_call(
        body,
        (
            struct((16, rows, count * rows), BF16),
            struct((4 * rows, 128), F32),
            struct((8, 4 * rows), F32),
            struct((seqs, rows), F32),
        ),
        (HBM, whole((4 * rows, 128)), whole((8, 4 * rows)), whole((seqs, rows))),
        [SMEM, SMEM, whole(docs.shape), whole(labels.shape)] + [ANY] * count,
        scratch=[
            VMEM((count, rows, feats), BF16),
            VMEM((4, rows, count * rows), BF16),
            VMEM((2, rows, 128), F32),
            DMA((count,)),
            DMA((4,)),
        ],
        flops=2 * 4 * rows * count * rows * feats,
        nbytes=count * rows * feats * 4,
        trans=4 * rows * count * rows,
        name="contrast_scores",
    )(place, ends, docs, labels, *units)


def contrast_grads(seq, place, ends, labels, units, exps, col_sums, row_own, row_got, cot, cot_got):
    rows, feats = units[0].shape[0] - EXTRA, units[0].shape[1]
    factor = CONTRAST_SCALE / feats
    count = len(units)
    span = 4 * rows

    def body(t_ref, end_ref, lab_ref, col, own, got, *rest):
        refs, (e_ref, cot_ref, other_ref), rest = rest[:count], rest[count : count + 3], rest[count + 3 :]
        full, low, both, exps, scales, cots, grad, gn, full_v, low_v, in_sem, e_sem, q_sem, c_sem, o_sem = rest
        t = t_ref[0]
        order = [k for k in range(count) if k // 4 != seq] + [k for k in range(count) if k // 4 == seq]
        e_loads = [move(e_ref.at[2 * seq + h], exps.at[h], e_sem.at[h]) for h in range(2)]
        loads = {
            k: move(refs[k].at[pl.ds(0, rows)], both.at[pl.ds(k * rows, rows)], in_sem.at[k]) for k in order
        }
        small = [
            (
                move(refs[seq * 4 + h * 2].at[pl.ds(rows, EXTRA)], scales.at[h], q_sem.at[h]),
                move(other_ref if h else cot_ref.at[seq], cots.at[h], c_sem.at[h]),
            )
            for h in range(2)
        ]
        single = end_ref[seq, 0] == end_ref[seq, 1]

        def weigh(h, blocks):
            s = 2 * seq + h
            own_lab = column(entries(lab_ref, seq, h * 2, t, rows))
            inv = CONTRAST_WEIGHT / col[s * rows : (s + 1) * rows, :]
            all_i, pos_i = inv[:, 0:1], inv[:, 1:2]
            for k in blocks:
                other, piece = k // 4, k % 4
                source = own if piece % 2 == 0 else got
                at = (other * 2 + piece // 2) * rows
                inv_j = CONTRAST_WEIGHT / source[0:2, at : at + rows]
                same = own_lab == entries(lab_ref, other, piece, t, rows)
                coef = (all_i + inv_j[0:1]) - jnp.where(same, pos_i + inv_j[1:2], 0.0)
                cols = slice(k * rows, (k + 1) * rows)
                grad[h, :, cols] = (exps[h, :, cols].astype(F32) * coef).astype(BF16)

        outer = slice((1 - seq) * span, (2 - seq) * span)
        inner = slice(seq * span, (seq + 1) * span)
        for h in range(2):
            e_loads[h].wait()
        weigh(0, order[:4])
        for k in order:
            loads[k].wait()
        for h in range(2):
            if h == 0:
                weigh(1, order[:4])
            gn[h] = dot(grad[h, :, outer], both[outer, :])

        @pl.when(jnp.logical_not(single))
        def _():
            for h in range(2):
                weigh(h, order[4:])
                gn[h] += dot(grad[h, :, inner], both[inner, :])

        pending = []
        for h in range(2):
            first = (seq * 4 + h * 2) * rows
            n = both[first : first + rows, :].astype(F32)
            g = gn[h] * factor
            change = g - n * jnp.mean(g * n, axis=-1, keepdims=True)
            for copy in small[h]:
                copy.wait()
            pieces = scales[h, :, :rows].astype(F32)
            gy = cots[h].astype(F32) + column(pieces[0:1] + pieces[1:2]) * change
            low_v[h] = gy.astype(BF16)
            pending.append(move(low_v.at[h], low.at[h], o_sem.at[h]))
            if h == 0:
                full_v[...] = gy
                pending.append(move(full_v, full, o_sem.at[2]))
        for copy in pending:
            copy.wait()

    return kernel_call(
        body,
        (struct((rows, feats), F32), struct((2, rows, feats), BF16)),
        (ANY,) * 2,
        [
            SMEM,
            SMEM,
            whole(labels.shape),
            whole((4 * rows, 128)),
            whole((8, 4 * rows)),
            whole((8, 4 * rows)),
        ]
        + [ANY] * count
        + [HBM] * 2
        + [ANY],
        scratch=[
            VMEM((count * rows, feats), BF16),
            VMEM((2, rows, count * rows), BF16),
            VMEM((2, EXTRA, feats), BF16),
            VMEM((2, rows, feats), BF16),
            VMEM((2, rows, count * rows), BF16),
            VMEM((2, rows, feats), F32),
            VMEM((rows, feats), F32),
            VMEM((2, rows, feats), BF16),
            DMA((count,)),
            DMA((2,)),
            DMA((2,)),
            DMA((2,)),
            DMA((3,)),
        ],
        flops=4 * rows * count * rows * feats,
        nbytes=count * rows * feats * 4,
        name="contrast_grads",
    )(place, ends, labels, col_sums, row_own, row_got, *units, exps, cot, cot_got)


def down_grad(saved, own, got):
    seqs, length, units = saved.shape[1:]
    rows, feats = own[0].shape[1:]
    tiles = units // TILE

    def body(a_ref, *rest):
        own_refs, got_refs = rest[:seqs], rest[seqs : 2 * seqs]
        out_ref, a, b, out, a_sem, b_sem, o_sem = rest[2 * seqs :]
        b_loads = []
        for s in range(seqs):
            for r in range(4):
                src = (got_refs if r % 2 else own_refs)[s].at[r // 2]
                b_loads.append(move(src, b.at[s, pl.ds(r * rows, rows)], b_sem.at[4 * s + r]))
        columns = [pl.ds(i * TILE, TILE) for i in range(tiles)]
        a_loads = [move(a_ref.at[ACT, :, :, columns[i]], a.at[i], a_sem.at[i]) for i in range(tiles)]
        for copy in b_loads:
            copy.wait()
        stores = []
        for i in range(tiles):
            a_loads[i].wait()
            out[i] = functools.reduce(jnp.add, [dot(a[i, s], b[s], TN) for s in range(seqs)]).astype(BF16)
            stores.append(move(out.at[i], out_ref.at[columns[i]], o_sem.at[i]))
        for copy in stores:
            copy.wait()

    return kernel_call(
        body,
        struct((units, feats), BF16),
        ANY,
        [HBM] + [ANY] * (2 * seqs),
        scratch=[
            VMEM((tiles, seqs, length, TILE), BF16),
            VMEM((seqs, length, feats), BF16),
            VMEM((tiles, TILE, feats), BF16),
            DMA((tiles,)),
            DMA((4 * seqs,)),
            DMA((tiles,)),
        ],
        flops=2 * seqs * length * units * feats,
        nbytes=4 * seqs * length * feats,
        name="down_grad",
    )(saved, *own, *got)


TILE = 256


def send_half(tile, tiles, high, src, to_other, kept, at, sem):
    upper = tile >= tiles // 2
    rows = pl.ds((tile % (tiles // 2)) * TILE, TILE)

    @pl.when(high == int(upper))
    def _():
        pltpu.make_async_copy(src, kept.at[rows, at], sem).start()

    @pl.when(high != int(upper))
    def _():
        pltpu.make_async_copy(src, to_other.at[rows, at], sem).start()

    return pltpu.make_async_copy(src, kept.at[rows, at], sem)


def weight_grad(saved, flags, bit):
    seqs, length, out_rows = saved.shape[1:]
    cols = out_rows
    tiles = out_rows // TILE

    def body(flag, s_ref, other_ref, kept_ref, a, b, out, a_sem, b_sem, o_sem):
        b_loads = [move(s_ref.at[GRAD, s], b.at[s], b_sem.at[s]) for s in range(seqs)]
        columns = [pl.ds(i * TILE, TILE) for i in range(tiles)]
        a_loads = [move(s_ref.at[ROWS, :, :, columns[i]], a.at[i], a_sem.at[i]) for i in range(tiles)]
        for copy in b_loads:
            copy.wait()
        stores = []
        for i in range(tiles):
            a_loads[i].wait()
            out[i] = functools.reduce(jnp.add, [dot(a[i, s], b[s], TN) for s in range(seqs)]).astype(BF16)
            stores.append(
                send_half(i, tiles, flag[bit], out.at[i], other_ref, kept_ref, pl.ds(0, cols), o_sem.at[i])
            )
        for copy in stores:
            copy.wait()

    return kernel_call(
        body,
        (struct((out_rows // 2, cols), BF16),) * 2,
        (ANY,) * 2,
        [pl.BlockSpec(memory_space=pltpu.SMEM)] + [HBM],
        scratch=[
            VMEM((tiles, seqs, length, TILE), BF16),
            VMEM((seqs, length, cols), BF16),
            VMEM((tiles, TILE, cols), BF16),
            DMA((tiles,)),
            DMA((seqs,)),
            DMA((tiles,)),
        ],
        flops=2 * seqs * length * out_rows * cols,
        nbytes=4 * seqs * length * cols,
        name="weight_grad",
    )(flags, saved)


def head_terms(seq, s_ref, h_ref, feats, width, a, g, r, a_sem, g_sem, r_sem):
    tiles = feats // width
    columns = [pl.ds(i * width, width) for i in range(tiles)]
    a_load = lambda i: move(s_ref.at[seq, :, columns[i]], a.at[i], a_sem.at[i])
    r_load = lambda i: move(h_ref.at[seq, :, columns[i]], r.at[i], r_sem.at[i])
    g_load = lambda n: move(
        (s_ref if n == 3 else h_ref).at[seq, :, pl.ds(feats + n * width, width)], g.at[n], g_sem.at[n]
    )
    a_loads = [a_load(0)]
    g_loads = [g_load(n) for n in range(4)]
    r_loads = [r_load(0)]
    for i in range(1, tiles):
        a_loads.append(a_load(i))
        r_loads.append(r_load(i))

    def tile(i):
        a_loads[i].wait()
        values = []
        for n in range(3):
            if i == 0:
                g_loads[n].wait()
            values.append(dot(a[i], g[n], TN))
        if i == 0:
            g_loads[3].wait()
        r_loads[i].wait()
        values.append(dot(g[3], r[i], TN))
        return values

    return tile, columns


def head_scratch(length, feats, width):
    tiles = feats // width
    return [
        VMEM((tiles, length, width), BF16),
        VMEM((4, length, width), BF16),
        VMEM((tiles, length, width), BF16),
        DMA((tiles,)),
        DMA((4,)),
        DMA((tiles,)),
    ]


def head_part(saved, grads, feats):
    length = saved.shape[1]
    width = (saved.shape[2] - feats) // 4
    tiles = feats // width

    def body(s_ref, h_ref, out_ref, a, g, r, a_sem, g_sem, r_sem, out, o_sem):
        tile, _ = head_terms(0, s_ref, h_ref, feats, width, a, g, r, a_sem, g_sem, r_sem)
        stores = []
        for i in range(tiles):
            for n, value in enumerate(tile(i)):
                out[i, :, n * width : (n + 1) * width] = value
            stores.append(move(out.at[i], out_ref.at[i], o_sem.at[i]))
        for copy in stores:
            copy.wait()

    return kernel_call(
        body,
        struct((tiles, width, 4 * width), F32),
        ANY,
        [HBM] * 2,
        scratch=head_scratch(length, feats, width) + [VMEM((tiles, width, 4 * width), F32), DMA((tiles,))],
        flops=8 * length * feats * width,
        nbytes=4 * length * feats,
        name="head_part",
    )(saved, grads)


def head_grads(saved, grads, part, feats, flags, bits):
    length = saved.shape[1]
    width = (saved.shape[2] - feats) // 4
    tiles = feats // width

    def body(flag, s_ref, h_ref, part_ref, *refs):
        first_refs, second_refs = refs[:2], refs[2:4]
        a, g, r, a_sem, g_sem, r_sem, old, first, second, p_sem, o_sem = refs[4:]
        tile, columns = head_terms(1, s_ref, h_ref, feats, width, a, g, r, a_sem, g_sem, r_sem)
        p_loads = [move(part_ref.at[i], old.at[i], p_sem.at[i]) for i in range(tiles)]
        stores = []
        for i in range(tiles):
            values = tile(i)
            p_loads[i].wait()
            for n, value in enumerate(values):
                total = value + old[i, :, n * width : (n + 1) * width]
                (first, second)[n // 2][i, :, n % 2 * width : (n % 2 + 1) * width] = total.astype(BF16)
            for n, (src, outs) in enumerate(((first, first_refs), (second, second_refs))):
                stores.append(
                    send_half(i, tiles, flag[bits[n]], src.at[i], *outs, pl.ds(0, 2 * width), o_sem.at[2 * i + n])
                )
        for copy in stores:
            copy.wait()

    return kernel_call(
        body,
        (struct((feats // 2, 2 * width), BF16),) * 4,
        (ANY,) * 4,
        [SMEM] + [HBM] * 2 + [ANY],
        scratch=head_scratch(length, feats, width)
        + [
            VMEM((tiles, width, 4 * width), F32),
            VMEM((tiles, width, 2 * width), BF16),
            VMEM((tiles, width, 2 * width), BF16),
            DMA((tiles,)),
            DMA((2 * tiles,)),
        ],
        flops=8 * length * feats * width,
        nbytes=4 * length * feats,
        name="head_grads",
    )(flags, saved, grads, part)


def halve_step(flags, bit, keep, got):
    rows, cols = keep.shape
    half = rows // 2

    def body(flag, k_ref, g_ref, *outs):
        if bit is None:
            outs[0][...] = (k_ref[...].astype(F32) + g_ref[...].astype(F32)).astype(BF16)
            return
        for high in (0, 1):

            @pl.when(flag[bit] == high)
            def _(high=high):
                for out, upper in ((outs[0], 1 - high), (outs[1], high)):
                    at = slice(upper * half, (upper + 1) * half)
                    out[...] = (k_ref[at, :].astype(F32) + g_ref[at, :].astype(F32)).astype(BF16)

    shape = (rows, cols) if bit is None else (half, cols)
    return kernel_call(
        body,
        (struct(shape, BF16),) * (1 if bit is None else 2),
        (whole(shape),) * (1 if bit is None else 2),
        [pl.BlockSpec(memory_space=pltpu.SMEM)] + [whole((rows, cols))] * 2,
        nbytes=rows * cols * 6,
        limit=SMALL,
        name="halve_step",
    )(flags, keep, got)


def join_step(flags, bit, own, got, dtype):
    rows, cols = own.shape
    steps = 2 if dtype == F32 else 1
    part = rows // steps

    def body(flag, own_ref, got_ref, out):
        for high in (0, 1):

            @pl.when(flag[bit] == high)
            def _(high=high):
                out[high] = own_ref[...].astype(dtype)
                out[1 - high] = got_ref[...].astype(dtype)

    block = pl.BlockSpec((part, cols), lambda i: (i, 0))
    return kernel_call(
        body,
        struct((2, rows, cols), dtype),
        pl.BlockSpec((2, part, cols), lambda i: (0, i, 0)),
        [pl.BlockSpec(memory_space=pltpu.SMEM), block, block],
        grid=(steps,),
        nbytes=rows * cols * 8,
        limit=SMALL,
        name="join_step",
    )(flags, own, got).reshape(2 * rows, cols)


def part_outputs(parts, order):
    rows, cols = parts.shape
    step = rows >> len(order)

    def place(i):
        return functools.reduce(
            jnp.add, [((i >> bit) & 1) << (len(order) - 1 - n) for n, bit in enumerate(order)]
        )

    def body(part, out):
        out[...] = part[...].astype(F32)

    return kernel_call(
        body,
        struct((rows, cols), F32),
        pl.BlockSpec((step, cols), lambda i: (place(i), 0)),
        [pl.BlockSpec((step, cols), lambda i: (i, 0))],
        grid=(1 << len(order),),
        nbytes=6 * rows * cols,
        limit=SMALL,
        name="part_outputs",
    )(parts)


def head_outputs(flags, bits, first, second):
    feats = 2 * first[0].shape[0]
    width = first[0].shape[1] // 2
    tile = width

    def body(h_ref, a_ref, b_ref, c_ref, d_ref, qkv, out):
        mine = (lax.div(pl.program_id(0) * tile, feats // 2) == h_ref[bits[0]])

        for case, x in ((True, a_ref), (False, b_ref)):
            @pl.when(mine == case)
            def _(x=x):
                qkv[0] = x[:, :width].astype(F32)
                qkv[1] = x[:, width:].astype(F32)

        mine_two = (lax.div(pl.program_id(0) * tile, feats // 2) == h_ref[bits[1]])
        for case, y in ((True, c_ref), (False, d_ref)):
            @pl.when(mine_two == case)
            def _(y=y):
                qkv[2] = y[:, :width].astype(F32)
                out[...] = y[:, width:].astype(F32)

    half = pl.BlockSpec((tile, 2 * width), lambda i, h: (lax.rem(i, feats // 2 // tile), 0))
    return kernel_call(
        body,
        (struct((3, feats, width), F32), struct((width, feats), F32)),
        (pl.BlockSpec((3, tile, width), lambda i, h: (0, i, 0)), pl.BlockSpec((width, tile), lambda i, h: (0, i))),
        [half] * 4,
        grid=(feats // tile,),
        nbytes=10 * feats * width * 4,
        prefetch=1,
        limit=SMALL,
        name="head_outputs",
    )(flags, *first, *second)


def swap(value, axis, size, bit):
    return lax.ppermute(value, axis, [(i, i ^ bit) for i in range(size)])


CORE, CROSS = 1, 2


def tensor_swap(value, bit):
    return swap(value, "tensor", 4, bit)


def tie(value, *earlier):
    return lax.optimization_barrier((value, *earlier))[0] if earlier else value


class Gather:
    def __init__(self, value):
        self.value = value
        self.cross = tensor_swap(value, CROSS)
        self.core = tensor_swap(value, CORE)

    def blocks(self, *earlier):
        return [self.value, self.core, self.cross, tensor_swap(tie(self.cross, *earlier), CORE)]


class Scatter:
    def __init__(self, blocks):
        self.own, self.other = blocks[0], blocks[2]
        self.core_other = tensor_swap(blocks[3], CORE)
        self.core_own = tensor_swap(blocks[1], CORE)
        self.mark = blocks[3]

    def cross(self, *earlier):
        block = (tie(self.other, *earlier).astype(F32) + self.core_other.astype(F32)).astype(BF16)
        self.parts = (self.own, self.core_own, tensor_swap(block, CROSS))
        return block


class DpSum:
    def __init__(self, send, keep, flags, size, order):
        self.send, self.value, self.flags, self.size = send, keep, flags, size
        self.left = [(bit, True) for bit in order] + [(bit, False) for bit in reversed(order)]
        self.got, self.now = None, None

    def advance(self, *earlier):
        if self.now is not None and self.now[1]:
            more = self.left and self.left[0][1]
            parts = halve_step(self.flags, self.left[0][0] if more else None, tie(self.value, *earlier), self.got)
            self.send, self.value = parts if more else (parts[0], parts[0])
        elif self.now is not None:
            self.send = self.value = join_step(self.flags, self.now[0], tie(self.value, *earlier), self.got, BF16)
        self.now = self.left.pop(0)
        self.got = swap(self.send, "dp", self.size, 1 << self.now[0])
        return self.send

    def halves(self):
        return self.value, self.got


def shards(
    dp_size,
    tokens,
    doc_ids,
    targets,
    cotangent,
    ln1_gain,
    ln1_bias,
    qkv_weight,
    query_bias,
    value_bias,
    output_weight,
    out_bias,
    ln2_gain,
    ln2_bias,
    up_weight,
    up_bias,
    down_weight,
    down_bias,
):
    seqs, rows, feats = tokens.shape
    length = doc_ids.shape[1]
    parts = length // rows
    me = lax.axis_index("tensor")
    place = me.reshape(1).astype(jnp.int32)
    vec = lambda v: v.astype(F32).reshape(1, -1)
    gain_one, shift_one, gain_two, shift_two = vec(ln1_gain), vec(ln1_bias), vec(ln2_gain), vec(ln2_bias)
    out_offset, down_offset, up_shift = vec(out_bias), vec(down_bias), vec(up_bias)
    head_shift = vec(jnp.concatenate([query_bias, value_bias]))
    ends = doc_ids[:, :: length - 1]

    fine = 16
    paired = (jnp.arange(feats, dtype=jnp.int32) // 2).astype(F32)
    freq = jnp.exp(paired * (-2.0 * math.log(10000.0) / feats))[None, :]
    odd = (jnp.arange(feats, dtype=jnp.int32) % 2 == 1)[None, :]
    coarse_at = (me * rows + fine * jnp.arange(rows // fine, dtype=jnp.int32)).astype(F32)[:, None] * freq
    fine_at = jnp.arange(fine, dtype=jnp.int32).astype(F32)[:, None] * freq
    sin_a, cos_a = jnp.sin(coarse_at), jnp.cos(coarse_at)
    tables = (jnp.where(odd, cos_a, sin_a), jnp.where(odd, -sin_a, cos_a), jnp.cos(fine_at), jnp.sin(fine_at))

    hidden, stream, grad_r = [None] * 2, [None] * 2, [None] * 2
    kept, up_sums, head_sums, sums_one, sums_two = [None] * 2, [None] * 2, [None] * 2, [None] * 2, [None] * 2
    shared = {"attend": None, "feed": None, "act": None, "heads": None, "input": None}

    def attend(s, gathered, *earlier):
        *blocks, shared["attend"], kept[s] = attend_forward(
            s, tie(place, *earlier), doc_ids, head_shift, gathered, qkv_weight, output_weight, shared["attend"]
        )
        return Scatter(blocks)

    def middle_rows(s, scatter, *earlier):
        stream[s], normed = second_norm(hidden[s], scatter.parts, tie(out_offset, *earlier), gain_two, shift_two)
        return normed, Gather(normed)

    def feed(s, gathered, *earlier):
        *blocks, shared["feed"] = feed_forward(
            s, seqs, gathered, tie(up_shift, *earlier), up_weight, down_weight, shared["feed"]
        )
        return Scatter(blocks)

    def last_rows(s, scatter, *earlier):
        shared["act"], unit = output_rows(
            s, seqs, stream[s], scatter.parts, tie(down_offset, *earlier), shared["act"]
        )
        return unit, Gather(unit)

    hidden[0], normed_a = first_norm(0, tokens, tables, gain_one, shift_one)
    rows_a = Gather(normed_a)
    hidden[1], normed_b = first_norm(1, tie(tokens, normed_a, head_shift), tables, gain_one, shift_one)
    rows_b = Gather(normed_b)
    at_a = attend(0, rows_a.blocks(normed_b))
    block = at_a.cross(rows_b.cross)
    at_b = attend(1, rows_b.blocks(), block)
    normed, rows_a = middle_rows(0, at_a, at_b.mark)
    block = at_b.cross(normed)
    ff_a = feed(0, rows_a.blocks(), block)
    normed, rows_b = middle_rows(1, at_b, ff_a.mark)
    block = ff_a.cross(normed)
    ff_b = feed(1, rows_b.blocks(), block)
    unit, units_a = last_rows(0, ff_a, ff_b.mark)
    block = ff_b.cross(unit)
    cot_rows = [cotangent[s] for s in range(2)]
    unit, units_b = last_rows(1, ff_b, block, *cot_rows)
    cots = [tensor_swap(tie(cot_rows[s], unit), CROSS) for s in range(2)]

    units = units_a.blocks() + units_b.blocks()
    exps, col_sums, row_sums, loss = contrast_scores(place, ends, doc_ids, targets, units)
    row_got = tensor_swap(row_sums, CORE)
    grad_y, low_y, got_y = [None] * 2, [None] * 2, [None] * 2
    for s in range(2):
        grad_y[s], low_y[s] = contrast_grads(
            s, tie(place, *low_y[:s]), ends, targets, units, exps, col_sums, row_sums, row_got, cotangent, cots[s]
        )
        got_y[s] = tensor_swap(tie(low_y[s], cots[1]), CORE)

    def feed_back(s, *earlier):
        *blocks, shared["feed"], up_sums[s] = feed_backward(
            s, low_y[s], got_y[s], shared["feed"], up_weight, down_weight, earlier
        )
        return Scatter(blocks)

    def middle_back(s, scatter, *earlier):
        grad_r[s], low, sums_two[s] = norm_backward(
            s, seqs, stream[s], scatter.parts, tie(gain_two, *earlier), grad_y[s], False, None
        )
        return low, Gather(low)

    def attend_back(s, gathered, *earlier, after=()):
        *blocks, shared["heads"], head_sums[s] = attend_backward(
            s, tie(place, *earlier), doc_ids, gathered, shared["attend"], kept[s], qkv_weight, output_weight,
            shared["heads"], after,
        )
        return Scatter(blocks)

    def first_back(s, scatter, *earlier):
        shared["input"], sums_one[s] = norm_backward(
            s, seqs, hidden[s], scatter.parts, tie(gain_one, *earlier), grad_r[s], True, shared["input"]
        )
        return sums_one[s]

    bits = list(range(dp_size.bit_length() - 1))
    other_bits = bits[1::-1] + bits[2:]
    flags = (lax.axis_index("dp") >> jnp.arange(len(bits), dtype=jnp.int32)) & 1
    grad_down_w = down_grad(shared["feed"], low_y, got_y)
    down_part = lax.psum_scatter(grad_down_w, "dp", scatter_dimension=0, tiled=True)
    fb_a = feed_back(0, grad_down_w)
    fb_b = feed_back(1, fb_a.cross())
    low, rows_a = middle_back(0, fb_a, fb_b.mark)
    block = fb_b.cross(low)
    up_sum = DpSum(*weight_grad(tie(shared["feed"], block), flags, bits[0]), flags, dp_size, bits)
    sent = up_sum.advance()
    ab_a = attend_back(0, rows_a.blocks(sent), sent)
    low, rows_b = middle_back(1, fb_b, ab_a.mark)
    block = ab_a.cross(low)
    part = head_part(tie(shared["attend"], block), shared["heads"], feats)
    sent = up_sum.advance(part, rows_b.cross)
    ab_b = attend_back(1, rows_b.blocks(sent), sent, down_part, after=(part,))
    down_all = lax.all_gather(tie(down_part, sent), "dp", axis=0, tiled=True)
    sent = up_sum.advance(ab_b.mark)
    sums = first_back(0, ab_a, sent)
    block = ab_b.cross(sums)
    first_send, first_keep, second_send, second_keep = head_grads(
        tie(shared["attend"], block), shared["heads"], part, feats, flags, (bits[0], other_bits[0])
    )
    first = DpSum(first_send, first_keep, flags, dp_size, bits)
    second = DpSum(second_send, second_keep, flags, dp_size, other_bits)
    sent = (first.advance(), second.advance())
    sums = first_back(1, ab_b, *sent)
    sent = (sums,)

    total = lambda items: functools.reduce(jnp.add, items)
    heads_sum = total(head_sums)
    heads_row = jnp.pad(heads_sum.reshape(1, -1), ((0, 0), (0, feats - heads_sum.size)))
    small = jnp.concatenate([total(sums_one)[:2], total(sums_two), total(up_sums), heads_row])
    swaps = [("tensor", 4, CROSS)] + [("dp", dp_size, 1 << bit) for bit in bits] + [("tensor", 4, CORE)]
    shared_rows = (jnp.arange(small.shape[0]) < 6).astype(F32)[:, None]
    axis, size, bit = swaps.pop(0)
    arriving = swap(small, axis, size, bit)
    sent = ()
    while first.left or arriving is not None or up_sum.left:
        if first.left:
            sent = (first.advance(*sent),)
        if up_sum.left:
            sent = (up_sum.advance(*sent),)
        if second.left:
            sent = (second.advance(*sent),)
        if len(first.left) == 2:
            grad_down_w = tie(down_all, *sent).astype(F32)
            sent += (grad_down_w,)
        small = tie(small, *sent)
        if arriving is not None:
            small = small + (arriving * shared_rows if axis == "tensor" else arriving)
        arriving = None
        if swaps:
            axis, size, bit = swaps.pop(0)
            arriving = swap(small, axis, size, bit)
        sent = (small,)
    local, small = small[6:], small[:6]
    own, got = up_sum.halves()
    grad_up_w = join_step(flags, bits[0], tie(own, *sent), got, F32)
    own, got = first.halves()
    grad_qkv_w, grad_out_w = head_outputs(
        flags, (bits[0], other_bits[0]), (tie(own, grad_up_w), got), second.halves()
    )
    return (
        shared["act"],
        loss,
        shared["input"],
        small[0],
        small[1],
        grad_qkv_w,
        local[1, : heads_sum.shape[1]],
        local[1, heads_sum.shape[1] : 2 * heads_sum.shape[1]],
        grad_out_w,
        small[4],
        small[2],
        small[3],
        grad_up_w,
        local[0],
        grad_down_w,
        small[5],
    )


def solution(mesh):
    in_specs = (
        P("dp", "tensor", None),
        P("dp", None),
        P("dp", None),
        P("dp", "tensor", None),
        P(),
        P(),
        P(None, None, "tensor"),
        P("tensor"),
        P("tensor"),
        P("tensor", None),
        P(),
        P(),
        P(),
        P(None, "tensor"),
        P("tensor"),
        P("tensor", None),
        P(),
    )
    out_specs = (
        P("dp", "tensor", None),
        P("dp", "tensor"),
        P("dp", "tensor", None),
        P(),
        P(),
        P(None, None, "tensor"),
        P("tensor"),
        P("tensor"),
        P("tensor", None),
        P(),
        P(),
        P(),
        P(None, "tensor"),
        P("tensor"),
        P("tensor", None),
        P(),
    )
    return jax.shard_map(
        functools.partial(shards, mesh.shape["dp"]),
        mesh=mesh,
        in_specs=in_specs,
        out_specs=out_specs,
        check_vma=False,
    )
```
